32 devices in a mesh: seq: 8 (over y, x, core), span: 4 (over z).
Axes of the slice: x: 2, y: 2, z: 4, core: 2. Of those that a mesh axis runs over, the one named last changes fastest.
Arguments:
- tokens: bfloat16 [8, 7552, 768], P('seq', 'span'), may hold values from -6 to 6
- item_lengths: int32 [8, 79], P('seq'), may hold values from 0 to 577, as said below
- attn_gain: bfloat16 [768], P(('seq', 'span')), may hold values from 0.099609375 to 1.8984375
- w_query: bfloat16 [768, 768], P(('seq', 'span')), may hold values from -0.21875 to 0.21875
- w_key: bfloat16 [768, 768], P(('seq', 'span')), may hold values from -0.21875 to 0.21875
- w_value: bfloat16 [768, 768], P(('seq', 'span')), may hold values from -0.21875 to 0.21875
- w_out: bfloat16 [768, 768], P(('seq', 'span')), may hold values from -2.5 to 2.5
- mlp_gain: bfloat16 [768], P(('seq', 'span')), may hold values from 0.099609375 to 1.8984375
- w_gate: bfloat16 [768, 2048], P(('seq', 'span')), may hold values from -0.21875 to 0.21875
- w_up: bfloat16 [768, 2048], P(('seq', 'span')), may hold values from -0.21875 to 0.21875
- w_down: bfloat16 [2048, 768], P(('seq', 'span')), may hold values from -0.25 to 0.25
- cotangent: bfloat16 [8, 7552, 768], P('seq', 'span'), may hold values from -6 to 6
Outputs:
- output: bfloat16 [8, 7552, 768], P('seq', 'span')
- input_grad: bfloat16 [8, 7552, 768], P('seq', 'span')
- attn_gain_grad: float32 [768], P(('seq', 'span'))
- w_query_grad: float32 [768, 768], P(('seq', 'span'))
- w_key_grad: float32 [768, 768], P(('seq', 'span'))
- w_value_grad: float32 [768, 768], P(('seq', 'span'))
- w_out_grad: float32 [768, 768], P(('seq', 'span'))
- mlp_gain_grad: float32 [768], P(('seq', 'span'))
- w_gate_grad: float32 [768, 2048], P(('seq', 'span'))
- w_up_grad: float32 [768, 2048], P(('seq', 'span'))
- w_down_grad: float32 [2048, 768], P(('seq', 'span'))
The draws below stay inside these ranges and needn't reach their ends.
Inputs may be any that keep to these rules, and one draw needn't show every extreme that they name: `item_lengths`: row s lists the items packed into sequence s of 7552 slots in order: every nonzero entry is 1 + 24 * h with h from 4 to 24, nonzero entries come first and sum to at most 7552, later entries are zero and the remaining slots, at most 576, are padding. Every row has an item of height 24.
All inputs are finite; a program needn't handle non-finite values.
Results may differ from the reference program's by a relative error of at most 0.014.
Values may be sent and summed in bfloat16 or wider, within the bound.
A program may use at most 256 MiB of HBM per device.

```python
import jax
import jax.numpy as jnp
from jax import lax

D = 768
HEADS = 12
HEAD_DIM = 64
FF = 2048
LEN = 7552
CROP = 24
HMIN = 4
HMAX = 24
CH = 1888
HALO = 576
SEQS = 8
ITEMS = 79


def draw_item_lengths(key, part):
    key = jax.random.fold_in(key, 11)
    key_heights, key_place = jax.random.split(key, 2)
    heights = jax.random.randint(key_heights, (SEQS, ITEMS), HMIN, HMAX + 1)
    place = jax.random.randint(key_place, (SEQS,), 0, 2)
    columns = jnp.arange(ITEMS)
    heights = jnp.where(columns[None, :] == place[:, None], HMAX, heights)
    lengths = 1 + CROP * heights
    running = jnp.cumsum(lengths, axis=1)
    return jnp.where(running <= LEN, lengths, 0).astype(jnp.int32)


def spiked(array, key, source, target, shards_of, factor):
    def block_of(axis_at):
        return (jnp.arange(array.shape[axis_at]) // (array.shape[axis_at] // shards_of)).reshape((-1,) + (1,) * (array.ndim - 1 - axis_at))

    near = jax.random.permutation(key, shards_of)[block_of(target)]
    other_side = (block_of(target) + shards_of // 2) % shards_of
    return jnp.where((block_of(source) == near) | (block_of(source) == other_side), factor * array, array)


def level_of(stream_key, shape, shards, least, top_value):
    loudness, own = 1.0, jax.random.fold_in(stream_key, 6)
    for dim, parts in shards:
        steps = jnp.exp(jax.random.uniform(jax.random.fold_in(own, dim), (parts,), jnp.float32, least / len(shards), top_value / len(shards)))
        loudness = loudness * jnp.repeat(steps, shape[dim] // parts).reshape([-1 if axis == dim else 1 for axis in range(len(shape))])
    return loudness


def normal_values(key, extent, width, most, pieces=(), held_as=jnp.bfloat16):
    entries = width * jax.random.normal(key, extent, jnp.float32)
    if pieces:
        entries = entries * level_of(key, extent, pieces, -0.22, 0.18)
    return jnp.clip(entries, -most, most).astype(held_as)


def bell_draw_with(own_key, shape, spread, most, cuts, heavy, held_as=jnp.bfloat16):
    entries = spread * jax.random.normal(own_key, shape, jnp.float32)
    if cuts:
        entries = entries * level_of(own_key, shape, cuts, -0.22, 0.18)
    return jnp.clip(spiked(entries, jax.random.fold_in(own_key, 3), *heavy), -most, most).astype(held_as)


def setup_inputs(seed: int = 0) -> dict:
    keys = jax.random.split(jax.random.key(seed), 13)
    return {
        "tokens": bell_draw_with(keys[0], (SEQS, LEN, D), 1.0, 6.0, ((0, 8), (1, 4)), (0, 2, 8, 2.0)),
        "item_lengths": draw_item_lengths(jax.random.fold_in(keys[12], 71), 0),
        "attn_gain": jnp.clip(1.0 + 0.18 * jax.random.normal(keys[2], (D,), jnp.float32), 0.099609375, 1.8984375).astype(jnp.bfloat16),
        "w_query": normal_values(keys[3], (D, D), D ** -0.5, 0.21875, ((0, 32),)),
        "w_key": normal_values(keys[4], (D, D), D ** -0.5, 0.21875, ((0, 32),)),
        "w_value": normal_values(keys[5], (D, D), D ** -0.5, 0.21875, ((0, 32),)),
        "w_out": normal_values(keys[6], (D, D), (D // 128) ** -0.5, 2.5, ((0, 32),)),
        "mlp_gain": jnp.clip(1.0 + 0.18 * jax.random.normal(keys[7], (D,), jnp.float32), 0.099609375, 1.8984375).astype(jnp.bfloat16),
        "w_gate": normal_values(keys[8], (D, FF), D ** -0.5, 0.21875, ((0, 32),)),
        "w_up": normal_values(keys[9], (D, FF), D ** -0.5, 0.21875, ((0, 32),)),
        "w_down": normal_values(keys[10], (FF, D), (FF // 4) ** -0.5, 0.25, ((0, 32),)),
        "cotangent": normal_values(keys[11], (SEQS, LEN, D), 1.0, 6.0, ((0, 8), (1, 4))),
    }


epsilon = 1e-05
score_scale = 0.125

@jax.custom_vjp
def low(v):
    return lax.optimization_barrier(v.astype(jnp.bfloat16)).astype(jnp.float32)

@jax.custom_vjp
def low_back(v):
    return v

def low_keep(v):
    return (low(v), None)

def low_pass(kept, grad):
    return (grad,)

def back_keep(v):
    return (v, None)

def back_low(kept, grad):
    return (low(grad),)
low.defvjp(low_keep, low_pass)
low_back.defvjp(back_keep, back_low)

def layout(item_lengths, seq_slots):
    item_ends = jnp.cumsum(item_lengths, axis=1).astype(jnp.int32)
    slot_ids = jnp.arange(seq_slots, dtype=jnp.int32)
    reached = slot_ids[None, :, None] >= item_ends[:, None, :]
    segment = lax.optimization_barrier(jnp.sum(reached.astype(jnp.int32), axis=2)).astype(jnp.int32)
    item_start = lax.optimization_barrier(jnp.max(jnp.where(reached, item_ends[:, None, :], 0), axis=2)).astype(jnp.int32)
    return (segment, (slot_ids[None, :] - item_start).astype(jnp.int32))

def angles(position, head_dim):
    half_dim = head_dim // 2
    frequency = 10000.0 ** (-jnp.arange(half_dim, dtype=jnp.float32) / half_dim)
    phases = position.astype(jnp.float32)[..., None] * frequency
    return (jnp.cos(phases), jnp.sin(phases))

def rotate(values, cosine, sine):
    half_dim = values.shape[-1] // 2
    first_half = values[..., :half_dim]
    second = values[..., half_dim:]
    return jnp.concatenate([first_half * cosine - second * sine, second * cosine + first_half * sine], axis=-1)

def normalize(values, gain_vec):
    inverse = lax.rsqrt(lax.optimization_barrier(jnp.mean(values * values, axis=-1, keepdims=True)) + epsilon)
    return values * inverse * gain_vec

def matmul(left_side, weight):
    return jnp.einsum('...e,ef->...f', left_side, weight, precision=lax.Precision.HIGHEST)

def block(params, inputs, segment, position):
    gain_one, query_w, key_w, value_w, out_w, gain_two, gate_w, up_w, down_w = params

    def run_seq(blocks_in):
        seq_x, seq_seg, seq_pos = blocks_in
        head_shape = (LEN, HEADS, HEAD_DIM)
        normed_one = low(normalize(seq_x, gain_one))
        query = low_back(matmul(normed_one, query_w))
        key_proj = low_back(matmul(normed_one, key_w))
        value_proj = low(low_back(matmul(normed_one, value_w)))
        cosine, sine = angles(seq_pos, HEAD_DIM)
        cosine = cosine[:, None, :]
        sine = sine[:, None, :]
        query_rot = low(rotate(query.reshape(head_shape), cosine, sine))
        key_rot = low(rotate(key_proj.reshape(head_shape), cosine, sine))
        padding = jnp.zeros((HALO, HEADS, HEAD_DIM), jnp.float32)
        key_pad = jnp.concatenate([padding, key_rot], axis=0)
        value_pad = jnp.concatenate([padding, value_proj.reshape(head_shape)], axis=0)
        seg_pad = jnp.concatenate([jnp.full((HALO,), -1, jnp.int32), seq_seg.astype(jnp.int32)], axis=0)

        def attend(index):
            start = (index * CH).astype(jnp.int32)
            query_one = lax.dynamic_slice_in_dim(query_rot, start, CH, 0)
            key_one = lax.dynamic_slice_in_dim(key_pad, start, HALO + CH, 0)
            value_one = lax.dynamic_slice_in_dim(value_pad, start, HALO + CH, 0)
            seg_query = lax.dynamic_slice_in_dim(seq_seg.astype(jnp.int32), start, CH, 0)
            seg_key = lax.dynamic_slice_in_dim(seg_pad, start, HALO + CH, 0)
            query_slot = HALO + start + jnp.arange(CH, dtype=jnp.int32)
            key_slot = start + jnp.arange(HALO + CH, dtype=jnp.int32)
            visible = (seg_query[:, None] == seg_key[None, :]) & (key_slot[None, :] <= query_slot[:, None])
            raw_scores = jnp.einsum('qhd,khd->hqk', query_one, key_one, precision=lax.Precision.HIGHEST) * score_scale
            scores = jnp.where(visible[None], low_back(raw_scores), -1e+30)
            row_top = lax.optimization_barrier(jnp.max(scores, axis=-1, keepdims=True))
            exp_scores = jnp.exp(scores - row_top)
            probs = exp_scores / lax.optimization_barrier(jnp.sum(exp_scores, axis=-1, keepdims=True))
            return jnp.einsum('hqk,khd->qhd', low(probs), value_one, precision=lax.Precision.HIGHEST)
        attended = lax.map(jax.checkpoint(attend), jnp.arange(LEN // CH, dtype=jnp.int32))
        mixed = low(low_back(attended.reshape(LEN, HEADS * HEAD_DIM)))
        resid = seq_x + low_back(matmul(mixed, out_w))
        normed_two = low(normalize(resid, gain_two))
        gate_proj = low_back(matmul(normed_two, gate_w))
        up_proj = low_back(matmul(normed_two, up_w))
        hidden = low(jax.nn.silu(gate_proj) * up_proj)
        return resid + low_back(matmul(hidden, down_w))
    return lax.map(jax.checkpoint(run_seq), (inputs, segment, position))

def reference(tokens, item_lengths, attn_gain, w_query, w_key, w_value, w_out, mlp_gain, w_gate, w_up, w_down, cotangent):
    segment, position = layout(item_lengths, LEN)
    params = tuple((weight.astype(jnp.float32) for weight in (attn_gain, w_query, w_key, w_value, w_out, mlp_gain, w_gate, w_up, w_down)))
    inputs = tokens.astype(jnp.float32)

    def forward(params_in, inputs_in):
        return block(params_in, inputs_in, segment, position)
    result, pullback = jax.vjp(forward, params, inputs)
    grads, input_grad = pullback(cotangent.astype(jnp.float32))
    return (result.astype(jnp.bfloat16), input_grad.astype(jnp.bfloat16), grads[0], grads[1], grads[2], grads[3], grads[4], grads[5], grads[6], grads[7], grads[8])
```

```python
import functools

import jax
import jax.numpy as jnp
from jax import lax
from jax.experimental import pallas as pl
from jax.experimental.pallas import tpu as pltpu
from jax.sharding import PartitionSpec as P

HEAD_DIM = 64
HALO = 576
FRONT = 640
QB = 128
WIN = FRONT + QB
LANES = 128
EPS = 1e-5
SCALE = 0.125
AWAY = -1e30
BF = jnp.bfloat16
F32 = jnp.float32
VMEM_LIMIT = 60 * 1024 * 1024


def dot(a, b):
    return lax.dot_general(a, b, (((1,), (0,)), ((), ())), preferred_element_type=F32)


def dot_nt(a, b):
    return lax.dot_general(a, b, (((1,), (1,)), ((), ())), preferred_element_type=F32)


def dot_tn(a, b):
    return lax.dot_general(a, b, (((0,), (0,)), ((), ())), preferred_element_type=F32)


def rotated(v, cos, sin):
    lane = lax.broadcasted_iota(jnp.int32, v.shape, 1)
    swapped = jnp.where(lane % 64 < 32, pltpu.roll(v, 96, 1), pltpu.roll(v, 32, 1))
    return v * cos + swapped * sin


def both_heads(v):
    lane = lax.broadcasted_iota(jnp.int32, v.shape, 1)
    zero = jnp.zeros_like(v)
    return jnp.concatenate([jnp.where(lane < 64, v, zero), jnp.where(lane < 64, zero, v)], axis=0)


def one_of_both(v):
    rows = v.shape[0] // 2
    lane = lax.broadcasted_iota(jnp.int32, (rows, v.shape[1]), 1)
    return jnp.where(lane < 64, v[:rows], v[rows:])


def norm_rows(x):
    return lax.rsqrt(jnp.mean(x * x, axis=-1, keepdims=True) + EPS)


def in_thirds(v, lane):
    high = v.astype(BF)
    rest = v - high.astype(F32)
    middle = rest.astype(BF)
    last = (rest - middle.astype(F32)).astype(BF)
    return jnp.where(lane < 48, high, jnp.where(lane < 64, middle, last))


def fwd_kernel(tok, halo, wq, wk, wv, gain, kaug, qaug, cos, sin, q_out, k_out, v_out, mixed_out, qaug_out):
    rows, width = tok.shape
    padded = q_out.shape[0]
    pairs = width // LANES
    g = gain[...]

    def project(x, key_at, count, query_at):
        normed = (x * norm_rows(x) * g).astype(BF)
        c, s = cos[pl.ds(key_at, count), :], sin[pl.ds(key_at, count), :]
        if query_at is not None:
            q = dot(normed, wq[...])
            for t in range(pairs):
                at = slice(t * LANES, (t + 1) * LANES)
                q_out[pl.ds(query_at, count), at] = (rotated(q[:, at], c, s) * SCALE).astype(BF)
        k = dot(normed, wk[...])
        for t in range(pairs):
            at = slice(t * LANES, (t + 1) * LANES)
            k_out[pl.ds(key_at, count), at] = rotated(k[:, at], c, s).astype(BF)
        v_out[pl.ds(key_at, count), :] = dot(normed, wv[...]).astype(BF)

    k_out[: FRONT - HALO, :] = jnp.zeros((FRONT - HALO, width), BF)
    v_out[: FRONT - HALO, :] = jnp.zeros((FRONT - HALO, width), BF)
    project(halo[...].astype(F32), FRONT - HALO, HALO, None)
    step = 480
    for at in range(0, rows, step):
        count = min(step, rows - at)
        project(tok[at : at + count, :].astype(F32), FRONT + at, count, at)
    if padded > rows:
        q_out[rows:, :] = jnp.zeros((padded - rows, width), BF)
        k_out[FRONT + rows :, :] = jnp.zeros((padded - rows, width), BF)
        v_out[FRONT + rows :, :] = jnp.zeros((padded - rows, width), BF)

    lane = lax.broadcasted_iota(jnp.int32, (QB, LANES), 1)
    row = lax.broadcasted_iota(jnp.int32, (2 * QB, QB), 0)
    behind = lax.broadcasted_iota(jnp.int32, (2 * QB, QB), 1) <= row % QB

    def block(b, carry):
        start = pl.multiple_of(b * QB, QB)
        k_a = kaug[pl.ds(start, WIN), :]
        q_a = qaug[pl.ds(start, QB), :]
        q_a2 = jnp.concatenate([q_a, q_a], axis=0)
        logs = jnp.zeros((QB, LANES), F32)
        for t in range(pairs):
            at = slice(t * LANES, (t + 1) * LANES)
            q2 = jnp.concatenate([both_heads(q_out[pl.ds(start, QB), at]), q_a2], axis=1)
            k2 = jnp.concatenate([k_out[pl.ds(start, WIN), at], k_a], axis=1)
            s = dot_nt(q2, k2)
            s = jnp.concatenate([s[:, :FRONT], jnp.where(behind, s[:, FRONT:], AWAY)], axis=1)
            top = jnp.max(s, axis=1, keepdims=True)
            p = jnp.exp(s - top).astype(BF)
            v = v_out[pl.ds(start, WIN), at]
            o = dot(p, jnp.concatenate([v, jnp.ones_like(v)], axis=1))
            total = o[:, LANES:]
            mixed_out[pl.ds(start, QB), at] = one_of_both(o[:, :LANES] / total).astype(BF)
            log = top + jnp.log(total)
            for e in range(2):
                h = 2 * t + e
                mine = (lane == 32 + h) | (lane == 48 + h) | (lane == 64 + h)
                logs = jnp.where(mine, log[e * QB : (e + 1) * QB], logs)
        qaug_out[pl.ds(start, QB), :] = jnp.where(lane < 32, q_a, in_thirds(-logs, lane))
        return carry

    lax.fori_loop(0, padded // QB, block, 0)


def bwd_kernel(q, k, v, mixed, dmixed, kaug, qaug, cos, sin, dq_out, dk_out, dv_out):
    padded, width = q.shape
    pairs = width // LANES
    heads = width // HEAD_DIM
    dk_out[...] = jnp.zeros_like(dk_out)
    dv_out[...] = jnp.zeros_like(dv_out)
    lead = FRONT - HALO
    win = WIN - lead

    lane = lax.broadcasted_iota(jnp.int32, (QB, LANES), 1)
    e_row = lax.broadcasted_iota(jnp.int32, (width, LANES), 0) // HEAD_DIM
    e_lane = lax.broadcasted_iota(jnp.int32, (width, LANES), 1)
    picks = ((e_lane >= 32) & (e_lane < 80) & (e_lane % 16 == e_row)).astype(F32).astype(BF)
    key_row = lax.broadcasted_iota(jnp.int32, (QB, 2 * QB), 0)
    behind = key_row <= lax.broadcasted_iota(jnp.int32, (QB, 2 * QB), 1) % QB

    def block(b, carry):
        start = pl.multiple_of(b * QB, QB)
        keys = pl.ds(pl.multiple_of(start + lead, 64), win)
        k_a = kaug[keys, :]
        q_a = qaug[pl.ds(start, QB), :]
        prod = dmixed[pl.ds(start, QB), :].astype(F32) * mixed[pl.ds(start, QB), :].astype(F32)
        high = prod.astype(BF)
        low = (prod - high.astype(F32)).astype(BF)
        delta = in_thirds(-(dot(high, picks) + dot(low, picks)), lane)
        c, s_ = cos[pl.ds(start + FRONT, QB), :], sin[pl.ds(start + FRONT, QB), :]
        zero = jnp.zeros_like(q_a)
        for t in range(pairs):
            at = slice(t * LANES, (t + 1) * LANES)
            mine = [(lane >= 32) & (lane % 16 == 2 * t + e) for e in range(2)]
            q_2 = both_heads(q[pl.ds(start, QB), at])
            q_aug = jnp.concatenate([jnp.where((lane < 32) | mine[e], q_a, zero) for e in range(2)], axis=0)
            d_2 = both_heads(dmixed[pl.ds(start, QB), at])
            d_aug = jnp.concatenate([jnp.where(mine[e], delta, zero) for e in range(2)], axis=0)
            k_p = k[keys, at]
            st = dot_nt(jnp.concatenate([k_p, k_a], axis=1), jnp.concatenate([q_2, q_aug], axis=1))
            st = jnp.concatenate([st[:HALO], jnp.where(behind, st[HALO:], AWAY)], axis=0)
            pt = jnp.exp(st)
            dpt = dot_nt(jnp.concatenate([v[keys, at], k_a], axis=1), jnp.concatenate([d_2, d_aug], axis=1))
            dst = (pt * dpt).astype(BF)
            dv_out[keys, at] += dot(pt.astype(BF), d_2)
            dk_out[keys, at] += dot(dst, q_2)
            dq = one_of_both(dot_tn(dst, k_p)) * SCALE
            dq_out[pl.ds(start, QB), at] = rotated(dq, c, -s_).astype(BF)
        return carry

    lax.fori_loop(0, padded // QB, block, 0)


FF_STEP = 512
ROW_STEP = 384


def mlp_kernel(rows, x_ref, mixed, c_ref, wo, wg, wu, wd, gain,
               out, d_resid_out, d_mixed_out, d_branch_out, n2_out, hid_out, dg_out, du_out, gain_grad):
    i = pl.program_id(0)
    count, width = x_ref.shape
    valid = lax.broadcasted_iota(jnp.int32, (count, width), 0) + i * count < rows
    c = jnp.where(valid, c_ref[...], jnp.zeros((count, width), BF))
    x = jnp.where(valid, x_ref[...].astype(F32), 0.0)
    resid = x + dot(mixed[...], wo[...])
    r = norm_rows(resid)
    g = gain[...]
    hat = resid * r
    n2 = (hat * g).astype(BF)
    n2_out[...] = n2
    acc = resid
    dn = jnp.zeros((count, width), F32)
    for f in range(0, wg.shape[1], FF_STEP):
        at = slice(f, f + FF_STEP)
        gate = dot(n2, wg[:, at])
        up = dot(n2, wu[:, at])
        sig = jax.nn.sigmoid(gate)
        silu = gate * sig
        hid = (silu * up).astype(BF)
        hid_out[:, at] = hid
        acc = acc + dot(hid, wd[at, :])
        dh = dot_nt(c, wd[at, :])
        dg = (dh * up * sig * (1.0 + gate * (1.0 - sig))).astype(BF)
        du = (dh * silu).astype(BF)
        dg_out[:, at] = dg
        du_out[:, at] = du
        dn = dn + dot_nt(dg, wg[:, at]) + dot_nt(du, wu[:, at])
    out[...] = acc.astype(BF)

    @pl.when(i == 0)
    def _():
        gain_grad[...] = jnp.zeros_like(gain_grad)

    gain_grad[...] += jnp.sum((dn * hat).reshape(count // 8, 8, width), axis=0)
    e = dn * g
    d_resid = c.astype(F32) + r * (e - hat * jnp.mean(e * hat, axis=-1, keepdims=True))
    d_resid_out[...] = d_resid
    d_branch = d_resid.astype(BF)
    d_branch_out[...] = d_branch
    d_mixed_out[...] = dot_nt(d_branch, wo[...]).astype(BF)


def slots_of(item_lengths, first, count):
    ends = jnp.cumsum(item_lengths[0])[None, :]
    slots = first + jnp.arange(count, dtype=jnp.int32)
    reached = (slots[:, None] >= ends) & (item_lengths[0] > 0)[None, :]
    segment = jnp.sum(reached.astype(jnp.int32), axis=1)
    begin = jnp.max(jnp.where(reached, ends, 0), axis=1)
    return slots, segment % 16, slots - begin


def side_arrays(item_lengths, local_rows, padded):
    offset = lax.axis_index("span") * local_rows
    count = FRONT + padded
    slots, group, position = slots_of(item_lengths, offset - FRONT, count)
    lane = jnp.arange(LANES, dtype=jnp.int32)[None, :]
    away = (slots < 0) | (jnp.arange(count) < FRONT - HALO)
    where_key = jnp.where(away, 16, group)[:, None]
    marks = (lane >= 32) & (lane < 80) & (lane % 16 < 12)
    kaug = ((lane == where_key) | marks).astype(BF)
    qaug = jnp.where((lane <= 16) & (lane != group[FRONT:, None]), AWAY, 0.0).astype(BF)
    half = HEAD_DIM // 2
    frequency = 10000.0 ** (-(lane % half).astype(F32) / half)
    phases = position[:, None].astype(F32) * frequency
    sign = jnp.where(lane % HEAD_DIM < half, -1.0, 1.0)
    return kaug, qaug, jnp.cos(phases), jnp.sin(phases) * sign


def vmem():
    return pl.BlockSpec(memory_space=pltpu.VMEM)


def params(**more):
    return pltpu.CompilerParams(vmem_limit_bytes=VMEM_LIMIT, **more)


def outer_sum(a, b):
    return lax.dot_general(a, b, (((0,), (0,)), ((), ())), preferred_element_type=F32)


def per_device(tokens, item_lengths, attn_gain, w_query, w_key, w_value, w_out, mlp_gain, w_gate, w_up, w_down, cotangent):
    rows, width = tokens.shape[1:]
    ff = w_gate.shape[1]
    padded = -(-rows // ROW_STEP) * ROW_STEP
    axes = ("seq", "span")
    sds = jax.ShapeDtypeStruct
    tok, cot = tokens[0], cotangent[0]

    packed = jnp.concatenate([w_query, w_key, w_value, w_out, w_gate, w_up], axis=1)
    gains = jnp.stack([attn_gain, mlp_gain], axis=1)
    packed = lax.all_gather(packed, axes, axis=0, tiled=True)
    down = lax.all_gather(w_down, axes, axis=0, tiled=True)
    gains = lax.all_gather(gains, axes, axis=0, tiled=True).astype(F32)
    gain_one, gain_two = gains[:, 0].reshape(1, width), gains[:, 1].reshape(1, width)
    wq, wk, wv, wo = (packed[:, i * width : (i + 1) * width] for i in range(4))
    wg, wu = packed[:, 4 * width : 4 * width + ff], packed[:, 4 * width + ff :]

    spans = lax.axis_size("span")
    halo = lax.ppermute(tok[rows - HALO :], "span", [(i, i + 1) for i in range(spans - 1)])
    kaug, qaug, cos, sin = side_arrays(item_lengths, rows, padded)
    ext = FRONT + padded
    q, k, v, mixed, qaug = pl.pallas_call(
        fwd_kernel,
        out_shape=[
            sds((padded, width), BF), sds((ext, width), BF), sds((ext, width), BF),
            sds((padded, width), BF), sds((padded, LANES), BF),
        ],
        in_specs=[vmem()] * 10,
        out_specs=[vmem()] * 5,
        compiler_params=params(),
        name="attend",
    )(tok, halo, wq, wk, wv, gain_one, kaug, qaug, cos, sin)

    steps = padded // ROW_STEP
    tile = lambda n: pl.BlockSpec((ROW_STEP, n), lambda i: (i, 0))
    whole = lambda a: pl.BlockSpec(a.shape, lambda i: (0, 0), pipeline_mode=pl.Buffered(1))
    output, d_resid, d_mixed, d_branch, n2, hid, dg, du, gain_two_grad = pl.pallas_call(
        functools.partial(mlp_kernel, rows),
        grid=(steps,),
        out_shape=[
            sds((rows, width), BF), sds((rows, width), F32), sds((padded, width), BF), sds((padded, width), BF),
            sds((padded, width), BF), sds((padded, ff), BF), sds((padded, ff), BF), sds((padded, ff), BF),
            sds((8, width), F32),
        ],
        in_specs=[tile(width)] * 3 + [whole(a) for a in (wo, wg, wu, down, gain_two)],
        out_specs=[tile(width)] * 5 + [tile(ff)] * 3 + [pl.BlockSpec((8, width), lambda i: (0, 0))],
        compiler_params=params(),
        name="mlp",
    )(tok, mixed, cot, wo, wg, wu, down, gain_two)

    grad_down = outer_sum(hid[:rows], cot)
    grad_gate = outer_sum(n2, dg)
    grad_up = outer_sum(n2, du)
    grad_out = outer_sum(mixed, d_branch)

    dq, dk, dv = pl.pallas_call(
        bwd_kernel,
        out_shape=[sds((padded, width), BF), sds((ext, width), F32), sds((ext, width), F32)],
        in_specs=[vmem()] * 9,
        out_specs=[vmem()] * 3,
        compiler_params=params(),
        name="attend_back",
    )(q, k, v, mixed, d_mixed, kaug, qaug, cos, sin)

    dq = dq[:rows]
    back = jnp.concatenate([dk[FRONT - HALO : FRONT], dv[FRONT - HALO : FRONT]], axis=1).astype(BF)
    back = lax.ppermute(back, "span", [(i + 1, i) for i in range(spans - 1)]).astype(F32)
    dk, dv = dk[FRONT : FRONT + rows], dv[FRONT : FRONT + rows]
    dk = jnp.concatenate([dk[: rows - HALO], dk[rows - HALO :] + back[:, :width]])
    dv = jnp.concatenate([dv[: rows - HALO], dv[rows - HALO :] + back[:, width:]]).astype(BF)
    heads = width // HEAD_DIM
    half = HEAD_DIM // 2
    c = cos[FRONT : FRONT + rows, None, :HEAD_DIM]
    s = sin[FRONT : FRONT + rows, None, :HEAD_DIM]
    dk3 = dk.reshape(rows, heads, HEAD_DIM)
    dk = (dk3 * c - jnp.concatenate([dk3[..., half:], dk3[..., :half]], axis=-1) * s).reshape(rows, width).astype(BF)
    x = tok.astype(F32)
    inv = norm_rows(x)
    hat = x * inv
    n1 = (hat * gain_one).astype(BF)
    grad_q, grad_k, grad_v = (outer_sum(n1, d) for d in (dq, dk, dv))
    dn = sum(lax.dot_general(d, w, (((1,), (1,)), ((), ())), preferred_element_type=F32) for d, w in ((dq, wq), (dk, wk), (dv, wv)))
    gain_one_grad = jnp.sum(dn * hat, axis=0)
    e = dn * gain_one
    input_grad = (d_resid + inv * (e - hat * jnp.mean(e * hat, axis=-1, keepdims=True))).astype(BF)

    scatter = lambda g: lax.psum_scatter(g, axes, scatter_dimension=0, tiled=True)
    sums = scatter(jnp.concatenate([grad_q, grad_k, grad_v, grad_out, grad_gate, grad_up], axis=1))
    gain_sums = scatter(jnp.stack([gain_one_grad, jnp.sum(gain_two_grad, axis=0)], axis=1))
    g_q, g_k, g_v, g_o = (sums[:, i * width : (i + 1) * width] for i in range(4))
    return (
        output[None], input_grad[None], gain_sums[:, 0], g_q, g_k, g_v, g_o, gain_sums[:, 1],
        sums[:, 4 * width : 4 * width + ff], sums[:, 4 * width + ff :], scatter(grad_down),
    )


def solution(mesh):
    rows_placed, vector, matrix = P("seq", "span", None), P(("seq", "span")), P(("seq", "span"), None)
    return jax.shard_map(
        per_device,
        mesh=mesh,
        in_specs=(rows_placed, P("seq", None), vector, matrix, matrix, matrix, matrix, vector, matrix, matrix, matrix, rows_placed),
        out_specs=(rows_placed, rows_placed, vector, matrix, matrix, matrix, matrix, vector, matrix, matrix, matrix),
        check_vma=False,
    )
```

```python
import functools

import jax
import jax.numpy as jnp
from jax import lax
from jax.experimental import pallas as pl
from jax.experimental.pallas import tpu as pltpu
from jax.sharding import PartitionSpec as P

HEAD_DIM = 64
HALO = 576
FRONT = 640
QB = 128
WIN = FRONT + QB
LANES = 128
EPS = 1e-5
SCALE = 0.125
AWAY = -1e30
BF = jnp.bfloat16
F32 = jnp.float32
VMEM_LIMIT = 63 * 1024 * 1024


def dot(a, b):
    return lax.dot_general(a, b, (((1,), (0,)), ((), ())), preferred_element_type=F32)


def dot_nt(a, b):
    return lax.dot_general(a, b, (((1,), (1,)), ((), ())), preferred_element_type=F32)


def dot_tn(a, b):
    return lax.dot_general(a, b, (((0,), (0,)), ((), ())), preferred_element_type=F32)


def rotated(v, cos, sin):
    lane = lax.broadcasted_iota(jnp.int32, v.shape, 1)
    swapped = jnp.where(lane % 64 < 32, pltpu.roll(v, 96, 1), pltpu.roll(v, 32, 1))
    return v * cos + swapped * sin


def both_heads(v):
    lane = lax.broadcasted_iota(jnp.int32, v.shape, 1)
    zero = jnp.zeros_like(v)
    return jnp.concatenate([jnp.where(lane < 64, v, zero), jnp.where(lane < 64, zero, v)], axis=0)


def one_of_both(v):
    rows = v.shape[0] // 2
    lane = lax.broadcasted_iota(jnp.int32, (rows, v.shape[1]), 1)
    return jnp.where(lane < 64, v[:rows], v[rows:])


def norm_rows(x):
    return lax.rsqrt(jnp.mean(x * x, axis=-1, keepdims=True) + EPS)


def in_thirds(v, lane):
    high = v.astype(BF)
    rest = v - high.astype(F32)
    middle = rest.astype(BF)
    last = (rest - middle.astype(F32)).astype(BF)
    return jnp.where(lane < 48, high, jnp.where(lane < 64, middle, last))


def coordinates():
    seq, span = lax.axis_index("seq"), lax.axis_index("span")
    return seq // 4, seq // 2 % 2, seq % 2, span


def device(y, x, core, span):
    return (y * 4 + x * 2 + core, span)


def greet():
    y, x, core, span = coordinates()
    barrier = pltpu.get_barrier_semaphore()
    peers = [device(y, x, core, (span + d) % 4) for d in (1, 2, 3)]
    peers += [device(1 - y, x, core, span), device(y, 1 - x, core, span), device(y, x, 1 - core, span)]
    for peer in peers:
        pl.semaphore_signal(barrier, inc=1, device_id=peer, device_id_type=pl.DeviceIdType.MESH)
    pl.semaphore_wait(barrier, len(peers))


def remote(src, dst, sems, at, to):
    return pltpu.make_async_remote_copy(
        src_ref=src, dst_ref=dst, send_sem=sems.at[0, at], recv_sem=sems.at[1, at], device_id=to,
        device_id_type=pl.DeviceIdType.MESH,
    )


GATHER_COPIES = 8


class Gathered:
    def __init__(self, shard, near, whole, at, count, sems, number):
        self.shard, self.near, self.whole, self.sems = shard, near, whole, sems
        self.first = number * GATHER_COPIES
        self.split = shard.shape[0] % 16 != 0
        self.columns = pl.ds(at, count)
        y, x, core, span = coordinates()
        half = count // 2
        left, right = pl.ds(at, half), pl.ds(at + half, half)
        over_y, over_x = device(1 - y, x, core, span), device(y, 1 - x, core, span)
        own = whole.at[y, x, core]
        rows = pl.ds(0, own.shape[0])
        refs = [(near.at[0], near.at[d], device(y, x, core, (span + d) % 4)) for d in (1, 2, 3)]
        refs += [(r, r, to) for r, to in (
            (whole.at[y, x, core, rows, left], over_y),
            (whole.at[y, x, core, rows, right], over_x),
            (whole.at[pl.ds(0, 2), x, core, rows, left], over_x),
            (whole.at[y, pl.ds(0, 2), core, rows, right], over_y),
            (whole.at[pl.ds(0, 2), pl.ds(0, 2), core, rows, self.columns], device(y, x, 1 - core, span)),
        )]
        self.copies = [remote(src, dst, sems, self.first + i, to) for i, (src, dst, to) in enumerate(refs)]

    def go(self, stage):
        if stage == 0:
            v = self.shard[:, self.columns]
            if self.split:
                half = v.shape[1] // 2
                v = v.astype(F32)
                v = jnp.concatenate([v[:, :half], v[:, half:]], axis=0).astype(BF)
            self.near[0] = v
            for i in (0, 1, 2):
                self.copies[i].start()
        if stage == 1:
            y, x, core, span = coordinates()
            for i in (0, 1, 2):
                self.copies[i].wait_recv()
            pieces = []
            for s in range(4):
                v = self.near[(span - s + 4) % 4]
                if self.split:
                    v = v.astype(F32)
                    half = v.shape[0] // 2
                    v = jnp.concatenate([v[:half], v[half:]], axis=1)
                pieces.append(v)
            self.whole[y, x, core, :, self.columns] = jnp.concatenate(pieces, axis=0).astype(BF)
            for i in (3, 4):
                self.copies[i].start()
        if stage == 2:
            for i in (3, 4):
                self.copies[i].wait_recv()
            for i in (5, 6):
                self.copies[i].start()
        if stage == 3:
            for i in (5, 6):
                self.copies[i].wait_recv()
            self.copies[7].start()
        if stage == 4:
            self.copies[7].wait_recv()

    def finish(self):
        for c in self.copies:
            c.wait_send()


def attention_forward(refs, q_out, k_out, v_out, mixed_out, qaug_out, steps, tick):
    tok, halo, weights, gain, kaug, qaug, cos, sin = refs
    rows, width = tok.shape
    padded = q_out.shape[0]
    pairs = width // LANES

    def project(which, spans):
        g = gain[0:1, :]
        w = weights[which]()
        for source, at, count, key_at, query_at in spans:
            x = source[at : at + count, :].astype(F32)
            product = dot((x * norm_rows(x) * g).astype(BF), w)
            if which == 2:
                v_out[key_at : key_at + count, :] = product.astype(BF)
                continue
            c, s = cos[key_at : key_at + count, :], sin[key_at : key_at + count, :]
            for t in range(pairs):
                lanes = slice(t * LANES, (t + 1) * LANES)
                turned = rotated(product[:, lanes], c, s)
                if which == 0:
                    q_out[query_at : query_at + count, lanes] = (turned * SCALE).astype(BF)
                else:
                    k_out[key_at : key_at + count, lanes] = turned.astype(BF)

    lead = FRONT - HALO
    k_out[:lead, :] = jnp.zeros((lead, width), BF)
    v_out[:lead, :] = jnp.zeros((lead, width), BF)
    if padded > rows:
        blank = jnp.zeros((padded - rows, width), BF)
        q_out[rows:, :] = blank
        k_out[FRONT + rows :, :] = blank
        v_out[FRONT + rows :, :] = blank
    for which in range(3):
        steps(which)
        project(which, [(tok, at, min(480, rows - at), FRONT + at, at) for at in range(0, rows, 480)])

    lane = lax.broadcasted_iota(jnp.int32, (QB, LANES), 1)
    row = lax.broadcasted_iota(jnp.int32, (2 * QB, QB), 0)
    behind = lax.broadcasted_iota(jnp.int32, (2 * QB, QB), 1) <= row % QB

    blocks = padded // QB

    def block(i, carry):
        tick(i)

        @pl.when(i == blocks - FRONT // QB)
        def _():
            steps(3)
            for which in (1, 2):
                project(which, [(halo, 0, HALO, lead, None)])

        start = pl.multiple_of((blocks - 1 - i) * QB, QB)
        k_a = kaug[pl.ds(start, WIN), :]
        q_a = qaug[pl.ds(start, QB), :]
        q_a2 = jnp.concatenate([q_a, q_a], axis=0)
        logs = jnp.zeros((QB, LANES), F32)
        for t in range(pairs):
            at = slice(t * LANES, (t + 1) * LANES)
            q2 = jnp.concatenate([both_heads(q_out[pl.ds(start, QB), at]), q_a2], axis=1)
            k2 = jnp.concatenate([k_out[pl.ds(start, WIN), at], k_a], axis=1)
            s = dot_nt(q2, k2)
            s = jnp.concatenate([s[:, :FRONT], jnp.where(behind, s[:, FRONT:], AWAY)], axis=1)
            top = jnp.max(s, axis=1, keepdims=True)
            p = jnp.exp(s - top).astype(BF)
            v = v_out[pl.ds(start, WIN), at]
            o = dot(p, jnp.concatenate([v, jnp.ones_like(v)], axis=1))
            total = o[:, LANES:]
            mixed_out[pl.ds(start, QB), at] = one_of_both(o[:, :LANES] / total).astype(BF)
            log = top + jnp.log(total)
            for e in range(2):
                h = 2 * t + e
                mine = (lane == 32 + h) | (lane == 48 + h) | (lane == 64 + h)
                logs = jnp.where(mine, log[e * QB : (e + 1) * QB], logs)
        qaug_out[pl.ds(start, QB), :] = jnp.where(lane < 32, q_a, in_thirds(-logs, lane))
        return carry

    lax.fori_loop(0, blocks, block, 0)


def fwd_kernel(tok, halo, wq, wk, wv, gain, kaug, qaug, cos, sin, q_out, k_out, v_out, mixed_out, qaug_out):
    weights = [lambda w=w: w[...] for w in (wq, wk, wv)]
    refs = (tok, halo, weights, gain, kaug, qaug, cos, sin)
    attention_forward(refs, q_out, k_out, v_out, mixed_out, qaug_out, lambda which: None, lambda b: None)


GATHER_CHUNKS = (
    (0, 0, 1024), (1, 0, 768), (2, 0, 768), (3, 0, 768), (4, 0, 1024), (4, 1024, 1024), (5, 0, 1024), (5, 1024, 1024),
    (6, 0, 256), (6, 256, 256), (6, 512, 256),
)
HALO_AFTER = (10, 1)
GATHER_FAST = 3


def gather_plan():
    ticks, end = [[] for _ in range(40)], []
    for chunk in range(len(GATHER_CHUNKS)):
        for stage in range(5):
            if chunk < GATHER_FAST:
                ticks[chunk + stage].append((chunk, stage))
            elif stage < 4:
                ticks[chunk + (0, 2, 5, 8)[stage]].append((chunk, stage))
            else:
                end.append((chunk, stage))
    return [sum(ticks[:5], []), ticks[5], ticks[6]], ticks[7:], end


def fwd_gather_kernel(tok, *refs):
    shards, refs = refs[:7], refs[7:]
    kaug, qaug, cos, sin = refs[:4]
    outs, refs = refs[4:9], refs[9:]
    gains, refs = refs[0], refs[1:]
    whole_outs, refs = refs[:7], refs[7:]
    n = len(GATHER_CHUNKS)
    halo, nears, wholes = refs[0], refs[1 : n + 1], refs[n + 1 : n + 8]
    sems, halo_sems, out_sems = refs[n + 8 :]
    rows, width = tok.shape
    y, x, core, span = coordinates()
    greet()
    to_next = remote(tok.at[pl.ds(rows - HALO, HALO)], halo, halo_sems, 0, device(y, x, core, (span + 1) % 4))

    chunks = [
        Gathered(shards[w], nears[i], wholes[w], at, count, sems, i) for i, (w, at, count) in enumerate(GATHER_CHUNKS)
    ]
    out_copies = [pltpu.make_async_copy(w, o, out_sems.at[i]) for i, (w, o) in enumerate(zip(wholes, whole_outs))]

    early, late, end = gather_plan()

    def go(chunk, stage):
        chunks[chunk].go(stage)
        if (chunk, stage) == HALO_AFTER:
            to_next.start()
        w, at, count = GATHER_CHUNKS[chunk]
        if stage == 4 and at + count == wholes[w].shape[-1]:
            out_copies[w].start()

    def steps(which):
        if which == 3:
            to_next.wait_recv()
            return
        for chunk, stage in early[which]:
            go(chunk, stage)
        if which == 0:
            both = wholes[0][...].reshape(width, -1)[:, width:].astype(F32)
            both = [jnp.transpose(both[:, i * LANES : (i + 1) * LANES])[:1] for i in range(2)]
            gains[...] = jnp.concatenate(both + [jnp.zeros((6, width), F32)], axis=0)

    def tick(b):
        for i, todo in enumerate(late):
            if todo:
                @pl.when(b == i)
                def _():
                    for chunk, stage in todo:
                        go(chunk, stage)

    weights = [lambda w=w: w[...].reshape(width, w.shape[-1])[:, :width] for w in wholes[:3]]
    attention_forward((tok, halo, weights, gains, kaug, qaug, cos, sin), *outs, steps, tick)
    for chunk, stage in end:
        go(chunk, stage)
    to_next.wait_send()
    for c in chunks:
        c.finish()
    for c in out_copies:
        c.wait()


def attention_backward(b, refs, dq_out, add):
    q, k, v, dmixed, kaug, qaug, daug, cos, sin = refs
    width = q.shape[1]
    lead = FRONT - HALO
    lane = lax.broadcasted_iota(jnp.int32, (QB, LANES), 1)
    key_row = lax.broadcasted_iota(jnp.int32, (QB, 2 * QB), 0)
    behind = key_row <= lax.broadcasted_iota(jnp.int32, (QB, 2 * QB), 1) % QB
    start = pl.multiple_of(b * QB, QB)
    keys = pl.ds(pl.multiple_of(start + lead, lead), WIN - lead)
    k_a = kaug[keys, :]
    q_a = qaug[pl.ds(start, QB), :]
    d_a = daug[pl.ds(start, QB), :]
    c, s_ = cos[pl.ds(start + FRONT, QB), :], sin[pl.ds(start + FRONT, QB), :]
    zero = jnp.zeros_like(q_a)
    for t in range(width // LANES):
        at = slice(t * LANES, (t + 1) * LANES)
        mine = [(lane >= 32) & (lane % 16 == 2 * t + e) for e in range(2)]
        q_2 = both_heads(q[pl.ds(start, QB), at])
        q_aug = jnp.concatenate([jnp.where((lane < 32) | mine[e], q_a, zero) for e in range(2)], axis=0)
        d_2 = both_heads(dmixed[pl.ds(start, QB), at])
        d_aug = jnp.concatenate([jnp.where(mine[e], d_a, zero) for e in range(2)], axis=0)
        k_p = k[keys, at]
        st = dot_nt(jnp.concatenate([k_p, k_a], axis=1), jnp.concatenate([q_2, q_aug], axis=1))
        st = jnp.concatenate([st[:HALO], jnp.where(behind, st[HALO:], AWAY)], axis=0)
        pt = jnp.exp(st)
        dpt = dot_nt(jnp.concatenate([v[keys, at], k_a], axis=1), jnp.concatenate([d_2, d_aug], axis=1))
        dst = (pt * dpt).astype(BF)
        add(t, dot(dst, q_2), dot(pt.astype(BF), d_2))
        dq = one_of_both(dot_tn(dst, k_p)) * SCALE
        dq_out[pl.ds(start, QB), at] = rotated(dq, c, -s_).astype(BF)


def bwd_kernel(*refs):
    dq_out, dk_out, dv_out = refs[9:]
    padded = dq_out.shape[0]
    dk_out[...] = jnp.zeros_like(dk_out)
    dv_out[...] = jnp.zeros_like(dv_out)
    lead = FRONT - HALO

    def block(b, carry):
        keys = pl.ds(pl.multiple_of(b * QB + lead, lead), WIN - lead)

        def add(t, dk, dv):
            at = slice(t * LANES, (t + 1) * LANES)
            dk_out[keys, at] += dk
            dv_out[keys, at] += dv

        attention_backward(b, refs[:9], dq_out, add)
        return carry

    lax.fori_loop(0, padded // QB, block, 0)


SCATTER_COPIES = 8
SCATTER_CHUNKS = (
    (0, 0, 768), (1, 0, 1024), (1, 1024, 1024), (2, 0, 1024), (2, 1024, 1024), (3, 0, 256), (3, 256, 256), (3, 512, 256),
)


class Scattered:
    def __init__(self, whole, at, count, out, bufs, sems, number, load=None):
        self.whole, self.out, self.load = whole, out, load
        self.got, self.left, self.right, self.left_2, self.right_2, self.near, self.far = bufs
        self.at, self.count = at, count
        self.columns = pl.ds(at, count)
        self.half = half = count // 2
        y, x, core, span = coordinates()
        rows = pl.ds(0, whole.shape[3])
        two = pl.ds(0, 2)
        lo, hi = pl.ds(0, half), pl.ds(half, half)
        over_y, over_x = device(1 - y, x, core, span), device(y, 1 - x, core, span)
        got = self.got
        refs = [
            (whole.at[two, two, 1 - core, rows, self.columns], got, device(y, x, 1 - core, span)),
            (got.at[two, 1 - x, rows, lo], self.left, over_x),
            (got.at[1 - y, two, rows, hi], self.right, over_y),
            (got.at[1 - y, x, rows, lo], self.left_2, over_y),
            (got.at[y, 1 - x, rows, hi], self.right_2, over_x),
        ]
        refs += [(self.near.at[(span + d) % 4], self.far.at[d - 1], device(y, x, core, (span + d) % 4)) for d in (1, 2, 3)]
        first = number * SCATTER_COPIES
        self.copies = [remote(src, dst, sems, first + i, to) for i, (src, dst, to) in enumerate(refs)]
        if load is not None:
            slot, sem = load
            self.load = pltpu.make_async_copy(
                whole.at[two, two, core, rows, self.columns], slot.at[two, two, rows, pl.ds(0, count)], sem
            )
            self.slot = slot

    def go(self, stage):
        y, x, core, span = coordinates()
        got, half = self.got, self.half
        lo, hi = pl.ds(0, half), pl.ds(half, half)
        if stage == 0:
            self.copies[0].start()
        if stage == 1 and self.load is not None:
            self.load.start()
        if stage == 2:
            self.copies[0].wait_recv()
            if self.load is not None:
                self.load.wait()
                own = lambda i, j: self.slot[i, j, :, : self.count]
            else:
                own = lambda i, j: self.whole[i, j, core, :, self.columns]
            for i in range(2):
                for j in range(2):
                    got[i, j] = got[i, j] + own(i, j)
            for i in (1, 2):
                self.copies[i].start()
        if stage == 3:
            for i in (1, 2):
                self.copies[i].wait_recv()
            for i in range(2):
                got[i, x, :, lo] = got[i, x, :, lo] + self.left[i]
                got[y, i, :, hi] = got[y, i, :, hi] + self.right[i]
            for i in (3, 4):
                self.copies[i].start()
        if stage == 4:
            for i in (3, 4):
                self.copies[i].wait_recv()
            total = jnp.concatenate(
                [got[y, x, :, r].astype(F32) + other[...].astype(F32) for r, other in ((lo, self.left_2), (hi, self.right_2))],
                axis=1,
            )
            depth = total.shape[0] // 4
            for s in range(4):
                v = total[s * depth : (s + 1) * depth]
                if depth % 16:
                    v = jnp.concatenate([v[:, :half], v[:, half:]], axis=0)
                self.near[s] = v.astype(BF)
            for i in (5, 6, 7):
                self.copies[i].start()
        if stage == 5:
            for i in (5, 6, 7):
                self.copies[i].wait_recv()
            v = self.near[span].astype(F32)
            for d in range(3):
                v = v + self.far[d].astype(F32)
            depth = self.out.shape[0]
            if depth % 16:
                v = jnp.concatenate([v[:depth], v[depth:]], axis=1)
            self.out[:, self.at : self.at + self.count] = v

    def finish(self):
        for c in self.copies:
            c.wait_send()


def scatter_buffers(rows, count):
    depth = rows // 4
    piece = (2 * depth, count // 2) if depth % 16 else (depth, count)
    shapes = [
        (2, 2, rows, count), (2, rows, count // 2), (2, rows, count // 2), (rows, count // 2), (rows, count // 2),
        (4,) + piece, (3,) + piece,
    ]
    return [pltpu.VMEM(shape, BF) for shape in shapes]


SCATTER_AT = (0, 0, 1, 3, 5, 8)
SCATTER_PACE = 1.25


def scatter_plan(ticks):
    events = []
    for j in range(len(SCATTER_CHUNKS)):
        for stage in range(6):
            events.append((int(SCATTER_PACE * j) + SCATTER_AT[stage], j, stage))
    events.sort()
    inside = [[(j, stage) for t, j, stage in events if t == i] for i in range(ticks)]
    return inside, [(j, stage) for t, j, stage in events if t >= ticks]


def bwd_scatter_kernel(
    q_in, k_in, v_in, dmixed_in, kaug, qaug, daug, cos, sin, tok, gains, d_resid, wq_in, wk_in, wv_in,
    g_out, g_gate, g_up, g_down,
    input_grad, s_query, s_key, s_value, s_out, s_gate, s_up, s_down,
    q, k, v, dmixed, dk_win, dv_win, halo_out, halo_in, weights, resid_block, out_block, loads, tall_loads, *refs,
):
    rows, width = tok.shape
    padded = q.shape[0]
    blocks = padded // QB
    pairs = width // LANES
    lead = FRONT - HALO
    slots = WIN // QB
    n = len(SCATTER_CHUNKS)
    chunk_bufs = [refs[7 * i : 7 * i + 7] for i in range(n + 3)]
    refs = refs[7 * (n + 3) :]
    own = refs[:3]
    sems, load_sems, in_sems, halo_sems, block_sems = refs[3:]
    y, x, core, span = coordinates()

    loads_in = [pltpu.make_async_copy(src, dst, in_sems.at[i]) for i, (src, dst) in enumerate(
        (
            (q_in, q), (k_in, k), (v_in, v), (dmixed_in, dmixed),
            (wq_in.at[pl.ds(0, width), pl.ds(0, width)], weights.at[0]), (wk_in, weights.at[1]), (wv_in, weights.at[2]),
        )
    )]
    for c in loads_in:
        c.start()
    greet()
    wholes, sums = (g_out, g_gate, g_up, g_down), (s_out, s_gate, s_up, s_down)
    chunks = [
        Scattered(
            wholes[w], at, count, sums[w], chunk_bufs[i], sems, i,
            ((loads if w < 3 else tall_loads).at[i % 2], load_sems.at[i]),
        )
        for i, (w, at, count) in enumerate(SCATTER_CHUNKS)
    ]
    chunks += [
        Scattered(own[i], 0, width, (s_query, s_key, s_value)[i], chunk_bufs[n + i], sems, n + i) for i in range(3)
    ]
    to_last = remote(halo_out.at[pl.ds(0, 2), pl.ds(0, HALO)], halo_in, halo_sems, 0, device(y, x, core, (span + 3) % 4))
    inside, after = scatter_plan(blocks)
    dk_win[...] = jnp.zeros_like(dk_win)
    dv_win[...] = jnp.zeros_like(dv_win)
    for c in loads_in[:4]:
        c.wait()

    def block(b, carry):
        for i, todo in enumerate(inside):
            if todo:
                @pl.when(b == i)
                def _():
                    for chunk, stage in todo:
                        chunks[chunk].go(stage)

        def add(t, dk, dv):
            at = slice(t * LANES, (t + 1) * LANES)
            for win, grad in ((dk_win, dk), (dv_win, dv)):
                for j in range(slots):
                    count = min(QB, WIN - lead - j * QB)
                    win[lax.rem(b + j, slots), :count, at] += grad[j * QB : j * QB + count]

        attention_backward(b, (q, k, v, dmixed, kaug, qaug, daug, cos, sin), q, add)

        slot = lax.rem(b, slots)
        at = pl.ds(pl.multiple_of(b * QB + lead, lead), QB)

        @pl.when(b < FRONT // QB)
        def _():
            to = pl.ds(pl.multiple_of(b * QB, QB), QB)
            halo_out[0, to, :] = dk_win[slot].astype(BF)
            halo_out[1, to, :] = dv_win[slot].astype(BF)

        @pl.when((b >= FRONT // QB - 1) & (b < blocks - 1))
        def _():
            for t in range(pairs):
                lanes = slice(t * LANES, (t + 1) * LANES)
                k[at, lanes] = rotated(dk_win[slot, :, lanes], cos[at, :], -sin[at, :]).astype(BF)
            v[at, :] = dv_win[slot].astype(BF)

        @pl.when(b < blocks - 1)
        def _():
            dk_win[slot] = jnp.zeros((QB, width), F32)
            dv_win[slot] = jnp.zeros((QB, width), F32)

        @pl.when(b == FRONT // QB - 1)
        def _():
            to_last.start()

        return carry

    lax.fori_loop(0, blocks, block, 0)

    step = resid_block.shape[1]
    parts = [(at, min(step, rows - at)) for at in range(0, rows, step)]
    resid_in = [
        pltpu.make_async_copy(
            d_resid.at[pl.ds(at, count)], resid_block.at[i % 2, pl.ds(0, count)], block_sems.at[0, i]
        ) for i, (at, count) in enumerate(parts)
    ]
    grad_copies = [
        pltpu.make_async_copy(
            out_block.at[i % 2, pl.ds(0, count)], input_grad.at[pl.ds(at, count)], block_sems.at[1, i]
        ) for i, (at, count) in enumerate(parts)
    ]
    resid_in[0].start()
    resid_in[1].start()
    todo = list(after)

    def events(count):
        for chunk, stage in todo[:count]:
            chunks[chunk].go(stage)
        del todo[:count]

    g = gains[0:1, :]
    normed = dmixed
    for at, count in parts:
        x = tok[at : at + count, :].astype(F32)
        normed[at : at + count, :] = (x * norm_rows(x) * g).astype(BF)

    def weight_grad(i, grad):
        for j in range(2):
            half = width // 2
            total = dot_tn(normed[:rows, j * half : (j + 1) * half], grad)
            own[i][j] = total.reshape(2, 2, half // 4, width).astype(BF)

    weight_grad(0, q[:rows, :])
    chunks[n].go(0)
    events(2)
    to_last.wait_recv()
    for j in range(slots):
        base = (blocks - 1) * QB + lead + j * QB
        slot = (blocks - 1 + j) % slots
        count = min(QB, FRONT + rows - base)
        first = max(base, FRONT + rows - HALO)
        for which, win, whole in ((0, dk_win, k), (1, dv_win, v)):
            grad = win[slot, :count, :]
            more = halo_in[which, first - (FRONT + rows - HALO) : base + count - (FRONT + rows - HALO), :].astype(F32)
            if first > base:
                more = jnp.concatenate([jnp.zeros((first - base, width), F32), more], axis=0)
            grad = grad + more
            if which:
                whole[base : base + count, :] = grad.astype(BF)
                continue
            c, s_ = cos[base : base + count, :], sin[base : base + count, :]
            for t in range(pairs):
                lanes = slice(t * LANES, (t + 1) * LANES)
                whole[base : base + count, lanes] = rotated(grad[:, lanes], c, -s_).astype(BF)
    weight_grad(1, k[FRONT : FRONT + rows, :])
    chunks[n].go(2)
    chunks[n + 1].go(0)
    events(2)
    weight_grad(2, v[FRONT : FRONT + rows, :])
    chunks[n].go(3)
    chunks[n + 1].go(2)
    chunks[n + 2].go(0)
    events(2)
    for c in loads_in[4:]:
        c.wait()
    between = (((0, 4), (1, 3), (2, 2)), ((0, 5), (1, 4), (2, 3)), ((1, 5), (2, 4)), ((2, 5),))
    for i, (at, count) in enumerate(parts):
        grads = (q[at : at + count, :], k[FRONT + at : FRONT + at + count, :], v[FRONT + at : FRONT + at + count, :])
        dn = sum(dot_nt(d, weights[w]) for w, d in enumerate(grads))
        x = tok[at : at + count, :].astype(F32)
        inv = norm_rows(x)
        hat = x * inv
        e = dn * g
        resid_in[i].wait()
        total = resid_block[i % 2, :count] + inv * (e - hat * jnp.mean(e * hat, axis=-1, keepdims=True))
        if i >= 2:
            grad_copies[i - 2].wait()
        out_block[i % 2, :count] = total.astype(BF)
        grad_copies[i].start()
        if i + 2 < len(parts):
            resid_in[i + 2].start()
        events(1)
        for chunk, stage in between[i] if i < len(between) else ():
            chunks[n + chunk].go(stage)
    events(len(todo))
    to_last.wait_send()
    for c in chunks:
        c.finish()
    for c in grad_copies[-2:]:
        c.wait()


FF_STEP = 512
ROW_STEP = 480


def mlp_kernel(rows, x_ref, mixed, c_ref, wo, wg, wu, wd, gains,
               out, d_resid_out, d_mixed_out, daug_out, p_out, p_gate, p_up, p_down,
               a_out, a_gate, a_up, a_down, narrow, wide, sems):
    i = pl.program_id(0)
    count, width = x_ref.shape
    valid = lax.broadcasted_iota(jnp.int32, (count, width), 0) + i * count < rows
    c = jnp.where(valid, c_ref[...], jnp.zeros((count, width), BF))
    x = jnp.where(valid, x_ref[...].astype(F32), 0.0)
    mix = mixed[...]
    resid = x + dot(mix, wo[...])
    r = norm_rows(resid)
    g = gains[1:2, :]
    hat = resid * r
    n2 = (hat * g).astype(BF)
    acc = resid
    dn = jnp.zeros((count, width), F32)

    def gather(ref, rows_at, columns, value):
        ref[rows_at, columns] = jnp.where(i == 0, 0.0, ref[rows_at, columns]) + value

    all_of = slice(None)
    for f in range(0, wg.shape[1], FF_STEP):
        at = slice(f, f + FF_STEP)
        gate = dot(n2, wg[:, at])
        up = dot(n2, wu[:, at])
        sig = jax.nn.sigmoid(gate)
        silu = gate * sig
        hid = (silu * up).astype(BF)
        acc = acc + dot(hid, wd[at, :])
        dh = dot_nt(c, wd[at, :])
        dg = (dh * up * sig * (1.0 + gate * (1.0 - sig))).astype(BF)
        du = (dh * silu).astype(BF)
        dn = dn + dot_nt(dg, wg[:, at]) + dot_nt(du, wu[:, at])
        gather(a_down, at, all_of, dot_tn(hid, c))
        gather(a_gate, all_of, at, dot_tn(n2, dg))
        gather(a_up, all_of, at, dot_tn(n2, du))
    out[...] = acc.astype(BF)
    e = dn * g
    d_resid = c.astype(F32) + r * (e - hat * jnp.mean(e * hat, axis=-1, keepdims=True))
    d_resid_out[...] = d_resid
    d_branch = d_resid.astype(BF)
    gather(a_out, all_of, all_of, dot_tn(mix, d_branch))
    d_mixed = dot_nt(d_branch, wo[...]).astype(BF)
    d_mixed_out[...] = d_mixed

    e_row = lax.broadcasted_iota(jnp.int32, (width, LANES), 0) // HEAD_DIM
    e_lane = lax.broadcasted_iota(jnp.int32, (width, LANES), 1)
    picks = ((e_lane >= 32) & (e_lane < 80) & (e_lane % 16 == e_row)).astype(F32).astype(BF)
    prod = d_mixed.astype(F32) * mix.astype(F32)
    high = prod.astype(BF)
    low = (prod - high.astype(F32)).astype(BF)
    lane = lax.broadcasted_iota(jnp.int32, (count, LANES), 1)
    daug_out[...] = in_thirds(-(dot(high, picks) + dot(low, picks)), lane)

    @pl.when(i == pl.num_programs(0) - 1)
    def _():
        copies = []
        for stage, pairs in ((narrow, ((a_out, p_out), (a_down, p_down))), (wide, ((a_gate, p_gate), (a_up, p_up)))):
            size, number = stage.shape[1], 0
            for total, payload in pairs:
                for at in range(0, total.shape[0], size):
                    some = min(size, total.shape[0] - at)
                    if number >= 2:
                        copies[-2].wait()
                    slot = number % 2
                    stage[slot, :some] = total[at : at + some, :].astype(BF)
                    copies.append(pltpu.make_async_copy(
                        stage.at[slot, pl.ds(0, some)], payload.at[pl.ds(at, some)], sems.at[len(copies)]
                    ))
                    copies[-1].start()
                    number += 1
            for copy in copies[-2:]:
                copy.wait()


def slots_of(item_lengths, first, count):
    ends = jnp.cumsum(item_lengths[0])[None, :]
    slots = first + jnp.arange(count, dtype=jnp.int32)
    reached = (slots[:, None] >= ends) & (item_lengths[0] > 0)[None, :]
    segment = jnp.sum(reached.astype(jnp.int32), axis=1)
    begin = jnp.max(jnp.where(reached, ends, 0), axis=1)
    return slots, segment % 16, slots - begin


def side_arrays(item_lengths, local_rows, padded):
    offset = lax.axis_index("span") * local_rows
    count = FRONT + padded
    slots, group, position = slots_of(item_lengths, offset - FRONT, count)
    lane = jnp.arange(LANES, dtype=jnp.int32)[None, :]
    away = (slots < 0) | (jnp.arange(count) < FRONT - HALO)
    where_key = jnp.where(away, 16, group)[:, None]
    marks = (lane >= 32) & (lane < 80) & (lane % 16 < 12)
    kaug = ((lane == where_key) | marks).astype(BF)
    qaug = jnp.where((lane <= 16) & (lane != group[FRONT:, None]), AWAY, 0.0).astype(BF)
    half = HEAD_DIM // 2
    frequency = 10000.0 ** (-(lane % half).astype(F32) / half)
    phases = position[:, None].astype(F32) * frequency
    sign = jnp.where(lane % HEAD_DIM < half, -1.0, 1.0)
    return kaug, qaug, jnp.cos(phases), jnp.sin(phases) * sign


def vmem():
    return pl.BlockSpec(memory_space=pltpu.VMEM)


def params(**more):
    return pltpu.CompilerParams(vmem_limit_bytes=VMEM_LIMIT, **more)


def per_device(tokens, item_lengths, attn_gain, w_query, w_key, w_value, w_out, mlp_gain, w_gate, w_up, w_down, cotangent):
    rows, width = tokens.shape[1:]
    ff = w_gate.shape[1]
    padded = -(-rows // ROW_STEP) * ROW_STEP
    ext = FRONT + padded
    axes = ("seq", "span")
    seqs, spans = (lax.axis_size(a) for a in axes)
    direct = (seqs, spans) == (8, 4)
    sds = jax.ShapeDtypeStruct
    anywhere = pl.BlockSpec(memory_space=pl.ANY)
    tok, cot = tokens[0], cotangent[0]

    kaug, qaug, cos, sin = side_arrays(item_lengths, rows, padded)
    fwd_shapes = [
        sds((padded, width), BF), sds((ext, width), BF), sds((ext, width), BF),
        sds((padded, width), BF), sds((padded, LANES), BF),
    ]
    if direct:
        shards = [
            jnp.concatenate([w_query] + [jnp.broadcast_to(v[:, None], (v.shape[0], LANES)) for v in (attn_gain, mlp_gain)], axis=1),
            w_key, w_value, w_out, w_gate, w_up, w_down,
        ]
        whole = [(2, 2, 2, 4 * w.shape[0], w.shape[1]) for w in shards]
        near = []
        for w, _, count in GATHER_CHUNKS:
            depth = shards[w].shape[0]
            near.append((4, 2 * depth, count // 2) if depth % 16 else (4, depth, count))
        results = pl.pallas_call(
            fwd_gather_kernel,
            out_shape=fwd_shapes + [sds((8, width), F32)] + [sds(w, BF) for w in whole],
            in_specs=[vmem()] * 12,
            out_specs=[vmem()] * 6 + [anywhere] * 7,
            scratch_shapes=[pltpu.VMEM((HALO, width), BF)]
            + [pltpu.VMEM(n, BF) for n in near]
            + [pltpu.VMEM(w, BF) for w in whole]
            + [
                pltpu.SemaphoreType.DMA((2, len(GATHER_CHUNKS) * GATHER_COPIES)),
                pltpu.SemaphoreType.DMA((2, 1)),
                pltpu.SemaphoreType.DMA((7,)),
            ],
            compiler_params=params(collective_id=0, has_side_effects=True),
            name="attend",
        )(tok, *shards, kaug, qaug, cos, sin)
        q, k, v, mixed, qaug, gains = results[:6]
        wq, wk, wv, wo, wg, wu, down = (w.reshape(-1, w.shape[-1]) for w in results[6:])
    else:
        packed = lax.all_gather(jnp.concatenate([w_query, w_key, w_value, w_out, w_gate, w_up], axis=1), axes, axis=0, tiled=True)
        down = lax.all_gather(w_down, axes, axis=0, tiled=True)
        gains = lax.all_gather(jnp.stack([attn_gain, mlp_gain], axis=1), axes, axis=0, tiled=True).astype(F32)
        gains = jnp.concatenate([jnp.transpose(gains), jnp.zeros((6, width), F32)], axis=0)
        wq, wk, wv, wo = (packed[:, i * width : (i + 1) * width] for i in range(4))
        wg, wu = packed[:, 4 * width : 4 * width + ff], packed[:, 4 * width + ff :]
        halo = lax.ppermute(tok[rows - HALO :], "span", [(i, i + 1) for i in range(spans - 1)])
        q, k, v, mixed, qaug = pl.pallas_call(
            fwd_kernel,
            out_shape=fwd_shapes,
            in_specs=[vmem()] * 10,
            out_specs=[vmem()] * 5,
            compiler_params=params(),
            name="attend",
        )(tok, halo, wq, wk, wv, gains, kaug, qaug, cos, sin)

    tile = lambda n: pl.BlockSpec((ROW_STEP, n), lambda i: (i, 0))
    whole = lambda a: pl.BlockSpec(a.shape, lambda i: (0, 0), pipeline_mode=pl.Buffered(1))
    weights = (wo, wg, wu, down)
    output, d_resid, d_mixed, daug, *payloads = pl.pallas_call(
        functools.partial(mlp_kernel, rows),
        grid=(padded // ROW_STEP,),
        out_shape=[sds((rows, width), BF), sds((rows, width), F32), sds((padded, width), BF), sds((padded, LANES), BF)]
        + [sds(w.shape, BF) for w in weights],
        in_specs=[tile(width)] * 3 + [whole(a) for a in weights + (gains,)],
        out_specs=[tile(width)] * 3 + [tile(LANES)] + [anywhere] * 4,
        scratch_shapes=[pltpu.VMEM(w.shape, F32) for w in weights] + [
            pltpu.VMEM((2, 512, width), BF), pltpu.VMEM((2, 256, ff), BF), pltpu.SemaphoreType.DMA((16,)),
        ],
        compiler_params=params(),
        name="mlp",
    )(tok, mixed, cot, *weights, gains)

    if direct:
        grouped = [p.reshape(2, 2, 2, p.shape[0] // 8, p.shape[1]) for p in payloads]
        buffers = []
        for w, _, count in SCATTER_CHUNKS:
            buffers += scatter_buffers(grouped[w].shape[3], count)
        for _ in range(3):
            buffers += scatter_buffers(width // 8, width)
        part = 320
        results = pl.pallas_call(
            bwd_scatter_kernel,
            out_shape=[sds((rows, width), BF)] + [sds((width // 32, width), F32)] * 4
            + [sds((width // 32, ff), F32)] * 2 + [sds((ff // 32, width), F32)],
            in_specs=[anywhere] * 4 + [vmem()] * 7 + [anywhere] * 8,
            out_specs=[anywhere] + [vmem()] * 7,
            scratch_shapes=[
                pltpu.VMEM((padded, width), BF), pltpu.VMEM((ext, width), BF), pltpu.VMEM((ext, width), BF),
                pltpu.VMEM((padded, width), BF),
                pltpu.VMEM((WIN // QB, QB, width), F32), pltpu.VMEM((WIN // QB, QB, width), F32),
                pltpu.VMEM((2, FRONT, width), BF), pltpu.VMEM((2, HALO, width), BF),
                pltpu.VMEM((3, width, width), BF),
                pltpu.VMEM((2, part, width), F32), pltpu.VMEM((2, part, width), BF),
                pltpu.VMEM((2, 2, 2, width // 8, 1024), BF), pltpu.VMEM((2, 2, 2, ff // 8, 256), BF),
            ] + buffers + [pltpu.VMEM((2, 2, 2, width // 8, width), BF)] * 3 + [
                pltpu.SemaphoreType.DMA((2, (len(SCATTER_CHUNKS) + 3) * SCATTER_COPIES)),
                pltpu.SemaphoreType.DMA((len(SCATTER_CHUNKS),)),
                pltpu.SemaphoreType.DMA((7,)),
                pltpu.SemaphoreType.DMA((2, 1)),
                pltpu.SemaphoreType.DMA((2, -(-rows // part))),
            ],
            compiler_params=params(collective_id=1, has_side_effects=True),
            name="attend_back",
        )(q, k, v, d_mixed, kaug, qaug, daug, cos, sin, tok, gains, d_resid, wq, wk, wv, *grouped)
        input_grad, g_q, g_k, g_v, g_o, g_g, g_u, g_d = results
    else:
        dq, dk, dv = pl.pallas_call(
            bwd_kernel,
            out_shape=[sds((padded, width), BF), sds((ext, width), F32), sds((ext, width), F32)],
            in_specs=[vmem()] * 9,
            out_specs=[vmem()] * 3,
            compiler_params=params(),
            name="attend_back",
        )(q, k, v, d_mixed, kaug, qaug, daug, cos, sin)
        dq = dq[:rows]
        back = jnp.concatenate([dk[FRONT - HALO : FRONT], dv[FRONT - HALO : FRONT]], axis=1).astype(BF)
        back = lax.ppermute(back, "span", [(i + 1, i) for i in range(spans - 1)]).astype(F32)
        dk, dv = dk[FRONT : FRONT + rows], dv[FRONT : FRONT + rows]
        dk = jnp.concatenate([dk[: rows - HALO], dk[rows - HALO :] + back[:, :width]])
        dv = jnp.concatenate([dv[: rows - HALO], dv[rows - HALO :] + back[:, width:]]).astype(BF)
        half = HEAD_DIM // 2
        c = cos[FRONT : FRONT + rows, None, :HEAD_DIM]
        s = sin[FRONT : FRONT + rows, None, :HEAD_DIM]
        dk3 = dk.reshape(rows, width // HEAD_DIM, HEAD_DIM)
        dk = (dk3 * c - jnp.concatenate([dk3[..., half:], dk3[..., :half]], axis=-1) * s).reshape(rows, width).astype(BF)
        x = tok.astype(F32)
        inv = norm_rows(x)
        hat = x * inv
        gain_one = gains[:1]
        n1 = (hat * gain_one).astype(BF)
        dn = sum(dot_nt(d, w) for d, w in ((dq, wq), (dk, wk), (dv, wv)))
        e = dn * gain_one
        input_grad = (d_resid + inv * (e - hat * jnp.mean(e * hat, axis=-1, keepdims=True))).astype(BF)
        sums = jnp.concatenate([dot_tn(n1, d) for d in (dq, dk, dv)] + [p.astype(F32) for p in payloads[:3]], axis=1)
        scatter = lambda g: lax.psum_scatter(g, axes, scatter_dimension=0, tiled=True)
        sums, g_d = scatter(sums), scatter(payloads[3].astype(F32))
        g_q, g_k, g_v, g_o = (sums[:, i * width : (i + 1) * width] for i in range(4))
        g_g, g_u = sums[:, 4 * width : 4 * width + ff], sums[:, 4 * width + ff :]

    def gain_grad(gain, *pairs):
        return sum(jnp.sum(g * w.astype(F32), axis=1) for g, w in pairs) / gain.astype(F32)

    gain_one_grad = gain_grad(attn_gain, (g_q, w_query), (g_k, w_key), (g_v, w_value))
    gain_two_grad = gain_grad(mlp_gain, (g_g, w_gate), (g_u, w_up))
    return output[None], input_grad[None], gain_one_grad, g_q, g_k, g_v, g_o, gain_two_grad, g_g, g_u, g_d


def solution(mesh):
    rows_placed, vector, matrix = P("seq", "span", None), P(("seq", "span")), P(("seq", "span"), None)
    return jax.shard_map(
        per_device,
        mesh=mesh,
        in_specs=(rows_placed, P("seq", None), vector, matrix, matrix, matrix, matrix, vector, matrix, matrix, matrix, rows_placed),
        out_specs=(rows_placed, rows_placed, vector, matrix, matrix, matrix, matrix, vector, matrix, matrix, matrix),
        check_vma=False,
    )
```

```python
import functools

import jax
import jax.numpy as jnp
from jax import lax
from jax.experimental import pallas as pl
from jax.experimental.pallas import tpu as pltpu
from jax.sharding import PartitionSpec as P

HEAD_DIM = 64
HALO = 576
FRONT = 640
QB = 128
WIN = FRONT + QB
LANES = 128
EPS = 1e-5
SCALE = 0.125
AWAY = -1e30
BF = jnp.bfloat16
F32 = jnp.float32
VMEM_LIMIT = 63 * 1024 * 1024


def dot(a, b):
    return lax.dot_general(a, b, (((1,), (0,)), ((), ())), preferred_element_type=F32)


def dot_nt(a, b):
    return lax.dot_general(a, b, (((1,), (1,)), ((), ())), preferred_element_type=F32)


def dot_tn(a, b):
    return lax.dot_general(a, b, (((0,), (0,)), ((), ())), preferred_element_type=F32)


def rotated(v, cos, sin):
    lane = lax.broadcasted_iota(jnp.int32, v.shape, 1)
    swapped = jnp.where(lane % 64 < 32, pltpu.roll(v, 96, 1), pltpu.roll(v, 32, 1))
    return v * cos + swapped * sin


def turns(table):
    first = lax.broadcasted_iota(jnp.int32, table.shape, 1) % 64 < 32
    cos = jnp.where(first, table, pltpu.roll(table, 32, 1))
    sin = jnp.where(first, -pltpu.roll(table, 96, 1), table)
    return cos, sin


def both_heads(v):
    lane = lax.broadcasted_iota(jnp.int32, v.shape, 1)
    zero = jnp.zeros_like(v)
    return jnp.concatenate([jnp.where(lane < 64, v, zero), jnp.where(lane < 64, zero, v)], axis=0)


def one_of_both(v):
    rows = v.shape[0] // 2
    lane = lax.broadcasted_iota(jnp.int32, (rows, v.shape[1]), 1)
    return jnp.where(lane < 64, v[:rows], v[rows:])


def norm_rows(x):
    return lax.rsqrt(jnp.mean(x * x, axis=-1, keepdims=True) + EPS)


def in_thirds(v, lane):
    high = v.astype(BF)
    rest = v - high.astype(F32)
    middle = rest.astype(BF)
    last = (rest - middle.astype(F32)).astype(BF)
    return jnp.where(lane < 48, high, jnp.where(lane < 64, middle, last))


def coordinates():
    seq, span = lax.axis_index("seq"), lax.axis_index("span")
    return seq // 4, seq // 2 % 2, seq % 2, span


def device(y, x, core, span):
    return (y * 4 + x * 2 + core, span)


def greet():
    y, x, core, span = coordinates()
    barrier = pltpu.get_barrier_semaphore()
    peers = [device(y, x, core, (span + d) % 4) for d in (1, 2, 3)]
    peers += [device(1 - y, x, core, span), device(y, 1 - x, core, span), device(y, x, 1 - core, span)]
    for peer in peers:
        pl.semaphore_signal(barrier, inc=1, device_id=peer, device_id_type=pl.DeviceIdType.MESH)
    pl.semaphore_wait(barrier, len(peers))


def remote(src, dst, sems, at, to):
    return pltpu.make_async_remote_copy(
        src_ref=src, dst_ref=dst, send_sem=sems.at[0, at], recv_sem=sems.at[1, at], device_id=to,
        device_id_type=pl.DeviceIdType.MESH,
    )


GATHER_COPIES = 8


class Gathered:
    def __init__(self, shard, near, whole, at, count, sems, number):
        self.shard, self.near, self.whole, self.sems = shard, near, whole, sems
        self.first = number * GATHER_COPIES
        self.split = shard.shape[0] % 16 != 0
        self.columns = pl.ds(at, count)
        y, x, core, span = coordinates()
        half = count // 2
        left, right = pl.ds(at, half), pl.ds(at + half, half)
        over_y, over_x = device(1 - y, x, core, span), device(y, 1 - x, core, span)
        own = whole.at[y, x, core]
        rows = pl.ds(0, own.shape[0])
        refs = [(near.at[0], near.at[d], device(y, x, core, (span + d) % 4)) for d in (1, 2, 3)]
        refs += [(r, r, to) for r, to in (
            (whole.at[y, x, core, rows, left], over_y),
            (whole.at[y, x, core, rows, right], over_x),
            (whole.at[pl.ds(0, 2), x, core, rows, left], over_x),
            (whole.at[y, pl.ds(0, 2), core, rows, right], over_y),
            (whole.at[pl.ds(0, 2), pl.ds(0, 2), core, rows, self.columns], device(y, x, 1 - core, span)),
        )]
        self.copies = [remote(src, dst, sems, self.first + i, to) for i, (src, dst, to) in enumerate(refs)]

    def go(self, stage):
        if stage == 0:
            v = self.shard[:, self.columns]
            if self.split:
                half = v.shape[1] // 2
                v = v.astype(F32)
                v = jnp.concatenate([v[:, :half], v[:, half:]], axis=0).astype(BF)
            self.near[0] = v
            for i in (0, 1, 2):
                self.copies[i].start()
        if stage == 1:
            y, x, core, span = coordinates()
            for i in (0, 1, 2):
                self.copies[i].wait_recv()
            pieces = []
            for s in range(4):
                v = self.near[(span - s + 4) % 4]
                if self.split:
                    v = v.astype(F32)
                    half = v.shape[0] // 2
                    v = jnp.concatenate([v[:half], v[half:]], axis=1)
                pieces.append(v)
            self.whole[y, x, core, :, self.columns] = jnp.concatenate(pieces, axis=0).astype(BF)
            for i in (3, 4):
                self.copies[i].start()
        if stage == 2:
            for i in (3, 4):
                self.copies[i].wait_recv()
            for i in (5, 6):
                self.copies[i].start()
        if stage == 3:
            for i in (5, 6):
                self.copies[i].wait_recv()
            self.copies[7].start()
        if stage == 4:
            self.copies[7].wait_recv()

    def finish(self):
        for c in self.copies:
            c.wait_send()


def attention_forward(refs, q_out, k_out, v_out, mixed_out, qaug_out, normed_out, steps, tick):
    tok, halo, weights, gain, kaug, qaug, table = refs
    rows, width = tok.shape
    padded = q_out.shape[0]
    pairs = width // LANES

    def normal(x):
        x = x.astype(F32)
        return (x * norm_rows(x) * gain[0:1, :]).astype(BF)

    def project(which, normed, key_at, query_at):
        count = normed.shape[0]
        product = dot(normed, weights[which]())
        if which == 2:
            v_out[key_at : key_at + count, :] = product.astype(BF)
            return
        c, s = turns(table[key_at : key_at + count, :])
        for t in range(pairs):
            lanes = slice(t * LANES, (t + 1) * LANES)
            turned = rotated(product[:, lanes], c, s)
            if which == 0:
                q_out[query_at : query_at + count, lanes] = (turned * SCALE).astype(BF)
            else:
                k_out[key_at : key_at + count, lanes] = turned.astype(BF)

    lead = FRONT - HALO
    k_out[:lead, :] = jnp.zeros((lead, width), BF)
    v_out[:lead, :] = jnp.zeros((lead, width), BF)
    if padded > rows:
        blank = jnp.zeros((padded - rows, width), BF)
        q_out[rows:, :] = blank
        k_out[FRONT + rows :, :] = blank
        v_out[FRONT + rows :, :] = blank
    parts = [(at, min(480, rows - at)) for at in range(0, rows, 480)]
    for which in range(3):
        steps(which)
        for at, count in parts:
            if which == 0:
                normed_out[at : at + count, :] = normal(tok[at : at + count, :])
            project(which, normed_out[at : at + count, :], FRONT + at, at)

    lane = lax.broadcasted_iota(jnp.int32, (QB, LANES), 1)
    row = lax.broadcasted_iota(jnp.int32, (2 * QB, QB), 0)
    behind = lax.broadcasted_iota(jnp.int32, (2 * QB, QB), 1) <= row % QB

    blocks = padded // QB

    def block(i, carry):
        tick(i)

        @pl.when(i == blocks - FRONT // QB)
        def _():
            steps(3)
            normed = normal(halo[...])
            for which in (1, 2):
                project(which, normed, lead, None)

        start = pl.multiple_of((blocks - 1 - i) * QB, QB)
        k_a = kaug[pl.ds(start, WIN), :]
        q_a = qaug[pl.ds(start, QB), :]
        q_a2 = jnp.concatenate([q_a, q_a], axis=0)
        logs = jnp.zeros((QB, LANES), F32)
        for t in range(pairs):
            at = slice(t * LANES, (t + 1) * LANES)
            q2 = jnp.concatenate([both_heads(q_out[pl.ds(start, QB), at]), q_a2], axis=1)
            k2 = jnp.concatenate([k_out[pl.ds(start, WIN), at], k_a], axis=1)
            s = dot_nt(q2, k2)
            s = jnp.concatenate([s[:, :FRONT], jnp.where(behind, s[:, FRONT:], AWAY)], axis=1)
            top = jnp.max(s, axis=1, keepdims=True)
            p = jnp.exp(s - top).astype(BF)
            v = v_out[pl.ds(start, WIN), at]
            o = dot(p, jnp.concatenate([v, jnp.ones_like(v)], axis=1))
            total = o[:, LANES:]
            mixed_out[pl.ds(start, QB), at] = one_of_both(o[:, :LANES] / total).astype(BF)
            log = top + jnp.log(total)
            for e in range(2):
                h = 2 * t + e
                mine = (lane == 32 + h) | (lane == 48 + h) | (lane == 64 + h)
                logs = jnp.where(mine, log[e * QB : (e + 1) * QB], logs)
        qaug_out[pl.ds(start, QB), :] = jnp.where(lane < 32, q_a, in_thirds(-logs, lane))
        return carry

    lax.fori_loop(0, blocks, block, 0)


def fwd_kernel(tok, halo, wq, wk, wv, gain, kaug, qaug, table, q_out, k_out, v_out, mixed_out, qaug_out, normed_out):
    weights = [lambda w=w: w[...] for w in (wq, wk, wv)]
    refs = (tok, halo, weights, gain, kaug, qaug, table)
    attention_forward(refs, q_out, k_out, v_out, mixed_out, qaug_out, normed_out, lambda which: None, lambda b: None)


GATHER_CHUNKS = (
    (0, 0, 1024), (1, 0, 768), (2, 0, 768), (3, 0, 768), (4, 0, 1024), (4, 1024, 1024), (5, 0, 1024), (5, 1024, 1024),
    (6, 0, 256), (6, 256, 256), (6, 512, 256),
)
HALO_AFTER = (10, 1)
GATHER_FAST = 3


def gather_plan():
    ticks, end = [[] for _ in range(40)], []
    for chunk in range(len(GATHER_CHUNKS)):
        for stage in range(5):
            if chunk < GATHER_FAST:
                ticks[chunk + stage].append((chunk, stage))
            elif stage < 4:
                ticks[chunk + (0, 2, 5, 8)[stage]].append((chunk, stage))
            else:
                end.append((chunk, stage))
    return [sum(ticks[:5], []), ticks[5], ticks[6]], ticks[7:], end


def fwd_gather_kernel(tok, *refs):
    shards, refs = refs[:7], refs[7:]
    kaug, qaug, table = refs[:3]
    outs, refs = refs[3:9], refs[9:]
    gains, refs = refs[0], refs[1:]
    whole_outs, refs = refs[:7], refs[7:]
    n = len(GATHER_CHUNKS)
    halo, nears, wholes = refs[0], refs[1 : n + 1], refs[n + 1 : n + 8]
    sems, halo_sems, out_sems = refs[n + 8 :]
    rows, width = tok.shape
    y, x, core, span = coordinates()
    greet()
    to_next = remote(tok.at[pl.ds(rows - HALO, HALO)], halo, halo_sems, 0, device(y, x, core, (span + 1) % 4))

    chunks = [
        Gathered(shards[w], nears[i], wholes[w], at, count, sems, i) for i, (w, at, count) in enumerate(GATHER_CHUNKS)
    ]
    out_copies = [pltpu.make_async_copy(w, o, out_sems.at[i]) for i, (w, o) in enumerate(zip(wholes, whole_outs))]

    early, late, end = gather_plan()

    def go(chunk, stage):
        chunks[chunk].go(stage)
        if (chunk, stage) == HALO_AFTER:
            to_next.start()
        w, at, count = GATHER_CHUNKS[chunk]
        if stage == 4 and at + count == wholes[w].shape[-1]:
            out_copies[w].start()

    def steps(which):
        if which == 3:
            to_next.wait_recv()
            return
        for chunk, stage in early[which]:
            go(chunk, stage)
        if which == 0:
            both = wholes[0][...].reshape(width, -1)[:, width:].astype(F32)
            both = [jnp.transpose(both[:, i * LANES : (i + 1) * LANES])[:1] for i in range(2)]
            gains[...] = jnp.concatenate(both + [jnp.zeros((6, width), F32)], axis=0)

    def tick(b):
        for i, todo in enumerate(late):
            if todo:
                @pl.when(b == i)
                def _():
                    for chunk, stage in todo:
                        go(chunk, stage)

    weights = [lambda w=w: w[...].reshape(width, w.shape[-1])[:, :width] for w in wholes[:3]]
    attention_forward((tok, halo, weights, gains, kaug, qaug, table), *outs, steps, tick)
    for chunk, stage in end:
        go(chunk, stage)
    to_next.wait_send()
    for c in chunks:
        c.finish()
    for c in out_copies:
        c.wait()


def attention_backward(b, refs, dq_out, add):
    q, k, v, dmixed, kaug, qaug, daug, table = refs
    width = q.shape[1]
    lead = FRONT - HALO
    lane = lax.broadcasted_iota(jnp.int32, (QB, LANES), 1)
    key_row = lax.broadcasted_iota(jnp.int32, (QB, 2 * QB), 0)
    behind = key_row <= lax.broadcasted_iota(jnp.int32, (QB, 2 * QB), 1) % QB
    start = pl.multiple_of(b * QB, QB)
    keys = pl.ds(pl.multiple_of(start + lead, lead), WIN - lead)
    k_a = kaug[keys, :]
    q_a = qaug[pl.ds(start, QB), :]
    d_a = daug[pl.ds(start, QB), :]
    c, s_ = turns(table[pl.ds(start + FRONT, QB), :])
    zero = jnp.zeros_like(q_a)
    for t in range(width // LANES):
        at = slice(t * LANES, (t + 1) * LANES)
        mine = [(lane >= 32) & (lane % 16 == 2 * t + e) for e in range(2)]
        q_2 = both_heads(q[pl.ds(start, QB), at])
        q_aug = jnp.concatenate([jnp.where((lane < 32) | mine[e], q_a, zero) for e in range(2)], axis=0)
        d_2 = both_heads(dmixed[pl.ds(start, QB), at])
        d_aug = jnp.concatenate([jnp.where(mine[e], d_a, zero) for e in range(2)], axis=0)
        k_p = k[keys, at]
        st = dot_nt(jnp.concatenate([k_p, k_a], axis=1), jnp.concatenate([q_2, q_aug], axis=1))
        st = jnp.concatenate([st[:HALO], jnp.where(behind, st[HALO:], AWAY)], axis=0)
        pt = jnp.exp(st)
        dpt = dot_nt(jnp.concatenate([v[keys, at], k_a], axis=1), jnp.concatenate([d_2, d_aug], axis=1))
        dst = (pt * dpt).astype(BF)
        add(t, dot(dst, q_2), dot(pt.astype(BF), d_2))
        dq = one_of_both(dot_tn(dst, k_p)) * SCALE
        dq_out[pl.ds(start, QB), at] = rotated(dq, c, -s_).astype(BF)


def bwd_kernel(*refs):
    dq_out, dk_out, dv_out = refs[8:]
    padded = dq_out.shape[0]
    dk_out[...] = jnp.zeros_like(dk_out)
    dv_out[...] = jnp.zeros_like(dv_out)
    lead = FRONT - HALO

    def block(b, carry):
        keys = pl.ds(pl.multiple_of(b * QB + lead, lead), WIN - lead)

        def add(t, dk, dv):
            at = slice(t * LANES, (t + 1) * LANES)
            dk_out[keys, at] += dk
            dv_out[keys, at] += dv

        attention_backward(b, refs[:8], dq_out, add)
        return carry

    lax.fori_loop(0, padded // QB, block, 0)


SCATTER_COPIES = 8
SCATTER_CHUNKS = (
    (0, 0, 768), (1, 0, 1024), (1, 1024, 1024), (2, 0, 1024), (2, 1024, 1024), (3, 0, 256), (3, 256, 256), (3, 512, 256),
)
SUB = 512
SUB_SLOTS = 2
TALL = 256


class Scattered:
    def __init__(self, whole, at, count, out, bufs, sems, number):
        self.whole, self.out = whole, out
        self.got, self.left, self.right, self.left_2, self.right_2, self.near, self.far = bufs
        self.at, self.count = at, count
        self.columns = pl.ds(0, count)
        self.half = half = count // 2
        self.left_whole = False
        y, x, core, span = coordinates()
        rows = pl.ds(0, whole.shape[3])
        two = pl.ds(0, 2)
        lo, hi = pl.ds(0, half), pl.ds(half, half)
        over_y, over_x = device(1 - y, x, core, span), device(y, 1 - x, core, span)
        got = self.got
        refs = [
            (whole.at[two, two, 1 - core, rows, self.columns], got, device(y, x, 1 - core, span)),
            (got.at[two, 1 - x, rows, lo], self.left, over_x),
            (got.at[1 - y, two, rows, hi], self.right, over_y),
            (got.at[1 - y, x, rows, lo], self.left_2, over_y),
            (got.at[y, 1 - x, rows, hi], self.right_2, over_x),
        ]
        refs += [(self.near.at[(span + d) % 4], self.far.at[d - 1], device(y, x, core, (span + d) % 4)) for d in (1, 2, 3)]
        first = number * SCATTER_COPIES
        self.copies = [remote(src, dst, sems, first + i, to) for i, (src, dst, to) in enumerate(refs)]
    def go(self, stage):
        y, x, core, span = coordinates()
        got, half = self.got, self.half
        lo, hi = pl.ds(0, half), pl.ds(half, half)
        if stage == 0:
            self.copies[0].start()
        if stage == 1:
            self.copies[0].wait_recv()
            for i in range(2):
                for j in range(2):
                    got[i, j] = got[i, j] + self.whole[i, j, core, :, self.columns]
            for i in (1, 2):
                self.copies[i].start()
        if stage == 2:
            for i in (1, 2):
                self.copies[i].wait_recv()
            for i in range(2):
                got[i, x, :, lo] = got[i, x, :, lo] + self.left[i]
                got[y, i, :, hi] = got[y, i, :, hi] + self.right[i]
            for i in (3, 4):
                self.copies[i].start()
        if stage == 3:
            for i in (3, 4):
                self.copies[i].wait_recv()
            total = jnp.concatenate(
                [got[y, x, :, r].astype(F32) + other[...].astype(F32) for r, other in ((lo, self.left_2), (hi, self.right_2))],
                axis=1,
            )
            depth = total.shape[0] // 4
            for s in range(4):
                v = total[s * depth : (s + 1) * depth]
                if depth % 16:
                    v = jnp.concatenate([v[:, :half], v[:, half:]], axis=0)
                self.near[s] = v.astype(BF)
            for i in (5, 6, 7):
                self.copies[i].start()
        if stage == 4:
            for i in (5, 6, 7):
                self.copies[i].wait_recv()
            v = self.near[span].astype(F32)
            for d in range(3):
                v = v + self.far[d].astype(F32)
            depth = self.out.shape[0]
            if depth % 16:
                v = jnp.concatenate([v[:depth], v[depth:]], axis=1)
            self.out[:, self.at : self.at + self.count] = v

    def leave_whole(self):
        if not self.left_whole:
            self.copies[0].wait_send()
        self.left_whole = True

    def finish(self):
        self.leave_whole()
        for c in self.copies[1:]:
            c.wait_send()


def scatter_buffers(rows, count):
    depth = rows // 4
    piece = (2 * depth, count // 2) if depth % 16 else (depth, count)
    shapes = [
        (2, 2, rows, count), (2, rows, count // 2), (2, rows, count // 2), (rows, count // 2), (rows, count // 2),
        (4,) + piece, (3,) + piece,
    ]
    return [pltpu.VMEM(shape, BF) for shape in shapes]


HALO_BLOCKS = FRONT // QB
SCATTER_AT = (
    (0, 1, 3, 4, 8), (5, 6, 8, 9, 12), (6, 7, 9, 13, 16), (7, 8, 9, 13, 16), (8, 9, 13, 17, 19),
    (9, 11, 17, 20, 22), (9, 11, 17, 20, 22), (9, 11, 17, 20, 22),
)


def scatter_plan(blocks):
    ticks, after = [[] for _ in range(blocks + 5)], []
    events = sorted((t, j, stage) for j, when in enumerate(SCATTER_AT) for stage, t in enumerate(when))
    for t, j, stage in events:
        (ticks[t] if t < len(ticks) else after).append((j, stage))
    return ticks, after


def bwd_scatter_kernel(
    q_in, k_in, v_in, dmixed_in, kaug, qaug, daug, table, tok, gains, d_resid, wq_in, wk_in, wv_in,
    normed_in, g_out, n2_in, cot_in, hid_in, dg_in, du_in,
    input_grad, s_query, s_key, s_value, s_out, s_gate, s_up, s_down,
    q, k, v, dmixed, dk_win, dv_win, halo_out, halo_in, resid_block, out_block, subs, wide, tall, *refs,
):
    rows, width = tok.shape
    padded = q.shape[0]
    blocks = padded // QB
    pairs = width // LANES
    lead = FRONT - HALO
    slots = WIN // QB
    n = len(SCATTER_CHUNKS)
    chunk_bufs = [refs[7 * i : 7 * i + 7] for i in range(n + 3)]
    refs = refs[7 * (n + 3) :]
    sems, in_sems, sub_sems, halo_sems, block_sems = refs
    y, x, core, span = coordinates()

    near_q, near_k = HALO_BLOCKS * QB, 2 * FRONT
    far_q = pl.ds(near_q, padded - near_q)
    lower, upper = pl.ds(0, padded - near_q), pl.ds(padded - near_q, near_q)
    upper_c = pl.ds(padded - near_q, rows - padded + near_q)
    far_k = pl.ds(near_k, near_q)
    rest = pl.ds(near_k + near_q, k.shape[0] - near_k - near_q)
    one, two = pl.ds(0, near_q), pl.ds(0, near_k)
    weights = [halo_out.at[0], halo_out.at[1], halo_in.at[0]]
    by_name = dict(
        q=(q_in.at[one], q.at[one]), k=(k_in.at[two], k.at[two]), v=(v_in.at[two], v.at[two]),
        d=(dmixed_in.at[one], dmixed.at[one]),
        o=(g_out, wide.at[0, pl.ds(0, 2), pl.ds(0, 2), pl.ds(0, 2), pl.ds(0, width // 8), pl.ds(0, width)]),
        n_low=(n2_in.at[lower], q.at[far_q]), n_high=(n2_in.at[upper], k.at[far_k]),
        c_low=(cot_in.at[lower], dmixed.at[far_q]),
        c_high=(cot_in.at[upper_c], v.at[pl.ds(near_k, rows - padded + near_q)]),
        k_rest=(k_in.at[rest], k.at[rest]), v_rest=(v_in.at[rest], v.at[rest]),
        q_far=(q_in.at[far_q], q.at[far_q]), k_far=(k_in.at[far_k], k.at[far_k]),
        d_far=(dmixed_in.at[far_q], dmixed.at[far_q]), v_far=(v_in.at[far_k], v.at[far_k]),
        w_q=(wq_in.at[pl.ds(0, width), pl.ds(0, width)], weights[0]),
        w_k=(wk_in, weights[1]), w_v=(wv_in, weights[2]),
        normed=(normed_in, dmixed.at[pl.ds(0, rows)]),
    )
    arrivals = {
        name: pltpu.make_async_copy(src, dst, in_sems.at[i]) for i, (name, (src, dst)) in enumerate(by_name.items())
    }
    brought = [(src, f) for src in (dg_in, du_in, hid_in) for f in range(src.shape[0])]
    sub_copies = [
        pltpu.make_async_copy(src.at[f], subs.at[i % SUB_SLOTS], sub_sems.at[i])
        for i, (src, f) in enumerate(brought)
    ]

    def bring(*names):
        for name in names:
            arrivals[name].start()

    def await_all(*names):
        for name in names:
            arrivals[name].wait()

    bring("o", "q", "k", "v", "d", "n_low", "n_high", "c_low", "c_high", "k_rest", "v_rest")
    for c in sub_copies[:SUB_SLOTS]:
        c.start()
    greet()

    sums = (s_out, s_gate, s_up, s_down)
    chunks = []
    for i, (w, at, count) in enumerate(SCATTER_CHUNKS):
        whole = wide.at[i % 3] if w < 3 else tall.at[at // count]
        chunks.append(Scattered(whole, at, count, sums[w], chunk_bufs[i], sems, i))
    own = [wide.at[i] for i in (2, 0, 1)]
    chunks += [
        Scattered(own[i], 0, width, (s_query, s_key, s_value)[i], chunk_bufs[n + i], sems, n + i) for i in range(3)
    ]
    to_last = remote(
        halo_out.at[pl.ds(0, 2), pl.ds(0, HALO)], halo_in.at[pl.ds(0, 2), pl.ds(0, HALO)], halo_sems, 0, device(y, x, core, (span + 3) % 4))
    ticks, after = scatter_plan(blocks)
    dk_win[...] = jnp.zeros_like(dk_win)
    dv_win[...] = jnp.zeros_like(dv_win)
    await_all("o", "q", "k", "v", "d")

    def block_of(inside):
        return functools.partial(block, inside)

    def block(inside, b, carry):
        for i, todo in inside.items():
            if todo:
                @pl.when(b == i)
                def _():
                    for chunk, stage in todo:
                        chunks[chunk].go(stage)

        def add(t, dk, dv):
            at = slice(t * LANES, (t + 1) * LANES)
            for win, grad in ((dk_win, dk), (dv_win, dv)):
                for j in range(slots):
                    count = min(QB, WIN - lead - j * QB)
                    win[lax.rem(b + j, slots), :count, at] += grad[j * QB : j * QB + count]

        attention_backward(b, (q, k, v, dmixed, kaug, qaug, daug, table), q, add)

        slot = lax.rem(b, slots)
        at = pl.ds(pl.multiple_of(b * QB + lead, lead), QB)

        @pl.when(b < FRONT // QB)
        def _():
            to = pl.ds(pl.multiple_of(b * QB, QB), QB)
            halo_out[0, to, :] = dk_win[slot].astype(BF)
            halo_out[1, to, :] = dv_win[slot].astype(BF)

        @pl.when((b >= FRONT // QB - 1) & (b < blocks - 1))
        def _():
            c, s_ = turns(table[at, :])
            for t in range(pairs):
                lanes = slice(t * LANES, (t + 1) * LANES)
                k[at, lanes] = rotated(dk_win[slot, :, lanes], c, -s_).astype(BF)
            v[at, :] = dv_win[slot].astype(BF)

        @pl.when(b < blocks - 1)
        def _():
            dk_win[slot] = jnp.zeros((QB, width), F32)
            dv_win[slot] = jnp.zeros((QB, width), F32)

        return carry

    lax.fori_loop(0, HALO_BLOCKS, block_of({b: ticks[b] for b in range(HALO_BLOCKS)}), 0)
    to_last.start()

    sub = 0
    low, high, group = padded - near_q, padded, tall.shape[4]
    await_all("n_low", "n_high")
    for i, (w, at, count) in enumerate(SCATTER_CHUNKS):
        if w == 0 or (w == 3 and at > 0):
            continue
        if w < 3 and i >= 3:
            chunks[i - 3].leave_whole()
        if w == 3:
            bring("q_far", "k_far")
            await_all("c_low", "c_high")
            v[near_k + rows - low : near_k + near_q, :] = jnp.zeros((padded - rows, width), BF)
        for f in range(0, count if w < 3 else hid_in.shape[0] * SUB, SUB):
            sub_copies[sub].wait()
            here = subs.at[sub % SUB_SLOTS]
            if w < 3:
                total = dot_tn(q[near_q:, :], here[:low, :]) + dot_tn(k[near_k : near_k + near_q, :], here[low:, :])
                wide[i % 3, :, :, :, :, f : f + SUB] = total.reshape(2, 2, 2, width // 8, SUB).astype(BF)
            else:
                total = dot_tn(here[:low, :], dmixed[near_q:, :]) + dot_tn(here[low:, :], v[near_k : near_k + near_q, :])
                total = total.astype(BF)
                for r in range(0, SUB, group):
                    g = (f + r) // group
                    for j in range(width // TALL):
                        tall[j, g // 4, g // 2 % 2, g % 2] = total[r : r + group, j * TALL : (j + 1) * TALL]
            if sub + SUB_SLOTS < len(sub_copies):
                sub_copies[sub + SUB_SLOTS].start()
            sub += 1
        if w == 3:
            bring("d_far", "v_far")
        for chunk, stage in ticks[HALO_BLOCKS + min(i, 5) - 1]:
            chunks[chunk].go(stage)
    await_all("q_far", "k_far", "d_far", "v_far", "k_rest", "v_rest")
    lax.fori_loop(HALO_BLOCKS, blocks, block_of({b: ticks[b + 5] for b in range(HALO_BLOCKS, blocks)}), 0)
    bring("normed")
    to_last.wait_send()
    bring("w_q", "w_k")

    step = resid_block.shape[1]
    parts = [(at, min(step, rows - at)) for at in range(0, rows, step)]
    resid_in = [
        pltpu.make_async_copy(
            d_resid.at[pl.ds(at, count)], resid_block.at[i % 2, pl.ds(0, count)], block_sems.at[0, i]
        ) for i, (at, count) in enumerate(parts)
    ]
    grad_copies = [
        pltpu.make_async_copy(
            out_block.at[i % 2, pl.ds(0, count)], input_grad.at[pl.ds(at, count)], block_sems.at[1, i]
        ) for i, (at, count) in enumerate(parts)
    ]
    resid_in[0].start()
    resid_in[1].start()
    todo = list(after)

    def events(count):
        for chunk, stage in todo[:count]:
            chunks[chunk].go(stage)
        del todo[:count]

    g = gains[0:1, :]
    normed = dmixed
    await_all("normed")

    def weight_grad(i, grad):
        for j in range(2):
            half = width // 2
            total = dot_tn(normed[:rows, j * half : (j + 1) * half], grad)
            own[i][j, :, :, :, pl.ds(0, width)] = total.reshape(2, 2, half // 4, width).astype(BF)

    for i in (2, 3, 4):
        chunks[i].leave_whole()
    weight_grad(0, q[:rows, :])
    chunks[n].go(0)
    events(2)
    to_last.wait_recv()
    for j in range(slots):
        base = (blocks - 1) * QB + lead + j * QB
        slot = (blocks - 1 + j) % slots
        count = min(QB, FRONT + rows - base)
        first = max(base, FRONT + rows - HALO)
        for which, win, whole in ((0, dk_win, k), (1, dv_win, v)):
            grad = win[slot, :count, :]
            more = halo_in[which, first - (FRONT + rows - HALO) : base + count - (FRONT + rows - HALO), :].astype(F32)
            if first > base:
                more = jnp.concatenate([jnp.zeros((first - base, width), F32), more], axis=0)
            grad = grad + more
            if which:
                whole[base : base + count, :] = grad.astype(BF)
                continue
            c, s_ = turns(table[base : base + count, :])
            for t in range(pairs):
                lanes = slice(t * LANES, (t + 1) * LANES)
                whole[base : base + count, lanes] = rotated(grad[:, lanes], c, -s_).astype(BF)
    bring("w_v")
    weight_grad(1, k[FRONT : FRONT + rows, :])
    chunks[n].go(1)
    chunks[n + 1].go(0)
    events(2)
    weight_grad(2, v[FRONT : FRONT + rows, :])
    chunks[n].go(2)
    chunks[n + 1].go(1)
    chunks[n + 2].go(0)
    events(2)
    await_all("w_q", "w_k", "w_v")
    between = (((0, 3), (1, 2), (2, 1)), ((1, 3), (2, 2)), ((0, 4), (2, 3)), ((1, 4),), ((2, 4),))
    for i, (at, count) in enumerate(parts):
        grads = (q[at : at + count, :], k[FRONT + at : FRONT + at + count, :], v[FRONT + at : FRONT + at + count, :])
        dn = sum(dot_nt(d, weights[w][...]) for w, d in enumerate(grads))
        x = tok[at : at + count, :].astype(F32)
        inv = norm_rows(x)
        hat = x * inv
        e = dn * g
        resid_in[i].wait()
        total = resid_block[i % 2, :count] + inv * (e - hat * jnp.mean(e * hat, axis=-1, keepdims=True))
        if i >= 2:
            grad_copies[i - 2].wait()
        out_block[i % 2, :count] = total.astype(BF)
        grad_copies[i].start()
        if i + 2 < len(parts):
            resid_in[i + 2].start()
        events(1)
        for chunk, stage in between[i] if i < len(between) else ():
            chunks[n + chunk].go(stage)
    events(len(todo))
    for c in chunks:
        c.finish()
    for c in grad_copies[-2:]:
        c.wait()


FF_STEP = 512
ROW_STEP = 480


def mlp_kernel(rows, x_ref, mixed, c_ref, wo, wg, wu, wd, gains,
               out, d_resid_out, d_mixed_out, daug_out, grad_out, n2_out, hid_out, dg_out, du_out, total):
    i = pl.program_id(0)
    count, width = x_ref.shape
    valid = lax.broadcasted_iota(jnp.int32, (count, width), 0) + i * count < rows
    c = jnp.where(valid, c_ref[...], jnp.zeros((count, width), BF))
    x = jnp.where(valid, x_ref[...].astype(F32), 0.0)
    mix = mixed[...]
    resid = x + dot(mix, wo[...])
    r = norm_rows(resid)
    g = gains[1:2, :]
    hat = resid * r
    n2 = (hat * g).astype(BF)
    n2_out[...] = n2
    acc = resid
    dn = jnp.zeros((count, width), F32)
    for f in range(0, wg.shape[1], FF_STEP):
        at = slice(f, f + FF_STEP)
        gate = dot(n2, wg[:, at])
        up = dot(n2, wu[:, at])
        sig = jax.nn.sigmoid(gate)
        silu = gate * sig
        hid = (silu * up).astype(BF)
        for j in range(0, FF_STEP, SUB):
            hid_out[(f + j) // SUB] = hid[:, j : j + SUB]
        acc = acc + dot(hid, wd[at, :])
        dh = dot_nt(c, wd[at, :])
        dg = (dh * up * sig * (1.0 + gate * (1.0 - sig))).astype(BF)
        du = (dh * silu).astype(BF)
        for j in range(0, FF_STEP, SUB):
            dg_out[(f + j) // SUB] = dg[:, j : j + SUB]
            du_out[(f + j) // SUB] = du[:, j : j + SUB]
        dn = dn + dot_nt(dg, wg[:, at]) + dot_nt(du, wu[:, at])
    out[...] = acc.astype(BF)
    e = dn * g
    d_resid = c.astype(F32) + r * (e - hat * jnp.mean(e * hat, axis=-1, keepdims=True))
    d_resid_out[...] = d_resid
    d_branch = d_resid.astype(BF)
    total[...] = jnp.where(i == 0, 0.0, total[...]) + dot_tn(mix, d_branch)

    @pl.when(i == pl.num_programs(0) - 1)
    def _():
        grad_out[...] = total[...].astype(BF)

    d_mixed = dot_nt(d_branch, wo[...]).astype(BF)
    d_mixed_out[...] = d_mixed

    e_row = lax.broadcasted_iota(jnp.int32, (width, LANES), 0) // HEAD_DIM
    e_lane = lax.broadcasted_iota(jnp.int32, (width, LANES), 1)
    picks = ((e_lane >= 32) & (e_lane < 80) & (e_lane % 16 == e_row)).astype(F32).astype(BF)
    prod = d_mixed.astype(F32) * mix.astype(F32)
    high = prod.astype(BF)
    low = (prod - high.astype(F32)).astype(BF)
    lane = lax.broadcasted_iota(jnp.int32, (count, LANES), 1)
    daug_out[...] = in_thirds(-(dot(high, picks) + dot(low, picks)), lane)


def slots_of(item_lengths, first, count):
    ends = jnp.cumsum(item_lengths[0])[None, :]
    slots = first + jnp.arange(count, dtype=jnp.int32)
    reached = (slots[:, None] >= ends) & (item_lengths[0] > 0)[None, :]
    segment = jnp.sum(reached.astype(jnp.int32), axis=1)
    begin = jnp.max(jnp.where(reached, ends, 0), axis=1)
    return slots, segment % 16, slots - begin


def side_arrays(item_lengths, local_rows, padded):
    offset = lax.axis_index("span") * local_rows
    count = FRONT + padded
    slots, group, position = slots_of(item_lengths, offset - FRONT, count)
    lane = jnp.arange(LANES, dtype=jnp.int32)[None, :]
    away = (slots < 0) | (jnp.arange(count) < FRONT - HALO)
    where_key = jnp.where(away, 16, group)[:, None]
    marks = (lane >= 32) & (lane < 80) & (lane % 16 < 12)
    kaug = ((lane == where_key) | marks).astype(BF)
    qaug = jnp.where((lane <= 16) & (lane != group[FRONT:, None]), AWAY, 0.0).astype(BF)
    half = HEAD_DIM // 2
    frequency = 10000.0 ** (-(lane % half).astype(F32) / half)
    phases = position[:, None].astype(F32) * frequency
    return kaug, qaug, jnp.where(lane % HEAD_DIM < half, jnp.cos(phases), jnp.sin(phases))


def vmem():
    return pl.BlockSpec(memory_space=pltpu.VMEM)


def params(**more):
    return pltpu.CompilerParams(vmem_limit_bytes=VMEM_LIMIT, **more)


def call_backward(tok, q, k, v, d_mixed, kaug, qaug, daug, table, gains, d_resid, wq, wk, wv, normed, grad_out, *factors):
    rows, width = tok.shape
    ff = factors[-1].shape[0] * SUB
    padded, ext = q.shape[0], k.shape[0]
    sds = jax.ShapeDtypeStruct
    anywhere = pl.BlockSpec(memory_space=pl.ANY)
    depths = (width // 8, width // 8, width // 8, ff // 8)
    grad_out = grad_out.reshape(2, 2, 2, width // 8, width)
    buffers = []
    for w, _, count in SCATTER_CHUNKS:
        buffers += scatter_buffers(depths[w], count)
    for _ in range(3):
        buffers += scatter_buffers(width // 8, width)
    part = 256
    return pl.pallas_call(
        bwd_scatter_kernel,
        out_shape=[sds((rows, width), BF)] + [sds((width // 32, width), F32)] * 4
        + [sds((width // 32, ff), F32)] * 2 + [sds((ff // 32, width), F32)],
        in_specs=[anywhere] * 4 + [vmem()] * 6 + [anywhere] * 11,
        out_specs=[anywhere] + [vmem()] * 7,
        scratch_shapes=[
            pltpu.VMEM((padded, width), BF), pltpu.VMEM((ext, width), BF), pltpu.VMEM((ext, width), BF),
            pltpu.VMEM((padded, width), BF),
            pltpu.VMEM((WIN // QB, QB, width), F32), pltpu.VMEM((WIN // QB, QB, width), F32),
            pltpu.VMEM((2, max(FRONT, width), width), BF), pltpu.VMEM((2, max(HALO, width), width), BF),
            pltpu.VMEM((2, part, width), F32), pltpu.VMEM((2, part, width), BF),
            pltpu.VMEM((SUB_SLOTS, padded, SUB), BF),
            pltpu.VMEM((3, 2, 2, 2, width // 8, 1024), BF), pltpu.VMEM((width // TALL, 2, 2, 2, ff // 8, TALL), BF),
        ] + buffers + [
            pltpu.SemaphoreType.DMA((2, (len(SCATTER_CHUNKS) + 3) * SCATTER_COPIES)),
            pltpu.SemaphoreType.DMA((19,)),
            pltpu.SemaphoreType.DMA((3 * ff // SUB,)),
            pltpu.SemaphoreType.DMA((2, 1)),
            pltpu.SemaphoreType.DMA((2, -(-rows // part))),
        ],
        compiler_params=params(collective_id=1, has_side_effects=True),
        name="attend_back",
    )(q, k, v, d_mixed, kaug, qaug, daug, table, tok, gains, d_resid, wq, wk, wv, normed, grad_out, *factors)


def per_device(tokens, item_lengths, attn_gain, w_query, w_key, w_value, w_out, mlp_gain, w_gate, w_up, w_down, cotangent):
    rows, width = tokens.shape[1:]
    ff = w_gate.shape[1]
    padded = -(-rows // ROW_STEP) * ROW_STEP
    ext = FRONT + padded
    axes = ("seq", "span")
    seqs, spans = (lax.axis_size(a) for a in axes)
    direct = (seqs, spans) == (8, 4)
    sds = jax.ShapeDtypeStruct
    anywhere = pl.BlockSpec(memory_space=pl.ANY)
    tok, cot = tokens[0], cotangent[0]

    kaug, qaug, table = side_arrays(item_lengths, rows, padded)
    fwd_shapes = [
        sds((padded, width), BF), sds((ext, width), BF), sds((ext, width), BF),
        sds((padded, width), BF), sds((padded, LANES), BF), sds((rows, width), BF),
    ]
    if direct:
        shards = [
            jnp.concatenate([w_query] + [jnp.broadcast_to(v[:, None], (v.shape[0], LANES)) for v in (attn_gain, mlp_gain)], axis=1),
            w_key, w_value, w_out, w_gate, w_up, w_down,
        ]
        whole = [(2, 2, 2, 4 * w.shape[0], w.shape[1]) for w in shards]
        near = []
        for w, _, count in GATHER_CHUNKS:
            depth = shards[w].shape[0]
            near.append((4, 2 * depth, count // 2) if depth % 16 else (4, depth, count))
        results = pl.pallas_call(
            fwd_gather_kernel,
            out_shape=fwd_shapes + [sds((8, width), F32)] + [sds(w, BF) for w in whole],
            in_specs=[vmem()] * 11,
            out_specs=[vmem()] * 7 + [anywhere] * 7,
            scratch_shapes=[pltpu.VMEM((HALO, width), BF)]
            + [pltpu.VMEM(n, BF) for n in near]
            + [pltpu.VMEM(w, BF) for w in whole]
            + [
                pltpu.SemaphoreType.DMA((2, len(GATHER_CHUNKS) * GATHER_COPIES)),
                pltpu.SemaphoreType.DMA((2, 1)),
                pltpu.SemaphoreType.DMA((7,)),
            ],
            compiler_params=params(collective_id=0, has_side_effects=True),
            name="attend",
        )(tok, *shards, kaug, qaug, table)
        q, k, v, mixed, qaug, normed, gains = results[:7]
        wq, wk, wv, wo, wg, wu, down = (w.reshape(-1, w.shape[-1]) for w in results[7:])
    else:
        packed = lax.all_gather(jnp.concatenate([w_query, w_key, w_value, w_out, w_gate, w_up], axis=1), axes, axis=0, tiled=True)
        down = lax.all_gather(w_down, axes, axis=0, tiled=True)
        gains = lax.all_gather(jnp.stack([attn_gain, mlp_gain], axis=1), axes, axis=0, tiled=True).astype(F32)
        gains = jnp.concatenate([jnp.transpose(gains), jnp.zeros((6, width), F32)], axis=0)
        wq, wk, wv, wo = (packed[:, i * width : (i + 1) * width] for i in range(4))
        wg, wu = packed[:, 4 * width : 4 * width + ff], packed[:, 4 * width + ff :]
        halo = lax.ppermute(tok[rows - HALO :], "span", [(i, i + 1) for i in range(spans - 1)])
        q, k, v, mixed, qaug, normed = pl.pallas_call(
            fwd_kernel,
            out_shape=fwd_shapes,
            in_specs=[vmem()] * 9,
            out_specs=[vmem()] * 6,
            compiler_params=params(),
            name="attend",
        )(tok, halo, wq, wk, wv, gains, kaug, qaug, table)

    tile = lambda n: pl.BlockSpec((ROW_STEP, n), lambda i: (i, 0))
    whole = lambda a: pl.BlockSpec(a.shape, lambda i: (0, 0), pipeline_mode=pl.Buffered(1))
    weights = (wo, wg, wu, down)
    output, d_resid, d_mixed, daug, g_o, n2, hid, dg, du = pl.pallas_call(
        functools.partial(mlp_kernel, rows),
        grid=(padded // ROW_STEP,),
        out_shape=[
            sds((rows, width), BF), sds((rows, width), F32), sds((padded, width), BF), sds((padded, LANES), BF),
            sds((width, width), BF), sds((padded, width), BF),
        ] + [sds((ff // SUB, padded, SUB), BF)] * 3,
        in_specs=[tile(width)] * 3 + [whole(a) for a in weights + (gains,)],
        out_specs=[tile(width)] * 3 + [tile(LANES), whole(wo), tile(width)]
        + [pl.BlockSpec((ff // SUB, ROW_STEP, SUB), lambda i: (0, i, 0))] * 3,
        scratch_shapes=[pltpu.VMEM((width, width), F32)],
        compiler_params=params(),
        name="mlp",
    )(tok, mixed, cot, *weights, gains)

    if direct:
        results = call_backward(
            tok, q, k, v, d_mixed, kaug, qaug, daug, table, gains, d_resid, wq, wk, wv, normed, g_o, n2, cot, hid, dg, du
        )
        input_grad, g_q, g_k, g_v, g_o, g_g, g_u, g_d = results
    else:
        dq, dk, dv = pl.pallas_call(
            bwd_kernel,
            out_shape=[sds((padded, width), BF), sds((ext, width), F32), sds((ext, width), F32)],
            in_specs=[vmem()] * 8,
            out_specs=[vmem()] * 3,
            compiler_params=params(),
            name="attend_back",
        )(q, k, v, d_mixed, kaug, qaug, daug, table)
        dq = dq[:rows]
        back = jnp.concatenate([dk[FRONT - HALO : FRONT], dv[FRONT - HALO : FRONT]], axis=1).astype(BF)
        back = lax.ppermute(back, "span", [(i + 1, i) for i in range(spans - 1)]).astype(F32)
        dk, dv = dk[FRONT : FRONT + rows], dv[FRONT : FRONT + rows]
        dk = jnp.concatenate([dk[: rows - HALO], dk[rows - HALO :] + back[:, :width]])
        dv = jnp.concatenate([dv[: rows - HALO], dv[rows - HALO :] + back[:, width:]]).astype(BF)
        half = HEAD_DIM // 2
        c, s = (table[FRONT : FRONT + rows, None, i * half : (i + 1) * half] for i in range(2))
        dk3 = dk.reshape(rows, width // HEAD_DIM, HEAD_DIM)
        a, b = dk3[..., :half], dk3[..., half:]
        dk = jnp.concatenate([a * c + b * s, b * c - a * s], axis=-1).reshape(rows, width).astype(BF)
        x = tok.astype(F32)
        inv = norm_rows(x)
        hat = x * inv
        gain_one = gains[:1]
        flat = lambda a: jnp.transpose(a, (1, 0, 2)).reshape(padded, ff)
        dn = sum(dot_nt(d, w) for d, w in ((dq, wq), (dk, wk), (dv, wv)))
        e = dn * gain_one
        input_grad = (d_resid + inv * (e - hat * jnp.mean(e * hat, axis=-1, keepdims=True))).astype(BF)
        sums = jnp.concatenate([dot_tn(normed, d) for d in (dq, dk, dv)] + [g_o.astype(F32), dot_tn(n2, flat(dg)), dot_tn(n2, flat(du))], axis=1)
        scatter = lambda g: lax.psum_scatter(g, axes, scatter_dimension=0, tiled=True)
        sums, g_d = scatter(sums), scatter(dot_tn(flat(hid)[:rows], cot))
        g_q, g_k, g_v, g_o = (sums[:, i * width : (i + 1) * width] for i in range(4))
        g_g, g_u = sums[:, 4 * width : 4 * width + ff], sums[:, 4 * width + ff :]

    def gain_grad(gain, *pairs):
        return sum(jnp.sum(g * w.astype(F32), axis=1) for g, w in pairs) / gain.astype(F32)

    gain_one_grad = gain_grad(attn_gain, (g_q, w_query), (g_k, w_key), (g_v, w_value))
    gain_two_grad = gain_grad(mlp_gain, (g_g, w_gate), (g_u, w_up))
    return output[None], input_grad[None], gain_one_grad, g_q, g_k, g_v, g_o, gain_two_grad, g_g, g_u, g_d


def solution(mesh):
    rows_placed, vector, matrix = P("seq", "span", None), P(("seq", "span")), P(("seq", "span"), None)
    return jax.shard_map(
        per_device,
        mesh=mesh,
        in_specs=(rows_placed, P("seq", None), vector, matrix, matrix, matrix, matrix, vector, matrix, matrix, matrix, rows_placed),
        out_specs=(rows_placed, rows_placed, vector, matrix, matrix, matrix, matrix, vector, matrix, matrix, matrix),
        check_vma=False,
    )
```

```python
import functools
import math

import jax
import jax.numpy as jnp
from jax import lax
from jax.experimental import pallas as pl
from jax.experimental.pallas import tpu as pltpu
from jax.sharding import PartitionSpec as P

HEAD_DIM = 64
HALO = 576
FRONT = 640
QB = 128
WIN = FRONT + QB
LANES = 128
EPS = 1e-5
SCALE = 0.125
AWAY = -1e30
BF = jnp.bfloat16
F32 = jnp.float32
VMEM_LIMIT = 63 * 1024 * 1024


def dot(a, b):
    return lax.dot_general(a, b, (((1,), (0,)), ((), ())), preferred_element_type=F32)


def dot_nt(a, b):
    return lax.dot_general(a, b, (((1,), (1,)), ((), ())), preferred_element_type=F32)


def dot_tn(a, b):
    return lax.dot_general(a, b, (((0,), (0,)), ((), ())), preferred_element_type=F32)


def rotated(v, cos, sin):
    lane = lax.broadcasted_iota(jnp.int32, v.shape, 1)
    swapped = jnp.where(lane % 64 < 32, pltpu.roll(v, 96, 1), pltpu.roll(v, 32, 1))
    return v * cos + swapped * sin


def turns(table):
    first = lax.broadcasted_iota(jnp.int32, table.shape, 1) % 64 < 32
    cos = jnp.where(first, table, pltpu.roll(table, 32, 1))
    sin = jnp.where(first, -pltpu.roll(table, 96, 1), table)
    return cos, sin


def both_heads(v):
    lane = lax.broadcasted_iota(jnp.int32, v.shape, 1)
    zero = jnp.zeros_like(v)
    return jnp.concatenate([jnp.where(lane < 64, v, zero), jnp.where(lane < 64, zero, v)], axis=0)


def one_of_both(v):
    rows = v.shape[0] // 2
    lane = lax.broadcasted_iota(jnp.int32, (rows, v.shape[1]), 1)
    return jnp.where(lane < 64, v[:rows], v[rows:])


def norm_rows(x):
    return lax.rsqrt(jnp.mean(x * x, axis=-1, keepdims=True) + EPS)


def in_thirds(v, lane):
    high = v.astype(BF)
    rest = v - high.astype(F32)
    middle = rest.astype(BF)
    last = (rest - middle.astype(F32)).astype(BF)
    return jnp.where(lane < 48, high, jnp.where(lane < 64, middle, last))


def coordinates():
    seq, span = lax.axis_index("seq"), lax.axis_index("span")
    return seq // 4, seq // 2 % 2, seq % 2, span


def device(y, x, core, span):
    return (y * 4 + x * 2 + core, span)


def greet():
    y, x, core, span = coordinates()
    barrier = pltpu.get_barrier_semaphore()
    peers = [device(y, x, core, (span + d) % 4) for d in (1, 2, 3)]
    peers += [device(1 - y, x, core, span), device(y, 1 - x, core, span), device(y, x, 1 - core, span)]
    for peer in peers:
        pl.semaphore_signal(barrier, inc=1, device_id=peer, device_id_type=pl.DeviceIdType.MESH)
    pl.semaphore_wait(barrier, len(peers))


def remote(src, dst, sems, at, to):
    return pltpu.make_async_remote_copy(
        src_ref=src, dst_ref=dst, send_sem=sems.at[0, at], recv_sem=sems.at[1, at], device_id=to,
        device_id_type=pl.DeviceIdType.MESH,
    )


GATHER_COPIES = 8


class Gathered:
    def __init__(self, shard, near, whole, at, count, sems, number):
        self.shard, self.near, self.whole, self.sems = shard, near, whole, sems
        self.first = number * GATHER_COPIES
        self.split = shard.shape[0] % 16 != 0
        self.columns = pl.ds(at, count)
        y, x, core, span = coordinates()
        half = count // 2
        left, right = pl.ds(at, half), pl.ds(at + half, half)
        over_y, over_x = device(1 - y, x, core, span), device(y, 1 - x, core, span)
        own = whole.at[y, x, core]
        rows = pl.ds(0, own.shape[0])
        refs = [(near.at[0], near.at[d], device(y, x, core, (span + d) % 4)) for d in (1, 2, 3)]
        refs += [(r, r, to) for r, to in (
            (whole.at[y, x, core, rows, left], over_y),
            (whole.at[y, x, core, rows, right], over_x),
            (whole.at[pl.ds(0, 2), x, core, rows, left], over_x),
            (whole.at[y, pl.ds(0, 2), core, rows, right], over_y),
            (whole.at[pl.ds(0, 2), pl.ds(0, 2), core, rows, self.columns], device(y, x, 1 - core, span)),
        )]
        self.copies = [remote(src, dst, sems, self.first + i, to) for i, (src, dst, to) in enumerate(refs)]

    def go(self, stage):
        if stage == 0:
            v = self.shard[:, self.columns]
            if self.split:
                half = v.shape[1] // 2
                v = v.astype(F32)
                v = jnp.concatenate([v[:, :half], v[:, half:]], axis=0).astype(BF)
            self.near[0] = v
            for i in (0, 1, 2):
                self.copies[i].start()
        if stage == 1:
            y, x, core, span = coordinates()
            for i in (0, 1, 2):
                self.copies[i].wait_recv()
            pieces = []
            for s in range(4):
                v = self.near[(span - s + 4) % 4]
                if self.split:
                    v = v.astype(F32)
                    half = v.shape[0] // 2
                    v = jnp.concatenate([v[:half], v[half:]], axis=1)
                pieces.append(v)
            self.whole[y, x, core, :, self.columns] = jnp.concatenate(pieces, axis=0).astype(BF)
            for i in (3, 4):
                self.copies[i].start()
        if stage == 2:
            for i in (3, 4):
                self.copies[i].wait_recv()
            for i in (5, 6):
                self.copies[i].start()
        if stage == 3:
            for i in (5, 6):
                self.copies[i].wait_recv()
            self.copies[7].start()
        if stage == 4:
            self.copies[7].wait_recv()

    def finish(self):
        for c in self.copies:
            c.wait_send()


def attention_forward(refs, q_out, k_out, v_out, mixed_out, qaug_out, normed_out, steps, tick):
    tok, halo, weights, gain, kaug, qaug, table = refs
    rows, width = tok.shape
    padded = q_out.shape[0]
    pairs = width // LANES

    def normal(x):
        x = x.astype(F32)
        return (x * norm_rows(x) * gain[0:1, :]).astype(BF)

    def project(which, normed, key_at, query_at):
        count = normed.shape[0]
        product = dot(normed, weights[which]())
        if which == 2:
            v_out[key_at : key_at + count, :] = product.astype(BF)
            return
        c, s = turns(table[key_at : key_at + count, :])
        for t in range(pairs):
            lanes = slice(t * LANES, (t + 1) * LANES)
            turned = rotated(product[:, lanes], c, s)
            if which == 0:
                q_out[query_at : query_at + count, lanes] = (turned * SCALE).astype(BF)
            else:
                k_out[key_at : key_at + count, lanes] = turned.astype(BF)

    lead = FRONT - HALO
    k_out[:lead, :] = jnp.zeros((lead, width), BF)
    v_out[:lead, :] = jnp.zeros((lead, width), BF)
    if padded > rows:
        blank = jnp.zeros((padded - rows, width), BF)
        q_out[rows:, :] = blank
        k_out[FRONT + rows :, :] = blank
        v_out[FRONT + rows :, :] = blank
    parts = [(at, min(480, rows - at)) for at in range(0, rows, 480)]
    for which in range(3):
        steps(which)
        for i, (at, count) in enumerate(parts):
            if which == 0:
                normed_out[at : at + count, :] = normal(tok[at : at + count, :])
            project(which, normed_out[at : at + count, :], FRONT + at, at)
            steps(which, i)

    lane = lax.broadcasted_iota(jnp.int32, (QB, LANES), 1)
    row = lax.broadcasted_iota(jnp.int32, (2 * QB, QB), 0)
    behind = lax.broadcasted_iota(jnp.int32, (2 * QB, QB), 1) <= row % QB

    blocks = padded // QB

    def block(i, carry):
        tick(i)

        @pl.when(i == blocks - FRONT // QB)
        def _():
            steps(3)
            normed = normal(halo[...])
            for which in (1, 2):
                project(which, normed, lead, None)

        start = pl.multiple_of((blocks - 1 - i) * QB, QB)
        k_a = kaug[pl.ds(start, WIN), :]
        q_a = qaug[pl.ds(start, QB), :]
        q_a2 = jnp.concatenate([q_a, q_a], axis=0)
        logs = jnp.zeros((QB, LANES), F32)
        for t in range(pairs):
            at = slice(t * LANES, (t + 1) * LANES)
            q2 = jnp.concatenate([both_heads(q_out[pl.ds(start, QB), at]), q_a2], axis=1)
            k2 = jnp.concatenate([k_out[pl.ds(start, WIN), at], k_a], axis=1)
            s = dot_nt(q2, k2)
            s = jnp.concatenate([s[:, :FRONT], jnp.where(behind, s[:, FRONT:], AWAY)], axis=1)
            top = jnp.max(s, axis=1, keepdims=True)
            p = jnp.exp(s - top).astype(BF)
            v = v_out[pl.ds(start, WIN), at]
            o = dot(p, jnp.concatenate([v, jnp.ones_like(v)], axis=1))
            total = o[:, LANES:]
            mixed_out[pl.ds(start, QB), at] = one_of_both(o[:, :LANES] / total).astype(BF)
            log = top + jnp.log(total)
            for e in range(2):
                h = 2 * t + e
                mine = (lane == 32 + h) | (lane == 48 + h) | (lane == 64 + h)
                logs = jnp.where(mine, log[e * QB : (e + 1) * QB], logs)
        qaug_out[pl.ds(start, QB), :] = jnp.where(lane < 32, q_a, in_thirds(-logs, lane))
        return carry

    lax.fori_loop(0, blocks, block, 0)


def fwd_kernel(tok, halo, wq, wk, wv, gain, kaug, qaug, table, q_out, k_out, v_out, mixed_out, qaug_out, normed_out):
    weights = [lambda w=w: w[...] for w in (wq, wk, wv)]
    refs = (tok, halo, weights, gain, kaug, qaug, table)
    attention_forward(refs, q_out, k_out, v_out, mixed_out, qaug_out, normed_out, lambda *_: None, lambda *_: None)


GATHER_CHUNKS = (
    (0, 0, 1024), (1, 0, 768), (2, 0, 768), (3, 0, 768), (4, 0, 1024), (4, 1024, 1024), (5, 0, 1024), (5, 1024, 1024),
    (6, 0, 256), (6, 256, 256), (6, 512, 256),
)
HALO_AFTER = (10, 1)
HALO_CHUNK = 11
GATHER_BEFORE = (
    ((0, 0), (1, 0), (2, 0), (3, 0), (0, 1), (4, 0), (1, 1), (0, 2), (2, 1), (5, 0), (1, 2), (3, 1), (6, 0), (0, 3), (4, 1), (2, 2), (7, 0), (0, 4)),
    ((8, 0), (4, 2), (1, 4)),
    ((10, 0), (5, 2), (7, 1), (2, 4)),
)
GATHER_PARTS = (
    (((1, 3),), ((5, 1),), ((3, 2),), ()),
    ((), ((6, 1), (9, 0)), (), ((2, 3),)),
    ((), ((3, 3), (8, 1)), ((11, 0),), ()),
)
GATHER_BLOCKS = (
    (1, ((9, 1),)),
    (2, ((4, 3),)),
    (3, ((10, 1), (6, 2))),
    (5, ((5, 3),)),
    (6, ((7, 2),)),
    (7, ((8, 2),)),
    (8, ((9, 2), (10, 2))),
    (10, ((6, 3), (7, 3))),
    (12, ((8, 3),)),
    (13, ((9, 3),)),
)
GATHER_END = ((10, 3), (3, 4), (4, 4), (5, 4), (6, 4), (7, 4), (8, 4), (9, 4), (10, 4))


def fwd_gather_kernel(tok, *refs):
    shards, refs = refs[:7], refs[7:]
    own_gains, kaug, qaug, table = refs[:4]
    outs, refs = refs[4:10], refs[10:]
    gains, refs = refs[0], refs[1:]
    whole_outs, refs = refs[:7], refs[7:]
    n = len(GATHER_CHUNKS)
    halo, nears, wholes = refs[0], refs[1 : n + 1], refs[n + 1 : n + 8]
    first_shard, *kept, sems, halo_sems, out_sems = refs[n + 8 :]
    q_out, k_out, v_out, mixed_out, qaug_out, normed_out = outs
    blocks = mixed_out.shape[0] // QB
    early_outs = [
        pltpu.make_async_copy(held, out, out_sems.at[7 + i])
        for i, (held, out) in enumerate(zip(kept, (q_out, normed_out, k_out, v_out)))
    ]
    rows, width = tok.shape
    y, x, core, span = coordinates()
    own_gains = own_gains[...].astype(F32)
    first_shard[:, :width] = shards[0][...]
    for i in range(2):
        first_shard[:, width + i * LANES : width + (i + 1) * LANES] = jnp.broadcast_to(
            own_gains[:, i : i + 1], (own_gains.shape[0], LANES)
        ).astype(BF)
    shards = (first_shard,) + tuple(shards[1:])
    greet()
    to_next = remote(tok.at[pl.ds(rows - HALO, HALO)], halo, halo_sems, 0, device(y, x, core, (span + 1) % 4))

    chunks = [
        Gathered(shards[w], nears[i], wholes[w], at, count, sems, i) for i, (w, at, count) in enumerate(GATHER_CHUNKS)
    ]
    out_copies = [pltpu.make_async_copy(w, o, out_sems.at[i]) for i, (w, o) in enumerate(zip(wholes, whole_outs))]

    def go(events):
        for chunk, stage in events:
            if chunk == HALO_CHUNK:
                to_next.start()
                continue
            chunks[chunk].go(stage)
            w, at, count = GATHER_CHUNKS[chunk]
            if stage == 4 and (chunk + 1 == len(GATHER_CHUNKS) or GATHER_CHUNKS[chunk + 1][0] != w):
                out_copies[w].start()

    def steps(which, part=None):
        if which == 3:
            to_next.wait_recv()
            return
        if part is not None:
            go(GATHER_PARTS[which][part])
            if (which, part) == (2, 3):
                for c in early_outs[:2]:
                    c.start()
            return
        go(GATHER_BEFORE[which])
        if which == 0:
            both = wholes[0][...].reshape(width, -1)[:, width:].astype(F32)
            both = [jnp.transpose(both[:, i * LANES : (i + 1) * LANES])[:1] for i in range(2)]
            gains[...] = jnp.concatenate(both + [jnp.zeros((6, width), F32)], axis=0)

    def tick(i):
        for at, events in GATHER_BLOCKS:
            @pl.when(i == at)
            def _():
                go(events)

        @pl.when(i == blocks - 1)
        def _():
            for c in early_outs[2:]:
                c.start()

    weights = [lambda w=w: w[...].reshape(width, w.shape[-1])[:, :width] for w in wholes[:3]]
    q, normed, k, v = kept
    attention_forward((tok, halo, weights, gains, kaug, qaug, table), q, k, v, mixed_out, qaug_out, normed, steps, tick)
    go(GATHER_END)
    to_next.wait_send()
    for c in chunks:
        c.finish()
    for c in out_copies + early_outs:
        c.wait()


def attention_backward(b, refs, dq_out, add):
    q, k, v, dmixed, kaug, qaug, daug, table = refs
    width = q.shape[1]
    lead = FRONT - HALO
    lane = lax.broadcasted_iota(jnp.int32, (QB, LANES), 1)
    key_row = lax.broadcasted_iota(jnp.int32, (QB, 2 * QB), 0)
    behind = key_row <= lax.broadcasted_iota(jnp.int32, (QB, 2 * QB), 1) % QB
    start = pl.multiple_of(b * QB, QB)
    keys = pl.ds(pl.multiple_of(start + lead, lead), WIN - lead)
    k_a = kaug[keys, :]
    q_a = qaug[pl.ds(start, QB), :]
    d_a = daug[pl.ds(start, QB), :]
    c, s_ = turns(table[pl.ds(start + FRONT, QB), :])
    zero = jnp.zeros_like(q_a)
    for t in range(width // LANES):
        at = slice(t * LANES, (t + 1) * LANES)
        mine = [(lane >= 32) & (lane % 16 == 2 * t + e) for e in range(2)]
        q_2 = both_heads(q[pl.ds(start, QB), at])
        q_aug = jnp.concatenate([jnp.where((lane < 32) | mine[e], q_a, zero) for e in range(2)], axis=0)
        d_2 = both_heads(dmixed[pl.ds(start, QB), at])
        d_aug = jnp.concatenate([jnp.where(mine[e], d_a, zero) for e in range(2)], axis=0)
        k_p = k[keys, at]
        st = dot_nt(jnp.concatenate([k_p, k_a], axis=1), jnp.concatenate([q_2, q_aug], axis=1))
        st = jnp.concatenate([st[:HALO], jnp.where(behind, st[HALO:], AWAY)], axis=0)
        pt = jnp.exp(st)
        dpt = dot_nt(jnp.concatenate([v[keys, at], k_a], axis=1), jnp.concatenate([d_2, d_aug], axis=1))
        dst = (pt * dpt).astype(BF)
        add(t, dot(dst, q_2), dot(pt.astype(BF), d_2))
        dq = one_of_both(dot_tn(dst, k_p)) * SCALE
        dq_out[pl.ds(start, QB), at] = rotated(dq, c, -s_).astype(BF)


def bwd_kernel(*refs):
    dq_out, dk_out, dv_out = refs[8:]
    padded = dq_out.shape[0]
    dk_out[...] = jnp.zeros_like(dk_out)
    dv_out[...] = jnp.zeros_like(dv_out)
    lead = FRONT - HALO

    def block(b, carry):
        keys = pl.ds(pl.multiple_of(b * QB + lead, lead), WIN - lead)

        def add(t, dk, dv):
            at = slice(t * LANES, (t + 1) * LANES)
            dk_out[keys, at] += dk
            dv_out[keys, at] += dv

        attention_backward(b, refs[:8], dq_out, add)
        return carry

    lax.fori_loop(0, padded // QB, block, 0)


SCATTER_COPIES = 8
SCATTER_CHUNKS = (
    (0, 0, 768), (1, 0, 1024), (1, 1024, 1024), (2, 0, 1024), (2, 1024, 1024), (3, 0, 256), (3, 256, 256), (3, 512, 256),
)
SUB = 512
SUB_SLOTS = 2
TALL = 256


class Scattered:
    def __init__(self, whole, at, count, out, bufs, sems, number):
        self.whole, self.out = whole, out
        self.got, self.left, self.right, self.left_2, self.right_2, self.near, self.far = bufs
        self.at, self.count = at, count
        self.columns = pl.ds(0, count)
        self.half = half = count // 2
        self.left_whole = False
        y, x, core, span = coordinates()
        rows = pl.ds(0, whole.shape[3])
        two = pl.ds(0, 2)
        lo, hi = pl.ds(0, half), pl.ds(half, half)
        over_y, over_x = device(1 - y, x, core, span), device(y, 1 - x, core, span)
        got = self.got
        refs = [
            (whole.at[two, two, 1 - core, rows, self.columns], got, device(y, x, 1 - core, span)),
            (got.at[two, 1 - x, rows, lo], self.left, over_x),
            (got.at[1 - y, two, rows, hi], self.right, over_y),
            (got.at[1 - y, x, rows, lo], self.left_2, over_y),
            (got.at[y, 1 - x, rows, hi], self.right_2, over_x),
        ]
        refs += [(self.near.at[(span + d) % 4], self.far.at[d - 1], device(y, x, core, (span + d) % 4)) for d in (1, 2, 3)]
        first = number * SCATTER_COPIES
        self.copies = [remote(src, dst, sems, first + i, to) for i, (src, dst, to) in enumerate(refs)]
    def go(self, stage):
        y, x, core, span = coordinates()
        got, half = self.got, self.half
        lo, hi = pl.ds(0, half), pl.ds(half, half)
        if stage == 0:
            self.copies[0].start()
        if stage == 1:
            self.copies[0].wait_recv()
            for i in range(2):
                for j in range(2):
                    got[i, j] = got[i, j] + self.whole[i, j, core, :, self.columns]
            for i in (1, 2):
                self.copies[i].start()
        if stage == 2:
            for i in (1, 2):
                self.copies[i].wait_recv()
            for i in range(2):
                got[i, x, :, lo] = got[i, x, :, lo] + self.left[i]
                got[y, i, :, hi] = got[y, i, :, hi] + self.right[i]
            for i in (3, 4):
                self.copies[i].start()
        if stage == 3:
            for i in (3, 4):
                self.copies[i].wait_recv()
            total = jnp.concatenate(
                [got[y, x, :, r].astype(F32) + other[...].astype(F32) for r, other in ((lo, self.left_2), (hi, self.right_2))],
                axis=1,
            )
            depth = total.shape[0] // 4
            for s in range(4):
                v = total[s * depth : (s + 1) * depth]
                if depth % 16:
                    v = jnp.concatenate([v[:, :half], v[:, half:]], axis=0)
                self.near[s] = v.astype(BF)
            for i in (5, 6, 7):
                self.copies[i].start()
        if stage == 4:
            for i in (5, 6, 7):
                self.copies[i].wait_recv()
            v = self.near[span].astype(F32)
            for d in range(3):
                v = v + self.far[d].astype(F32)
            depth = self.out.shape[0]
            if depth % 16:
                v = jnp.concatenate([v[:depth], v[depth:]], axis=1)
            self.out[:, self.at : self.at + self.count] = v

    def leave_whole(self):
        if not self.left_whole:
            self.copies[0].wait_send()
        self.left_whole = True

    def finish(self):
        self.leave_whole()
        for c in self.copies[1:]:
            c.wait_send()


def scatter_buffers(rows, count):
    depth = rows // 4
    piece = (2 * depth, count // 2) if depth % 16 else (depth, count)
    shapes = [
        (2, 2, rows, count), (2, rows, count // 2), (2, rows, count // 2), (rows, count // 2), (rows, count // 2),
        (4,) + piece, (3,) + piece,
    ]
    return [pltpu.VMEM(shape, BF) for shape in shapes]


HALO_BLOCKS = FRONT // QB
SCATTER_AT = (
    (0, 1, 3, 4, 8), (5, 6, 8, 9, 12), (6, 7, 9, 13, 16), (7, 8, 9, 13, 16), (8, 9, 13, 17, 19),
    (9, 11, 17, 20, 22), (9, 11, 17, 20, 22), (9, 11, 17, 20, 22),
)


def scatter_plan(blocks):
    ticks, after = [[] for _ in range(blocks + 5)], []
    events = sorted((t, j, stage) for j, when in enumerate(SCATTER_AT) for stage, t in enumerate(when))
    for t, j, stage in events:
        (ticks[t] if t < len(ticks) else after).append((j, stage))
    return ticks, after


def bwd_scatter_kernel(
    q_in, k_in, v_in, dmixed_in, kaug, qaug, daug, table, tok, gains, d_resid, wq_in, wk_in, wv_in,
    normed_in, g_out, n2_in, cot_in, hid_in, dg_in, du_in,
    input_grad, s_query, s_key, s_value, s_out, s_gate, s_up, s_down,
    q, k, v, dmixed, dk_win, dv_win, halo_out, halo_in, resid_block, out_block, subs, wide, tall, *refs,
):
    rows, width = tok.shape
    padded = q.shape[0]
    blocks = padded // QB
    pairs = width // LANES
    lead = FRONT - HALO
    slots = WIN // QB
    n = len(SCATTER_CHUNKS)
    chunk_bufs = [refs[7 * i : 7 * i + 7] for i in range(n + 3)]
    refs = refs[7 * (n + 3) :]
    sems, in_sems, sub_sems, halo_sems, block_sems = refs
    y, x, core, span = coordinates()

    near_q, near_k = HALO_BLOCKS * QB, 2 * FRONT
    far_q = pl.ds(near_q, padded - near_q)
    lower, upper = pl.ds(0, padded - near_q), pl.ds(padded - near_q, near_q)
    upper_c = pl.ds(padded - near_q, rows - padded + near_q)
    far_k = pl.ds(near_k, near_q)
    rest = pl.ds(near_k + near_q, k.shape[0] - near_k - near_q)
    one, two = pl.ds(0, near_q), pl.ds(0, near_k)
    weights = [halo_out.at[0], halo_out.at[1], halo_in.at[0]]
    by_name = dict(
        q=(q_in.at[one], q.at[one]), k=(k_in.at[two], k.at[two]), v=(v_in.at[two], v.at[two]),
        d=(dmixed_in.at[one], dmixed.at[one]),
        o=(g_out, wide.at[0, pl.ds(0, 2), pl.ds(0, 2), pl.ds(0, 2), pl.ds(0, width // 8), pl.ds(0, width)]),
        n_low=(n2_in.at[lower], q.at[far_q]), n_high=(n2_in.at[upper], k.at[far_k]),
        c_low=(cot_in.at[lower], dmixed.at[far_q]),
        c_high=(cot_in.at[upper_c], v.at[pl.ds(near_k, rows - padded + near_q)]),
        k_rest=(k_in.at[rest], k.at[rest]), v_rest=(v_in.at[rest], v.at[rest]),
        q_far=(q_in.at[far_q], q.at[far_q]), k_far=(k_in.at[far_k], k.at[far_k]),
        d_far=(dmixed_in.at[far_q], dmixed.at[far_q]), v_far=(v_in.at[far_k], v.at[far_k]),
        w_q=(wq_in.at[pl.ds(0, width), pl.ds(0, width)], weights[0]),
        w_k=(wk_in, weights[1]), w_v=(wv_in, weights[2]),
        normed=(normed_in, dmixed.at[pl.ds(0, rows)]),
    )
    arrivals = {
        name: pltpu.make_async_copy(src, dst, in_sems.at[i]) for i, (name, (src, dst)) in enumerate(by_name.items())
    }
    brought = [(src, f) for src in (dg_in, du_in, hid_in) for f in range(src.shape[0])]
    sub_copies = [
        pltpu.make_async_copy(src.at[f], subs.at[i % SUB_SLOTS], sub_sems.at[i])
        for i, (src, f) in enumerate(brought)
    ]

    def bring(*names):
        for name in names:
            arrivals[name].start()

    def await_all(*names):
        for name in names:
            arrivals[name].wait()

    bring("o", "q", "k", "v", "d", "n_low", "n_high", "c_low", "c_high", "k_rest", "v_rest")
    for c in sub_copies[:SUB_SLOTS]:
        c.start()
    greet()

    sums = (s_out, s_gate, s_up, s_down)
    chunks = []
    for i, (w, at, count) in enumerate(SCATTER_CHUNKS):
        whole = wide.at[i % 3] if w < 3 else tall.at[at // count]
        chunks.append(Scattered(whole, at, count, sums[w], chunk_bufs[i], sems, i))
    own = [wide.at[i] for i in (2, 0, 1)]
    chunks += [
        Scattered(own[i], 0, width, (s_query, s_key, s_value)[i], chunk_bufs[n + i], sems, n + i) for i in range(3)
    ]
    to_last = remote(
        halo_out.at[pl.ds(0, 2), pl.ds(0, HALO)], halo_in.at[pl.ds(0, 2), pl.ds(0, HALO)], halo_sems, 0, device(y, x, core, (span + 3) % 4))
    ticks, after = scatter_plan(blocks)
    dk_win[...] = jnp.zeros_like(dk_win)
    dv_win[...] = jnp.zeros_like(dv_win)
    await_all("o", "q", "k", "v", "d")

    def block_of(inside):
        return functools.partial(block, inside)

    def block(inside, b, carry):
        for i, todo in inside.items():
            if todo:
                @pl.when(b == i)
                def _():
                    for chunk, stage in todo:
                        chunks[chunk].go(stage)

        def add(t, dk, dv):
            at = slice(t * LANES, (t + 1) * LANES)
            for win, grad in ((dk_win, dk), (dv_win, dv)):
                for j in range(slots):
                    count = min(QB, WIN - lead - j * QB)
                    win[lax.rem(b + j, slots), :count, at] += grad[j * QB : j * QB + count]

        attention_backward(b, (q, k, v, dmixed, kaug, qaug, daug, table), q, add)

        slot = lax.rem(b, slots)
        at = pl.ds(pl.multiple_of(b * QB + lead, lead), QB)

        @pl.when(b < FRONT // QB)
        def _():
            to = pl.ds(pl.multiple_of(b * QB, QB), QB)
            halo_out[0, to, :] = dk_win[slot].astype(BF)
            halo_out[1, to, :] = dv_win[slot].astype(BF)

        @pl.when((b >= FRONT // QB - 1) & (b < blocks - 1))
        def _():
            c, s_ = turns(table[at, :])
            for t in range(pairs):
                lanes = slice(t * LANES, (t + 1) * LANES)
                k[at, lanes] = rotated(dk_win[slot, :, lanes], c, -s_).astype(BF)
            v[at, :] = dv_win[slot].astype(BF)

        @pl.when(b < blocks - 1)
        def _():
            dk_win[slot] = jnp.zeros((QB, width), F32)
            dv_win[slot] = jnp.zeros((QB, width), F32)

        return carry

    lax.fori_loop(0, HALO_BLOCKS, block_of({b: ticks[b] for b in range(HALO_BLOCKS)}), 0)
    to_last.start()

    sub = 0
    low, high, group = padded - near_q, padded, tall.shape[4]
    await_all("n_low", "n_high")
    for i, (w, at, count) in enumerate(SCATTER_CHUNKS):
        if w == 0 or (w == 3 and at > 0):
            continue
        if w < 3 and i >= 3:
            chunks[i - 3].leave_whole()
        if w == 3:
            bring("q_far", "k_far")
            await_all("c_low", "c_high")
            v[near_k + rows - low : near_k + near_q, :] = jnp.zeros((padded - rows, width), BF)
        for f in range(0, count if w < 3 else hid_in.shape[0] * SUB, SUB):
            sub_copies[sub].wait()
            here = subs.at[sub % SUB_SLOTS]
            if w < 3:
                total = dot_tn(q[near_q:, :], here[:low, :]) + dot_tn(k[near_k : near_k + near_q, :], here[low:, :])
                wide[i % 3, :, :, :, :, f : f + SUB] = total.reshape(2, 2, 2, width // 8, SUB).astype(BF)
            else:
                total = dot_tn(here[:low, :], dmixed[near_q:, :]) + dot_tn(here[low:, :], v[near_k : near_k + near_q, :])
                total = total.astype(BF)
                for r in range(0, SUB, group):
                    g = (f + r) // group
                    for j in range(width // TALL):
                        tall[j, g // 4, g // 2 % 2, g % 2] = total[r : r + group, j * TALL : (j + 1) * TALL]
            if sub + SUB_SLOTS < len(sub_copies):
                sub_copies[sub + SUB_SLOTS].start()
            sub += 1
        if w == 3:
            bring("d_far", "v_far")
        for chunk, stage in ticks[HALO_BLOCKS + min(i, 5) - 1]:
            chunks[chunk].go(stage)
    await_all("q_far", "k_far", "d_far", "v_far", "k_rest", "v_rest")
    lax.fori_loop(HALO_BLOCKS, blocks, block_of({b: ticks[b + 5] for b in range(HALO_BLOCKS, blocks)}), 0)
    bring("normed")
    to_last.wait_send()
    bring("w_q", "w_k")

    step = resid_block.shape[1]
    parts = [(at, min(step, rows - at)) for at in range(0, rows, step)]
    resid_in = [
        pltpu.make_async_copy(
            d_resid.at[pl.ds(at, count)], resid_block.at[i % 2, pl.ds(0, count)], block_sems.at[0, i]
        ) for i, (at, count) in enumerate(parts)
    ]
    grad_copies = [
        pltpu.make_async_copy(
            out_block.at[i % 2, pl.ds(0, count)], input_grad.at[pl.ds(at, count)], block_sems.at[1, i]
        ) for i, (at, count) in enumerate(parts)
    ]
    resid_in[0].start()
    resid_in[1].start()
    todo = list(after)

    def events(count):
        for chunk, stage in todo[:count]:
            chunks[chunk].go(stage)
        del todo[:count]

    g = gains[0:1, :]
    normed = dmixed
    await_all("normed")

    def weight_grad(i, grad):
        for j in range(2):
            half = width // 2
            total = dot_tn(normed[:rows, j * half : (j + 1) * half], grad)
            own[i][j, :, :, :, pl.ds(0, width)] = total.reshape(2, 2, half // 4, width).astype(BF)

    for i in (2, 3, 4):
        chunks[i].leave_whole()
    weight_grad(0, q[:rows, :])
    chunks[n].go(0)
    events(2)
    to_last.wait_recv()
    for j in range(slots):
        base = (blocks - 1) * QB + lead + j * QB
        slot = (blocks - 1 + j) % slots
        count = min(QB, FRONT + rows - base)
        first = max(base, FRONT + rows - HALO)
        for which, win, whole in ((0, dk_win, k), (1, dv_win, v)):
            grad = win[slot, :count, :]
            more = halo_in[which, first - (FRONT + rows - HALO) : base + count - (FRONT + rows - HALO), :].astype(F32)
            if first > base:
                more = jnp.concatenate([jnp.zeros((first - base, width), F32), more], axis=0)
            grad = grad + more
            if which:
                whole[base : base + count, :] = grad.astype(BF)
                continue
            c, s_ = turns(table[base : base + count, :])
            for t in range(pairs):
                lanes = slice(t * LANES, (t + 1) * LANES)
                whole[base : base + count, lanes] = rotated(grad[:, lanes], c, -s_).astype(BF)
    bring("w_v")
    weight_grad(1, k[FRONT : FRONT + rows, :])
    chunks[n].go(1)
    chunks[n + 1].go(0)
    events(2)
    weight_grad(2, v[FRONT : FRONT + rows, :])
    chunks[n].go(2)
    chunks[n + 1].go(1)
    chunks[n + 2].go(0)
    events(2)
    await_all("w_q", "w_k", "w_v")
    between = (((0, 3), (1, 2), (2, 1)), ((1, 3), (2, 2)), ((0, 4), (2, 3)), ((1, 4),), ((2, 4),))
    for i, (at, count) in enumerate(parts):
        grads = (q[at : at + count, :], k[FRONT + at : FRONT + at + count, :], v[FRONT + at : FRONT + at + count, :])
        dn = sum(dot_nt(d, weights[w][...]) for w, d in enumerate(grads))
        x = tok[at : at + count, :].astype(F32)
        inv = norm_rows(x)
        hat = x * inv
        e = dn * g
        resid_in[i].wait()
        total = resid_block[i % 2, :count] + inv * (e - hat * jnp.mean(e * hat, axis=-1, keepdims=True))
        if i >= 2:
            grad_copies[i - 2].wait()
        out_block[i % 2, :count] = total.astype(BF)
        grad_copies[i].start()
        if i + 2 < len(parts):
            resid_in[i + 2].start()
        events(1)
        for chunk, stage in between[i] if i < len(between) else ():
            chunks[n + chunk].go(stage)
    events(len(todo))
    for c in chunks:
        c.finish()
    for c in grad_copies[-2:]:
        c.wait()


def finish_kernel(input_in, *refs):
    grads, (wq, wk, wv, wg, wu, gains) = refs[:7], refs[7:13]
    input_out, gain_out, outs = refs[13], refs[14], refs[15:]
    input_out[...] = input_in[...]

    @pl.when(pl.program_id(0) == 0)
    def _():
        for grad, out in zip(grads, outs):
            out[...] = grad[...]
        sums = []
        for pairs in (((0, wq), (1, wk), (2, wv)), ((4, wg), (5, wu))):
            sums.append(sum(jnp.sum(grads[i][...] * w[...].astype(F32), axis=1, keepdims=True) for i, w in pairs))
        gain_out[...] = jnp.concatenate(sums, axis=1) / gains[...].astype(F32)


FF_STEP = 512
ROW_STEP = 480


def mlp_kernel(rows, x_ref, mixed, c_ref, wo, wg, wu, wd, gains,
               out, d_resid_out, d_mixed_out, daug_out, grad_out, n2_out, hid_out, dg_out, du_out, total):
    i = pl.program_id(0)
    count, width = x_ref.shape
    valid = lax.broadcasted_iota(jnp.int32, (count, width), 0) + i * count < rows
    c = jnp.where(valid, c_ref[...], jnp.zeros((count, width), BF))
    x = jnp.where(valid, x_ref[...].astype(F32), 0.0)
    mix = mixed[...]
    resid = x + dot(mix, wo[...])
    r = norm_rows(resid)
    g = gains[1:2, :]
    hat = resid * r
    n2 = (hat * g).astype(BF)
    n2_out[...] = n2
    acc = resid
    dn = jnp.zeros((count, width), F32)
    for f in range(0, wg.shape[1], FF_STEP):
        at = slice(f, f + FF_STEP)
        gate = dot(n2, wg[:, at])
        up = dot(n2, wu[:, at])
        sig = jax.nn.sigmoid(gate)
        silu = gate * sig
        hid = (silu * up).astype(BF)
        for j in range(0, FF_STEP, SUB):
            hid_out[(f + j) // SUB] = hid[:, j : j + SUB]
        acc = acc + dot(hid, wd[at, :])
        dh = dot_nt(c, wd[at, :])
        dg = (dh * up * sig * (1.0 + gate * (1.0 - sig))).astype(BF)
        du = (dh * silu).astype(BF)
        for j in range(0, FF_STEP, SUB):
            dg_out[(f + j) // SUB] = dg[:, j : j + SUB]
            du_out[(f + j) // SUB] = du[:, j : j + SUB]
        dn = dn + dot_nt(dg, wg[:, at]) + dot_nt(du, wu[:, at])
    out[...] = acc.astype(BF)
    e = dn * g
    d_resid = c.astype(F32) + r * (e - hat * jnp.mean(e * hat, axis=-1, keepdims=True))
    d_resid_out[...] = d_resid
    d_branch = d_resid.astype(BF)
    total[...] = jnp.where(i == 0, 0.0, total[...]) + dot_tn(mix, d_branch)

    @pl.when(i == pl.num_programs(0) - 1)
    def _():
        grad_out[...] = total[...].astype(BF)

    d_mixed = dot_nt(d_branch, wo[...]).astype(BF)
    d_mixed_out[...] = d_mixed

    e_row = lax.broadcasted_iota(jnp.int32, (width, LANES), 0) // HEAD_DIM
    e_lane = lax.broadcasted_iota(jnp.int32, (width, LANES), 1)
    picks = ((e_lane >= 32) & (e_lane < 80) & (e_lane % 16 == e_row)).astype(F32).astype(BF)
    prod = d_mixed.astype(F32) * mix.astype(F32)
    high = prod.astype(BF)
    low = (prod - high.astype(F32)).astype(BF)
    lane = lax.broadcasted_iota(jnp.int32, (count, LANES), 1)
    daug_out[...] = in_thirds(-(dot(high, picks) + dot(low, picks)), lane)


def slots_of(item_lengths, first, count):
    ends = jnp.cumsum(item_lengths[0])[None, :]
    slots = first + jnp.arange(count, dtype=jnp.int32)
    reached = (slots[:, None] >= ends) & (item_lengths[0] > 0)[None, :]
    segment = jnp.sum(reached.astype(jnp.int32), axis=1)
    begin = jnp.max(jnp.where(reached, ends, 0), axis=1)
    return slots, segment % 16, slots - begin


def side_arrays(item_lengths, local_rows, padded):
    offset = lax.axis_index("span") * local_rows
    count = FRONT + padded
    slots, group, position = slots_of(item_lengths, offset - FRONT, count)
    lane = jnp.arange(LANES, dtype=jnp.int32)[None, :]
    away = (slots < 0) | (jnp.arange(count) < FRONT - HALO)
    where_key = jnp.where(away, 16, group)[:, None]
    marks = (lane >= 32) & (lane < 80) & (lane % 16 < 12)
    kaug = ((lane == where_key) | marks).astype(BF)
    qaug = jnp.where((lane <= 16) & (lane != group[FRONT:, None]), AWAY, 0.0).astype(BF)
    half = HEAD_DIM // 2
    frequency = 10000.0 ** (-(lane % half).astype(F32) / half)
    quarter = jnp.where(lane % HEAD_DIM < half, 0.0, 0.5 * math.pi)
    return kaug, qaug, cosine(position[:, None].astype(F32) * frequency - quarter)


def cosine(v):
    number = jnp.floor(v * (0.5 / math.pi) + 0.5)
    rest = (v - number * 6.28125) - number * (2.0 * math.pi - 6.28125)
    square = rest * rest
    total = jnp.full_like(v, 1.0 / math.factorial(18))
    for k in range(8, -1, -1):
        total = 1.0 / math.factorial(2 * k) - total * square
    return total


def vmem():
    return pl.BlockSpec(memory_space=pltpu.VMEM)


def params(**more):
    return pltpu.CompilerParams(vmem_limit_bytes=VMEM_LIMIT, **more)


def call_backward(tok, q, k, v, d_mixed, kaug, qaug, daug, table, gains, d_resid, wq, wk, wv, normed, grad_out, *factors):
    rows, width = tok.shape
    ff = factors[-1].shape[0] * SUB
    padded, ext = q.shape[0], k.shape[0]
    sds = jax.ShapeDtypeStruct
    anywhere = pl.BlockSpec(memory_space=pl.ANY)
    depths = (width // 8, width // 8, width // 8, ff // 8)
    grad_out = grad_out.reshape(2, 2, 2, width // 8, width)
    buffers = []
    for w, _, count in SCATTER_CHUNKS:
        buffers += scatter_buffers(depths[w], count)
    for _ in range(3):
        buffers += scatter_buffers(width // 8, width)
    part = 256
    return pl.pallas_call(
        bwd_scatter_kernel,
        out_shape=[sds((rows, width), BF)] + [sds((width // 32, width), F32)] * 4
        + [sds((width // 32, ff), F32)] * 2 + [sds((ff // 32, width), F32)],
        in_specs=[anywhere] * 4 + [vmem()] * 6 + [anywhere] * 11,
        out_specs=[anywhere] + [vmem()] * 7,
        scratch_shapes=[
            pltpu.VMEM((padded, width), BF), pltpu.VMEM((ext, width), BF), pltpu.VMEM((ext, width), BF),
            pltpu.VMEM((padded, width), BF),
            pltpu.VMEM((WIN // QB, QB, width), F32), pltpu.VMEM((WIN // QB, QB, width), F32),
            pltpu.VMEM((2, max(FRONT, width), width), BF), pltpu.VMEM((2, max(HALO, width), width), BF),
            pltpu.VMEM((2, part, width), F32), pltpu.VMEM((2, part, width), BF),
            pltpu.VMEM((SUB_SLOTS, padded, SUB), BF),
            pltpu.VMEM((3, 2, 2, 2, width // 8, 1024), BF), pltpu.VMEM((width // TALL, 2, 2, 2, ff // 8, TALL), BF),
        ] + buffers + [
            pltpu.SemaphoreType.DMA((2, (len(SCATTER_CHUNKS) + 3) * SCATTER_COPIES)),
            pltpu.SemaphoreType.DMA((19,)),
            pltpu.SemaphoreType.DMA((3 * ff // SUB,)),
            pltpu.SemaphoreType.DMA((2, 1)),
            pltpu.SemaphoreType.DMA((2, -(-rows // part))),
        ],
        compiler_params=params(collective_id=1, has_side_effects=True),
        name="attend_back",
    )(q, k, v, d_mixed, kaug, qaug, daug, table, tok, gains, d_resid, wq, wk, wv, normed, grad_out, *factors)


def per_device(tokens, item_lengths, attn_gain, w_query, w_key, w_value, w_out, mlp_gain, w_gate, w_up, w_down, cotangent):
    rows, width = tokens.shape[1:]
    ff = w_gate.shape[1]
    padded = -(-rows // ROW_STEP) * ROW_STEP
    ext = FRONT + padded
    axes = ("seq", "span")
    seqs, spans = (lax.axis_size(a) for a in axes)
    direct = (seqs, spans) == (8, 4)
    sds = jax.ShapeDtypeStruct
    anywhere = pl.BlockSpec(memory_space=pl.ANY)
    tok, cot = tokens[0], cotangent[0]
    own_gains = jnp.stack([attn_gain, mlp_gain], axis=1)

    kaug, qaug, table = side_arrays(item_lengths, rows, padded)
    fwd_shapes = [
        sds((padded, width), BF), sds((ext, width), BF), sds((ext, width), BF),
        sds((padded, width), BF), sds((padded, LANES), BF), sds((rows, width), BF),
    ]
    if direct:
        shards = [w_query, w_key, w_value, w_out, w_gate, w_up, w_down]
        whole = [(2, 2, 2, 4 * w.shape[0], w.shape[1]) for w in shards]
        whole[0] = whole[0][:4] + (width + 2 * LANES,)
        near = []
        for w, _, count in GATHER_CHUNKS:
            depth = shards[w].shape[0]
            near.append((4, 2 * depth, count // 2) if depth % 16 else (4, depth, count))
        results = pl.pallas_call(
            fwd_gather_kernel,
            out_shape=fwd_shapes + [sds((8, width), F32)] + [sds(w, BF) for w in whole],
            in_specs=[vmem()] * 12,
            out_specs=[anywhere] * 3 + [vmem()] * 2 + [anywhere, vmem()] + [anywhere] * 7,
            scratch_shapes=[pltpu.VMEM((HALO, width), BF)]
            + [pltpu.VMEM(n, BF) for n in near]
            + [pltpu.VMEM(w, BF) for w in whole]
            + [
                pltpu.VMEM((w_query.shape[0], width + 2 * LANES), BF),
                pltpu.VMEM((padded, width), BF), pltpu.VMEM((rows, width), BF),
                pltpu.VMEM((ext, width), BF), pltpu.VMEM((ext, width), BF),
                pltpu.SemaphoreType.DMA((2, len(GATHER_CHUNKS) * GATHER_COPIES)),
                pltpu.SemaphoreType.DMA((2, 1)),
                pltpu.SemaphoreType.DMA((11,)),
            ],
            compiler_params=params(collective_id=0, has_side_effects=True),
            name="attend",
        )(tok, *shards, own_gains, kaug, qaug, table)
        q, k, v, mixed, qaug, normed, gains = results[:7]
        wq, wk, wv, wo, wg, wu, down = (w.reshape(-1, w.shape[-1]) for w in results[7:])
    else:
        packed = lax.all_gather(jnp.concatenate([w_query, w_key, w_value, w_out, w_gate, w_up], axis=1), axes, axis=0, tiled=True)
        down = lax.all_gather(w_down, axes, axis=0, tiled=True)
        gains = lax.all_gather(own_gains, axes, axis=0, tiled=True).astype(F32)
        gains = jnp.concatenate([jnp.transpose(gains), jnp.zeros((6, width), F32)], axis=0)
        wq, wk, wv, wo = (packed[:, i * width : (i + 1) * width] for i in range(4))
        wg, wu = packed[:, 4 * width : 4 * width + ff], packed[:, 4 * width + ff :]
        halo = lax.ppermute(tok[rows - HALO :], "span", [(i, i + 1) for i in range(spans - 1)])
        q, k, v, mixed, qaug, normed = pl.pallas_call(
            fwd_kernel,
            out_shape=fwd_shapes,
            in_specs=[vmem()] * 9,
            out_specs=[vmem()] * 6,
            compiler_params=params(),
            name="attend",
        )(tok, halo, wq, wk, wv, gains, kaug, qaug, table)

    tile = lambda n: pl.BlockSpec((ROW_STEP, n), lambda i: (i, 0))
    whole = lambda a: pl.BlockSpec(a.shape, lambda i: (0, 0), pipeline_mode=pl.Buffered(1))
    weights = (wo, wg, wu, down)
    output, d_resid, d_mixed, daug, g_o, n2, hid, dg, du = pl.pallas_call(
        functools.partial(mlp_kernel, rows),
        grid=(padded // ROW_STEP,),
        out_shape=[
            sds((rows, width), BF), sds((rows, width), F32), sds((padded, width), BF), sds((padded, LANES), BF),
            sds((width, width), BF), sds((padded, width), BF),
        ] + [sds((ff // SUB, padded, SUB), BF)] * 3,
        in_specs=[tile(width)] * 3 + [whole(a) for a in weights + (gains,)],
        out_specs=[tile(width)] * 3 + [tile(LANES), whole(wo), tile(width)]
        + [pl.BlockSpec((ff // SUB, ROW_STEP, SUB), lambda i: (0, i, 0))] * 3,
        scratch_shapes=[pltpu.VMEM((width, width), F32)],
        compiler_params=params(),
        name="mlp",
    )(tok, mixed, cot, *weights, gains)

    if direct:
        results = call_backward(
            tok, q, k, v, d_mixed, kaug, qaug, daug, table, gains, d_resid, wq, wk, wv, normed, g_o, n2, cot, hid, dg, du
        )
        input_grad, g_q, g_k, g_v, g_o, g_g, g_u, g_d = results
    else:
        dq, dk, dv = pl.pallas_call(
            bwd_kernel,
            out_shape=[sds((padded, width), BF), sds((ext, width), F32), sds((ext, width), F32)],
            in_specs=[vmem()] * 8,
            out_specs=[vmem()] * 3,
            compiler_params=params(),
            name="attend_back",
        )(q, k, v, d_mixed, kaug, qaug, daug, table)
        dq = dq[:rows]
        back = jnp.concatenate([dk[FRONT - HALO : FRONT], dv[FRONT - HALO : FRONT]], axis=1).astype(BF)
        back = lax.ppermute(back, "span", [(i + 1, i) for i in range(spans - 1)]).astype(F32)
        dk, dv = dk[FRONT : FRONT + rows], dv[FRONT : FRONT + rows]
        dk = jnp.concatenate([dk[: rows - HALO], dk[rows - HALO :] + back[:, :width]])
        dv = jnp.concatenate([dv[: rows - HALO], dv[rows - HALO :] + back[:, width:]]).astype(BF)
        half = HEAD_DIM // 2
        c, s = (table[FRONT : FRONT + rows, None, i * half : (i + 1) * half] for i in range(2))
        dk3 = dk.reshape(rows, width // HEAD_DIM, HEAD_DIM)
        a, b = dk3[..., :half], dk3[..., half:]
        dk = jnp.concatenate([a * c + b * s, b * c - a * s], axis=-1).reshape(rows, width).astype(BF)
        x = tok.astype(F32)
        inv = norm_rows(x)
        hat = x * inv
        gain_one = gains[:1]
        flat = lambda a: jnp.transpose(a, (1, 0, 2)).reshape(padded, ff)
        dn = sum(dot_nt(d, w) for d, w in ((dq, wq), (dk, wk), (dv, wv)))
        e = dn * gain_one
        input_grad = (d_resid + inv * (e - hat * jnp.mean(e * hat, axis=-1, keepdims=True))).astype(BF)
        sums = jnp.concatenate([dot_tn(normed, d) for d in (dq, dk, dv)] + [g_o.astype(F32), dot_tn(n2, flat(dg)), dot_tn(n2, flat(du))], axis=1)
        scatter = lambda g: lax.psum_scatter(g, axes, scatter_dimension=0, tiled=True)
        sums, g_d = scatter(sums), scatter(dot_tn(flat(hid)[:rows], cot))
        g_q, g_k, g_v, g_o = (sums[:, i * width : (i + 1) * width] for i in range(4))
        g_g, g_u = sums[:, 4 * width : 4 * width + ff], sums[:, 4 * width + ff :]

    grads = (g_q, g_k, g_v, g_o, g_g, g_u, g_d)
    owned = (w_query, w_key, w_value, w_gate, w_up, own_gains)
    shapes = [sds((w_query.shape[0], 2), F32)] + [sds(g.shape, F32) for g in grads]
    input_grad, gain_grads, *grads = pl.pallas_call(
        finish_kernel,
        grid=(padded // ROW_STEP,),
        out_shape=[sds((rows, width), BF)] + shapes,
        in_specs=[tile(width)] + [whole(a) for a in grads + owned],
        out_specs=[tile(width)] + [whole(a) for a in shapes],
        compiler_params=params(),
        name="finish",
    )(input_grad, *grads, *owned)
    g_q, g_k, g_v, g_o, g_g, g_u, g_d = grads
    return output[None], input_grad[None], gain_grads[:, 0], g_q, g_k, g_v, g_o, gain_grads[:, 1], g_g, g_u, g_d


def solution(mesh):
    rows_placed, vector, matrix = P("seq", "span", None), P(("seq", "span")), P(("seq", "span"), None)
    return jax.shard_map(
        per_device,
        mesh=mesh,
        in_specs=(rows_placed, P("seq", None), vector, matrix, matrix, matrix, matrix, vector, matrix, matrix, matrix, rows_placed),
        out_specs=(rows_placed, rows_placed, vector, matrix, matrix, matrix, matrix, vector, matrix, matrix, matrix),
        check_vma=False,
    )
```

```python
import functools
import math

import jax
import jax.numpy as jnp
from jax import lax
from jax.experimental import pallas as pl
from jax.experimental.pallas import tpu as pltpu
from jax.sharding import PartitionSpec as P

HEAD_DIM = 64
HALO = 576
FRONT = 640
QB = 128
WIN = FRONT + QB
LANES = 128
EPS = 1e-5
SCALE = 0.125
AWAY = -1e30
BF = jnp.bfloat16
F32 = jnp.float32
VMEM_LIMIT = 63 * 1024 * 1024


def dot(a, b):
    return lax.dot_general(a, b, (((1,), (0,)), ((), ())), preferred_element_type=F32)


def dot_nt(a, b):
    return lax.dot_general(a, b, (((1,), (1,)), ((), ())), preferred_element_type=F32)


def dot_tn(a, b):
    return lax.dot_general(a, b, (((0,), (0,)), ((), ())), preferred_element_type=F32)


def rotated(v, cos, sin):
    lane = lax.broadcasted_iota(jnp.int32, v.shape, 1)
    swapped = jnp.where(lane % 64 < 32, pltpu.roll(v, 96, 1), pltpu.roll(v, 32, 1))
    return v * cos + swapped * sin


def turns(table):
    first = lax.broadcasted_iota(jnp.int32, table.shape, 1) % 64 < 32
    cos = jnp.where(first, table, pltpu.roll(table, 32, 1))
    sin = jnp.where(first, -pltpu.roll(table, 96, 1), table)
    return cos, sin


def both_heads(v):
    lane = lax.broadcasted_iota(jnp.int32, v.shape, 1)
    zero = jnp.zeros_like(v)
    return jnp.concatenate([jnp.where(lane < 64, v, zero), jnp.where(lane < 64, zero, v)], axis=0)


def one_of_both(v):
    rows = v.shape[0] // 2
    lane = lax.broadcasted_iota(jnp.int32, (rows, v.shape[1]), 1)
    return jnp.where(lane < 64, v[:rows], v[rows:])


def norm_rows(x):
    return lax.rsqrt(jnp.mean(x * x, axis=-1, keepdims=True) + EPS)


def in_thirds(v, lane):
    high = v.astype(BF)
    rest = v - high.astype(F32)
    middle = rest.astype(BF)
    last = (rest - middle.astype(F32)).astype(BF)
    return jnp.where(lane < 48, high, jnp.where(lane < 64, middle, last))


def coordinates():
    seq, span = lax.axis_index("seq"), lax.axis_index("span")
    return seq // 4, seq // 2 % 2, seq % 2, span


def device(y, x, core, span):
    return (y * 4 + x * 2 + core, span)


def greet():
    y, x, core, span = coordinates()
    barrier = pltpu.get_barrier_semaphore()
    peers = [device(y, x, core, (span + d) % 4) for d in (1, 2, 3)]
    peers += [device(1 - y, x, core, span), device(y, 1 - x, core, span), device(y, x, 1 - core, span)]
    for peer in peers:
        pl.semaphore_signal(barrier, inc=1, device_id=peer, device_id_type=pl.DeviceIdType.MESH)
    pl.semaphore_wait(barrier, len(peers))


def remote(src, dst, sems, at, to):
    return pltpu.make_async_remote_copy(
        src_ref=src, dst_ref=dst, send_sem=sems.at[0, at], recv_sem=sems.at[1, at], device_id=to,
        device_id_type=pl.DeviceIdType.MESH,
    )


GATHER_COPIES = 8


class Gathered:
    def __init__(self, shard, near, whole, at, count, sems, number):
        self.shard, self.near, self.whole, self.sems = shard, near, whole, sems
        self.first = number * GATHER_COPIES
        self.split = shard.shape[0] % 16 != 0
        self.columns = pl.ds(at, count)
        y, x, core, span = coordinates()
        half = count // 2
        left, right = pl.ds(at, half), pl.ds(at + half, half)
        over_y, over_x = device(1 - y, x, core, span), device(y, 1 - x, core, span)
        own = whole.at[y, x, core]
        rows = pl.ds(0, own.shape[0])
        refs = [(near.at[0], near.at[d], device(y, x, core, (span + d) % 4)) for d in (1, 2, 3)]
        refs += [(r, r, to) for r, to in (
            (whole.at[y, x, core, rows, left], over_y),
            (whole.at[y, x, core, rows, right], over_x),
            (whole.at[pl.ds(0, 2), x, core, rows, left], over_x),
            (whole.at[y, pl.ds(0, 2), core, rows, right], over_y),
            (whole.at[pl.ds(0, 2), pl.ds(0, 2), core, rows, self.columns], device(y, x, 1 - core, span)),
        )]
        self.copies = [remote(src, dst, sems, self.first + i, to) for i, (src, dst, to) in enumerate(refs)]

    def go(self, stage):
        if stage == 0:
            v = self.shard[:, self.columns]
            if self.split:
                half = v.shape[1] // 2
                v = v.astype(F32)
                v = jnp.concatenate([v[:, :half], v[:, half:]], axis=0).astype(BF)
            self.near[0] = v
            for i in (0, 1, 2):
                self.copies[i].start()
        if stage == 1:
            y, x, core, span = coordinates()
            for i in (0, 1, 2):
                self.copies[i].wait_recv()
            pieces = []
            for s in range(4):
                v = self.near[(span - s + 4) % 4]
                if self.split:
                    v = v.astype(F32)
                    half = v.shape[0] // 2
                    v = jnp.concatenate([v[:half], v[half:]], axis=1)
                pieces.append(v)
            self.whole[y, x, core, :, self.columns] = jnp.concatenate(pieces, axis=0).astype(BF)
            for i in (3, 4):
                self.copies[i].start()
        if stage == 2:
            for i in (3, 4):
                self.copies[i].wait_recv()
            for i in (5, 6):
                self.copies[i].start()
        if stage == 3:
            for i in (5, 6):
                self.copies[i].wait_recv()
            self.copies[7].start()
        if stage == 4:
            self.copies[7].wait_recv()

    def finish(self):
        for c in self.copies:
            c.wait_send()


def attention_forward(refs, q_out, k_out, v_out, mixed_out, qaug_out, normed_out, steps, tick):
    tok, halo, weights, gain, kaug, qaug, table = refs
    rows, width = tok.shape
    padded = q_out.shape[0]
    pairs = width // LANES

    def normal(x):
        x = x.astype(F32)
        return (x * norm_rows(x) * gain[0:1, :]).astype(BF)

    def project(which, normed, key_at, query_at):
        count = normed.shape[0]
        product = dot(normed, weights[which]())
        if which == 2:
            v_out[key_at : key_at + count, :] = product.astype(BF)
            return
        c, s = turns(table[key_at : key_at + count, :])
        for t in range(pairs):
            lanes = slice(t * LANES, (t + 1) * LANES)
            turned = rotated(product[:, lanes], c, s)
            if which == 0:
                q_out[query_at : query_at + count, lanes] = (turned * SCALE).astype(BF)
            else:
                k_out[key_at : key_at + count, lanes] = turned.astype(BF)

    lead = FRONT - HALO
    k_out[:lead, :] = jnp.zeros((lead, width), BF)
    v_out[:lead, :] = jnp.zeros((lead, width), BF)
    if padded > rows:
        blank = jnp.zeros((padded - rows, width), BF)
        q_out[rows:, :] = blank
        k_out[FRONT + rows :, :] = blank
        v_out[FRONT + rows :, :] = blank
    parts = [(at, min(480, rows - at)) for at in range(0, rows, 480)]
    for which in range(3):
        steps(which)
        for i, (at, count) in enumerate(parts):
            if which == 0:
                normed_out[at : at + count, :] = normal(tok[at : at + count, :])
            project(which, normed_out[at : at + count, :], FRONT + at, at)
            steps(which, i)

    lane = lax.broadcasted_iota(jnp.int32, (QB, LANES), 1)
    row = lax.broadcasted_iota(jnp.int32, (2 * QB, QB), 0)
    behind = lax.broadcasted_iota(jnp.int32, (2 * QB, QB), 1) <= row % QB

    blocks = padded // QB

    def block(i, carry):
        tick(i)

        @pl.when(i == blocks - FRONT // QB)
        def _():
            steps(3)
            normed = normal(halo[...])
            for which in (1, 2):
                project(which, normed, lead, None)

        start = pl.multiple_of((blocks - 1 - i) * QB, QB)
        k_a = kaug[pl.ds(start, WIN), :]
        q_a = qaug[pl.ds(start, QB), :]
        q_a2 = jnp.concatenate([q_a, q_a], axis=0)
        logs = jnp.zeros((QB, LANES), F32)
        for t in range(pairs):
            at = slice(t * LANES, (t + 1) * LANES)
            q2 = jnp.concatenate([both_heads(q_out[pl.ds(start, QB), at]), q_a2], axis=1)
            k2 = jnp.concatenate([k_out[pl.ds(start, WIN), at], k_a], axis=1)
            s = dot_nt(q2, k2)
            s = jnp.concatenate([s[:, :FRONT], jnp.where(behind, s[:, FRONT:], AWAY)], axis=1)
            top = jnp.max(s, axis=1, keepdims=True)
            p = jnp.exp(s - top).astype(BF)
            v = v_out[pl.ds(start, WIN), at]
            o = dot(p, jnp.concatenate([v, jnp.ones_like(v)], axis=1))
            total = o[:, LANES:]
            mixed_out[pl.ds(start, QB), at] = one_of_both(o[:, :LANES] / total).astype(BF)
            log = top + jnp.log(total)
            for e in range(2):
                h = 2 * t + e
                mine = (lane == 32 + h) | (lane == 48 + h) | (lane == 64 + h)
                logs = jnp.where(mine, log[e * QB : (e + 1) * QB], logs)
        qaug_out[pl.ds(start, QB), :] = jnp.where(lane < 32, q_a, in_thirds(-logs, lane))
        return carry

    lax.fori_loop(0, blocks, block, 0)


def fwd_kernel(tok, halo, wq, wk, wv, gain, kaug, qaug, table, q_out, k_out, v_out, mixed_out, qaug_out, normed_out):
    weights = [lambda w=w: w[...] for w in (wq, wk, wv)]
    refs = (tok, halo, weights, gain, kaug, qaug, table)
    attention_forward(refs, q_out, k_out, v_out, mixed_out, qaug_out, normed_out, lambda *_: None, lambda *_: None)


GATHER_CHUNKS = (
    (0, 0, 1024), (1, 0, 768), (2, 0, 768), (3, 0, 768), (4, 0, 1024), (4, 1024, 1024), (5, 0, 1024), (5, 1024, 1024),
    (6, 0, 256), (6, 256, 256), (6, 512, 256),
)
HALO_AFTER = (10, 1)
HALO_CHUNK = 11
GATHER_BEFORE = (
    ((0, 0), (1, 0), (2, 0), (3, 0), (0, 1), (4, 0), (1, 1), (0, 2), (2, 1), (5, 0), (1, 2), (3, 1), (6, 0), (0, 3), (4, 1), (2, 2), (7, 0), (0, 4)),
    ((4, 2), (6, 1), (1, 4), (9, 0)),
    ((7, 1), (5, 2), (2, 4)),
)
GATHER_PARTS = (
    (((1, 3), (5, 1)), (), ((3, 2), (8, 0)), ()),
    ((), (), ((2, 3),), ((10, 0),)),
    (((3, 3), (8, 1), (11, 0)), (), (), ((9, 1),)),
)
GATHER_BLOCKS = (
    (1, ((4, 3),)),
    (2, ((10, 1), (6, 2))),
    (3, ((7, 2),)),
    (5, ((5, 3),)),
    (6, ((8, 2),)),
    (7, ((9, 2), (10, 2))),
    (9, ((6, 3),)),
    (11, ((7, 3),)),
    (12, ((8, 3),)),
    (13, ((9, 3),)),
)
GATHER_END = ((10, 3), (3, 4), (4, 4), (5, 4), (6, 4), (7, 4), (8, 4), (9, 4), (10, 4))


def fwd_gather_kernel(tok, *refs):
    shards, refs = refs[:7], refs[7:]
    own_gains, kaug, qaug, table = refs[:4]
    outs, refs = refs[4:10], refs[10:]
    gains, refs = refs[0], refs[1:]
    whole_outs, refs = refs[:7], refs[7:]
    n = len(GATHER_CHUNKS)
    halo, nears, wholes = refs[0], refs[1 : n + 1], refs[n + 1 : n + 8]
    first_shard, *kept, sems, halo_sems, out_sems = refs[n + 8 :]
    q_out, k_out, v_out, mixed_out, qaug_out, normed_out = outs
    blocks = mixed_out.shape[0] // QB
    early_outs = [
        pltpu.make_async_copy(held, out, out_sems.at[7 + i])
        for i, (held, out) in enumerate(zip(kept, (q_out, normed_out, k_out, v_out)))
    ]
    rows, width = tok.shape
    y, x, core, span = coordinates()
    own_gains = own_gains[...].astype(F32)
    first_shard[:, :width] = shards[0][...]
    for i in range(2):
        first_shard[:, width + i * LANES : width + (i + 1) * LANES] = jnp.broadcast_to(
            own_gains[:, i : i + 1], (own_gains.shape[0], LANES)
        ).astype(BF)
    shards = (first_shard,) + tuple(shards[1:])
    greet()
    to_next = remote(tok.at[pl.ds(rows - HALO, HALO)], halo, halo_sems, 0, device(y, x, core, (span + 1) % 4))

    chunks = [
        Gathered(shards[w], nears[i], wholes[w], at, count, sems, i) for i, (w, at, count) in enumerate(GATHER_CHUNKS)
    ]
    out_copies = [pltpu.make_async_copy(w, o, out_sems.at[i]) for i, (w, o) in enumerate(zip(wholes, whole_outs))]

    def go(events):
        for chunk, stage in events:
            if chunk == HALO_CHUNK:
                to_next.start()
                continue
            chunks[chunk].go(stage)
            w, at, count = GATHER_CHUNKS[chunk]
            if stage == 4 and (chunk + 1 == len(GATHER_CHUNKS) or GATHER_CHUNKS[chunk + 1][0] != w):
                out_copies[w].start()

    def steps(which, part=None):
        if which == 3:
            to_next.wait_recv()
            return
        if part is not None:
            go(GATHER_PARTS[which][part])
            if (which, part) == (2, 3):
                for c in early_outs[:2]:
                    c.start()
            return
        go(GATHER_BEFORE[which])
        if which == 0:
            both = wholes[0][...].reshape(width, -1)[:, width:].astype(F32)
            both = [jnp.transpose(both[:, i * LANES : (i + 1) * LANES])[:1] for i in range(2)]
            gains[...] = jnp.concatenate(both + [jnp.zeros((6, width), F32)], axis=0)

    def tick(i):
        for at, events in GATHER_BLOCKS:
            @pl.when(i == at)
            def _():
                go(events)

        @pl.when(i == blocks - 1)
        def _():
            for c in early_outs[2:]:
                c.start()

    weights = [lambda w=w: w[...].reshape(width, w.shape[-1])[:, :width] for w in wholes[:3]]
    q, normed, k, v = kept
    attention_forward((tok, halo, weights, gains, kaug, qaug, table), q, k, v, mixed_out, qaug_out, normed, steps, tick)
    go(GATHER_END)
    to_next.wait_send()
    for c in chunks:
        c.finish()
    for c in out_copies + early_outs:
        c.wait()


def attention_backward(b, refs, dq_out, add):
    q, k, v, dmixed, kaug, qaug, daug, table = refs
    width = q.shape[1]
    lead = FRONT - HALO
    lane = lax.broadcasted_iota(jnp.int32, (QB, LANES), 1)
    key_row = lax.broadcasted_iota(jnp.int32, (QB, 2 * QB), 0)
    behind = key_row <= lax.broadcasted_iota(jnp.int32, (QB, 2 * QB), 1) % QB
    start = pl.multiple_of(b * QB, QB)
    keys = pl.ds(pl.multiple_of(start + lead, lead), WIN - lead)
    k_a = kaug[keys, :]
    q_a = qaug[pl.ds(start, QB), :]
    d_a = daug[pl.ds(start, QB), :]
    c, s_ = turns(table[pl.ds(start + FRONT, QB), :])
    zero = jnp.zeros_like(q_a)
    for t in range(width // LANES):
        at = slice(t * LANES, (t + 1) * LANES)
        mine = [(lane >= 32) & (lane % 16 == 2 * t + e) for e in range(2)]
        q_2 = both_heads(q[pl.ds(start, QB), at])
        q_aug = jnp.concatenate([jnp.where((lane < 32) | mine[e], q_a, zero) for e in range(2)], axis=0)
        d_2 = both_heads(dmixed[pl.ds(start, QB), at])
        d_aug = jnp.concatenate([jnp.where(mine[e], d_a, zero) for e in range(2)], axis=0)
        k_p = k[keys, at]
        st = dot_nt(jnp.concatenate([k_p, k_a], axis=1), jnp.concatenate([q_2, q_aug], axis=1))
        st = jnp.concatenate([st[:HALO], jnp.where(behind, st[HALO:], AWAY)], axis=0)
        pt = jnp.exp(st)
        dpt = dot_nt(jnp.concatenate([v[keys, at], k_a], axis=1), jnp.concatenate([d_2, d_aug], axis=1))
        dst = (pt * dpt).astype(BF)
        add(t, dot(dst, q_2), dot(pt.astype(BF), d_2))
        dq = one_of_both(dot_tn(dst, k_p)) * SCALE
        dq_out[pl.ds(start, QB), at] = rotated(dq, c, -s_).astype(BF)


def bwd_kernel(*refs):
    dq_out, dk_out, dv_out = refs[8:]
    padded = dq_out.shape[0]
    dk_out[...] = jnp.zeros_like(dk_out)
    dv_out[...] = jnp.zeros_like(dv_out)
    lead = FRONT - HALO

    def block(b, carry):
        keys = pl.ds(pl.multiple_of(b * QB + lead, lead), WIN - lead)

        def add(t, dk, dv):
            at = slice(t * LANES, (t + 1) * LANES)
            dk_out[keys, at] += dk
            dv_out[keys, at] += dv

        attention_backward(b, refs[:8], dq_out, add)
        return carry

    lax.fori_loop(0, padded // QB, block, 0)


SCATTER_COPIES = 8
SCATTER_CHUNKS = (
    (0, 0, 768), (1, 0, 1024), (1, 1024, 1024), (2, 0, 1024), (2, 1024, 1024), (3, 0, 256), (3, 256, 256), (3, 512, 256),
)
SUB = 512
SUB_SLOTS = 2
TALL = 256


class Scattered:
    def __init__(self, whole, at, count, out, bufs, sems, number):
        self.whole, self.out = whole, out
        self.got, self.left, self.right, self.left_2, self.right_2, self.near, self.far = bufs
        self.at, self.count = at, count
        self.columns = pl.ds(0, count)
        self.half = half = count // 2
        self.left_whole = False
        y, x, core, span = coordinates()
        rows = pl.ds(0, whole.shape[3])
        two = pl.ds(0, 2)
        lo, hi = pl.ds(0, half), pl.ds(half, half)
        over_y, over_x = device(1 - y, x, core, span), device(y, 1 - x, core, span)
        got = self.got
        refs = [
            (whole.at[two, two, 1 - core, rows, self.columns], got, device(y, x, 1 - core, span)),
            (got.at[two, 1 - x, rows, lo], self.left, over_x),
            (got.at[1 - y, two, rows, hi], self.right, over_y),
            (got.at[1 - y, x, rows, lo], self.left_2, over_y),
            (got.at[y, 1 - x, rows, hi], self.right_2, over_x),
        ]
        refs += [(self.near.at[(span + d) % 4], self.far.at[d - 1], device(y, x, core, (span + d) % 4)) for d in (1, 2, 3)]
        first = number * SCATTER_COPIES
        self.copies = [remote(src, dst, sems, first + i, to) for i, (src, dst, to) in enumerate(refs)]
    def go(self, stage):
        y, x, core, span = coordinates()
        got, half = self.got, self.half
        lo, hi = pl.ds(0, half), pl.ds(half, half)
        if stage == 0:
            self.copies[0].start()
        if stage == 1:
            self.copies[0].wait_recv()
            for i in range(2):
                for j in range(2):
                    got[i, j] = got[i, j] + self.whole[i, j, core, :, self.columns]
            for i in (1, 2):
                self.copies[i].start()
        if stage == 2:
            for i in (1, 2):
                self.copies[i].wait_recv()
            for i in range(2):
                got[i, x, :, lo] = got[i, x, :, lo] + self.left[i]
                got[y, i, :, hi] = got[y, i, :, hi] + self.right[i]
            for i in (3, 4):
                self.copies[i].start()
        if stage == 3:
            for i in (3, 4):
                self.copies[i].wait_recv()
            total = jnp.concatenate(
                [got[y, x, :, r].astype(F32) + other[...].astype(F32) for r, other in ((lo, self.left_2), (hi, self.right_2))],
                axis=1,
            )
            depth = total.shape[0] // 4
            for s in range(4):
                v = total[s * depth : (s + 1) * depth]
                if depth % 16:
                    v = jnp.concatenate([v[:, :half], v[:, half:]], axis=0)
                self.near[s] = v.astype(BF)
            for i in (5, 6, 7):
                self.copies[i].start()
        if stage == 4:
            for i in (5, 6, 7):
                self.copies[i].wait_recv()
            v = self.near[span].astype(F32)
            for d in range(3):
                v = v + self.far[d].astype(F32)
            depth = self.out.shape[0]
            if depth % 16:
                v = jnp.concatenate([v[:depth], v[depth:]], axis=1)
            self.out[:, self.at : self.at + self.count] = v

    def leave_whole(self):
        if not self.left_whole:
            self.copies[0].wait_send()
        self.left_whole = True

    def finish(self):
        self.leave_whole()
        for c in self.copies[1:]:
            c.wait_send()


def scatter_buffers(rows, count):
    depth = rows // 4
    piece = (2 * depth, count // 2) if depth % 16 else (depth, count)
    shapes = [
        (2, 2, rows, count), (2, rows, count // 2), (2, rows, count // 2), (rows, count // 2), (rows, count // 2),
        (4,) + piece, (3,) + piece,
    ]
    return [pltpu.VMEM(shape, BF) for shape in shapes]


HALO_BLOCKS = FRONT // QB
SCATTER_AT = ((0, 1, 3, 5), (5, 6, 8, 11), (6, 7, 10, 14), (7, 8, 12, 15), (8, 9, 13, 16))
GRAD_TICKS = 4


def scatter_plan(blocks):
    ticks = [[] for _ in range(blocks + GRAD_TICKS)]
    for t, j, stage in sorted((t, j, stage) for j, when in enumerate(SCATTER_AT) for stage, t in enumerate(when)):
        ticks[t].append((j, stage))
    return ticks


def bwd_scatter_kernel(
    q_in, k_in, v_in, dmixed_in, kaug, qaug, daug, table, tok, gains, d_resid, wq_in, wk_in, wv_in,
    normed_in, g_out, n2_in, cot_in, hid_in, dg_in, du_in,
    input_grad, s_query, s_key, s_value, s_out, s_gate, s_up, s_down,
    q, k, v, dmixed, dk_win, dv_win, halo_out, halo_in, resid_block, out_block, subs, wide, tall, *refs,
):
    rows, width = tok.shape
    padded = q.shape[0]
    blocks = padded // QB
    pairs = width // LANES
    lead = FRONT - HALO
    slots = WIN // QB
    n = len(SCATTER_CHUNKS)
    chunk_bufs = [refs[7 * i : 7 * i + 7] for i in range(n + 3)]
    refs = refs[7 * (n + 3) :]
    sems, in_sems, sub_sems, halo_sems, block_sems = refs
    y, x, core, span = coordinates()

    near_q, near_k = HALO_BLOCKS * QB, 2 * FRONT
    far_q = pl.ds(near_q, padded - near_q)
    lower, upper = pl.ds(0, padded - near_q), pl.ds(padded - near_q, near_q)
    far_k = pl.ds(near_k, near_q)
    rest = pl.ds(near_k + near_q, k.shape[0] - near_k - near_q)
    one, two = pl.ds(0, near_q), pl.ds(0, near_k)
    early_rows = (blocks - 3) * QB
    weights = [halo_out.at[0], halo_out.at[1], halo_in.at[0]]
    by_name = dict(
        q=(q_in.at[one], q.at[one]), k=(k_in.at[two], k.at[two]), v=(v_in.at[two], v.at[two]),
        d=(dmixed_in.at[one], dmixed.at[one]),
        o=(g_out, wide.at[0, pl.ds(0, 2), pl.ds(0, 2), pl.ds(0, 2), pl.ds(0, width // 8), pl.ds(0, width)]),
        n_low=(n2_in.at[lower], q.at[far_q]), n_high=(n2_in.at[upper], k.at[far_k]),
        c=(cot_in, dmixed.at[pl.ds(0, rows)]),
        k_rest=(k_in.at[rest], k.at[rest]), v_rest=(v_in.at[rest], v.at[rest]),
        q_far=(q_in.at[far_q], q.at[far_q]), k_far=(k_in.at[far_k], k.at[far_k]),
        d_far=(dmixed_in.at[far_q], dmixed.at[far_q]), v_far=(v_in.at[far_k], v.at[far_k]),
        w_q=(wq_in.at[pl.ds(0, width), pl.ds(0, width)], weights[0]),
        w_k=(wk_in, weights[1]), w_v=(wv_in, weights[2]),
        normed_low=(normed_in.at[pl.ds(0, early_rows)], dmixed.at[pl.ds(0, early_rows)]),
        normed_high=(
            normed_in.at[pl.ds(early_rows, rows - early_rows)], dmixed.at[pl.ds(early_rows, rows - early_rows)]
        ),
    )
    arrivals = {
        name: pltpu.make_async_copy(src, dst, in_sems.at[i]) for i, (name, (src, dst)) in enumerate(by_name.items())
    }
    brought = [(src, f) for src in (dg_in, du_in, hid_in) for f in range(src.shape[0])]
    sub_copies = [
        pltpu.make_async_copy(src.at[f], subs.at[i % SUB_SLOTS], sub_sems.at[i])
        for i, (src, f) in enumerate(brought)
    ]

    def bring(*names):
        for name in names:
            arrivals[name].start()

    def await_all(*names):
        for name in names:
            arrivals[name].wait()

    bring("o", "q", "k", "v", "d", "n_low", "n_high", "k_rest", "v_rest", "d_far", "v_far")
    for c in sub_copies[:SUB_SLOTS]:
        c.start()
    greet()

    sums = (s_out, s_gate, s_up, s_down)
    chunks = []
    for i, (w, at, count) in enumerate(SCATTER_CHUNKS):
        whole = wide.at[i % 3] if w < 3 else tall.at[at // count]
        chunks.append(Scattered(whole, at, count, sums[w], chunk_bufs[i], sems, i))
    own = [wide.at[i] for i in (2, 0, 1)]
    chunks += [
        Scattered(own[i], 0, width, (s_query, s_key, s_value)[i], chunk_bufs[n + i], sems, n + i) for i in range(3)
    ]
    to_last = remote(
        halo_out.at[pl.ds(0, 2), pl.ds(0, HALO)], halo_in.at[pl.ds(0, 2), pl.ds(0, HALO)], halo_sems, 0, device(y, x, core, (span + 3) % 4))
    ticks = scatter_plan(blocks)
    dk_win[...] = jnp.zeros_like(dk_win)
    dv_win[...] = jnp.zeros_like(dv_win)
    await_all("o", "q", "k", "v", "d")

    def block_of(inside):
        return functools.partial(block, inside)

    def block(inside, b, carry):
        for i, todo in inside.items():
            if todo:
                @pl.when(b == i)
                def _():
                    for chunk, stage in todo:
                        chunks[chunk].go(stage)

        @pl.when(b == blocks - 3)
        def _():
            bring("normed_low")

        def add(t, dk, dv):
            at = slice(t * LANES, (t + 1) * LANES)
            for win, grad in ((dk_win, dk), (dv_win, dv)):
                for j in range(slots):
                    count = min(QB, WIN - lead - j * QB)
                    win[lax.rem(b + j, slots), :count, at] += grad[j * QB : j * QB + count]

        attention_backward(b, (q, k, v, dmixed, kaug, qaug, daug, table), q, add)

        slot = lax.rem(b, slots)
        at = pl.ds(pl.multiple_of(b * QB + lead, lead), QB)

        @pl.when(b < FRONT // QB)
        def _():
            to = pl.ds(pl.multiple_of(b * QB, QB), QB)
            halo_out[0, to, :] = dk_win[slot].astype(BF)
            halo_out[1, to, :] = dv_win[slot].astype(BF)

        @pl.when((b >= FRONT // QB - 1) & (b < blocks - 1))
        def _():
            c, s_ = turns(table[at, :])
            for t in range(pairs):
                lanes = slice(t * LANES, (t + 1) * LANES)
                k[at, lanes] = rotated(dk_win[slot, :, lanes], c, -s_).astype(BF)
            v[at, :] = dv_win[slot].astype(BF)

        @pl.when(b < blocks - 1)
        def _():
            dk_win[slot] = jnp.zeros((QB, width), F32)
            dv_win[slot] = jnp.zeros((QB, width), F32)

        return carry

    lax.fori_loop(0, HALO_BLOCKS, block_of({b: ticks[b] for b in range(HALO_BLOCKS)}), 0)
    to_last.start()

    sub = 0
    low, group = padded - near_q, tall.shape[4]
    await_all("n_low", "n_high")

    def next_sub():
        nonlocal sub
        if sub + SUB_SLOTS < len(sub_copies):
            sub_copies[sub + SUB_SLOTS].start()
        sub += 1

    for i, (w, at, count) in enumerate(SCATTER_CHUNKS[: GRAD_TICKS + 1]):
        if w == 0:
            continue
        if i >= 3:
            chunks[i - 3].leave_whole()
        for f in range(0, count, SUB):
            sub_copies[sub].wait()
            here = subs.at[sub % SUB_SLOTS]
            total = dot_tn(q[near_q:, :], here[:low, :]) + dot_tn(k[near_k : near_k + near_q, :], here[low:, :])
            wide[i % 3, :, :, :, :, f : f + SUB] = total.reshape(2, 2, 2, width // 8, SUB).astype(BF)
            next_sub()
        if i == GRAD_TICKS:
            bring("q_far", "k_far")
        for chunk, stage in ticks[HALO_BLOCKS + i - 1]:
            chunks[chunk].go(stage)
    await_all("q_far", "k_far", "d_far", "v_far", "k_rest", "v_rest")
    lax.fori_loop(HALO_BLOCKS, blocks, block_of({b: ticks[b + GRAD_TICKS] for b in range(HALO_BLOCKS, blocks)}), 0)
    bring("normed_high")
    to_last.wait_send()
    bring("w_q", "w_k")

    step = resid_block.shape[1]
    parts = [(at, min(step, rows - at)) for at in range(0, rows, step)]
    resid_in = [
        pltpu.make_async_copy(
            d_resid.at[pl.ds(at, count)], resid_block.at[i % 2, pl.ds(0, count)], block_sems.at[0, i]
        ) for i, (at, count) in enumerate(parts)
    ]
    grad_copies = [
        pltpu.make_async_copy(
            out_block.at[i % 2, pl.ds(0, count)], input_grad.at[pl.ds(at, count)], block_sems.at[1, i]
        ) for i, (at, count) in enumerate(parts)
    ]
    resid_in[0].start()
    resid_in[1].start()

    def go(*events):
        for chunk, stage in events:
            chunks[chunk].go(stage)

    g = gains[0:1, :]
    normed = dmixed
    await_all("normed_low", "normed_high")

    def weight_grad(i, grad):
        for j in range(2):
            half = width // 2
            total = dot_tn(normed[:rows, j * half : (j + 1) * half], grad)
            own[i][j, :, :, :, pl.ds(0, width)] = total.reshape(2, 2, half // 4, width).astype(BF)

    for i in (2, 3, 4):
        chunks[i].leave_whole()
    weight_grad(0, q[:rows, :])
    go((n, 0), (0, 4))
    to_last.wait_recv()
    for j in range(slots):
        base = (blocks - 1) * QB + lead + j * QB
        slot = (blocks - 1 + j) % slots
        count = min(QB, FRONT + rows - base)
        first = max(base, FRONT + rows - HALO)
        for which, win, whole in ((0, dk_win, k), (1, dv_win, v)):
            grad = win[slot, :count, :]
            more = halo_in[which, first - (FRONT + rows - HALO) : base + count - (FRONT + rows - HALO), :].astype(F32)
            if first > base:
                more = jnp.concatenate([jnp.zeros((first - base, width), F32), more], axis=0)
            grad = grad + more
            if which:
                whole[base : base + count, :] = grad.astype(BF)
                continue
            c, s_ = turns(table[base : base + count, :])
            for t in range(pairs):
                lanes = slice(t * LANES, (t + 1) * LANES)
                whole[base : base + count, lanes] = rotated(grad[:, lanes], c, -s_).astype(BF)
    bring("w_v")
    weight_grad(1, k[FRONT : FRONT + rows, :])
    go((n, 1), (n + 1, 0), (1, 4))
    weight_grad(2, v[FRONT : FRONT + rows, :])
    bring("c")
    go((n, 2), (n + 1, 1), (n + 2, 0), (2, 4))

    await_all("c")
    beside = (((n + 1, 2), (n + 2, 1)), ((n, 3),), ((n + 1, 3), (n + 2, 2)), ((n + 2, 3),))
    for i in range(hid_in.shape[0]):
        sub_copies[sub].wait()
        total = dot_tn(subs[sub % SUB_SLOTS, :rows, :], dmixed[:rows, :]).astype(BF)
        for r in range(0, SUB, group):
            to = (i * SUB + r) // group
            for j in range(width // TALL):
                tall[j, to // 4, to // 2 % 2, to % 2] = total[r : r + group, j * TALL : (j + 1) * TALL]
        next_sub()
        go(*beside[i])
    go((5, 0), (6, 0), (7, 0))
    await_all("w_q", "w_k", "w_v")
    between = (
        ((5, 1), (6, 1), (7, 1)), ((n, 4), (3, 4)), ((5, 2), (6, 2)), ((7, 2), (n + 1, 4)), ((5, 3), (6, 3)),
        ((7, 3), (n + 2, 4)), ((4, 4), (5, 4)), ((6, 4), (7, 4)),
    )
    for i, (at, count) in enumerate(parts):
        grads = (q[at : at + count, :], k[FRONT + at : FRONT + at + count, :], v[FRONT + at : FRONT + at + count, :])
        dn = sum(dot_nt(d, weights[w][...]) for w, d in enumerate(grads))
        x = tok[at : at + count, :].astype(F32)
        inv = norm_rows(x)
        hat = x * inv
        e = dn * g
        resid_in[i].wait()
        total = resid_block[i % 2, :count] + inv * (e - hat * jnp.mean(e * hat, axis=-1, keepdims=True))
        if i >= 2:
            grad_copies[i - 2].wait()
        out_block[i % 2, :count] = total.astype(BF)
        grad_copies[i].start()
        if i + 2 < len(parts):
            resid_in[i + 2].start()
        go(*between[i])
    for c in chunks:
        c.finish()
    for c in grad_copies[-2:]:
        c.wait()


def finish_kernel(input_in, *refs):
    grads, (wq, wk, wv, wg, wu, gains) = refs[:7], refs[7:13]
    input_out, gain_out, outs = refs[13], refs[14], refs[15:]
    input_out[...] = input_in[...]

    @pl.when(pl.program_id(0) == 0)
    def _():
        for grad, out in zip(grads, outs):
            out[...] = grad[...]
        sums = []
        for pairs in (((0, wq), (1, wk), (2, wv)), ((4, wg), (5, wu))):
            sums.append(sum(jnp.sum(grads[i][...] * w[...].astype(F32), axis=1, keepdims=True) for i, w in pairs))
        gain_out[...] = jnp.concatenate(sums, axis=1) / gains[...].astype(F32)


FF_STEP = 512
ROW_STEP = 480


def mlp_kernel(rows, x_ref, mixed, c_ref, wo, wg, wu, wd, gains,
               out, d_resid_out, d_mixed_out, daug_out, grad_out, n2_out, hid_out, dg_out, du_out, total):
    i = pl.program_id(0)
    count, width = x_ref.shape
    valid = lax.broadcasted_iota(jnp.int32, (count, width), 0) + i * count < rows
    c = jnp.where(valid, c_ref[...], jnp.zeros((count, width), BF))
    x = jnp.where(valid, x_ref[...].astype(F32), 0.0)
    mix = mixed[...]
    resid = x + dot(mix, wo[...])
    r = norm_rows(resid)
    g = gains[1:2, :]
    hat = resid * r
    n2 = (hat * g).astype(BF)
    n2_out[...] = n2
    acc = resid
    dn = jnp.zeros((count, width), F32)
    for f in range(0, wg.shape[1], FF_STEP):
        at = slice(f, f + FF_STEP)
        gate = dot(n2, wg[:, at])
        up = dot(n2, wu[:, at])
        sig = jax.nn.sigmoid(gate)
        silu = gate * sig
        hid = (silu * up).astype(BF)
        for j in range(0, FF_STEP, SUB):
            hid_out[(f + j) // SUB] = hid[:, j : j + SUB]
        acc = acc + dot(hid, wd[at, :])
        dh = dot_nt(c, wd[at, :])
        dg = (dh * up * sig * (1.0 + gate * (1.0 - sig))).astype(BF)
        du = (dh * silu).astype(BF)
        for j in range(0, FF_STEP, SUB):
            dg_out[(f + j) // SUB] = dg[:, j : j + SUB]
            du_out[(f + j) // SUB] = du[:, j : j + SUB]
        dn = dn + dot_nt(dg, wg[:, at]) + dot_nt(du, wu[:, at])
    out[...] = acc.astype(BF)
    e = dn * g
    d_resid = c.astype(F32) + r * (e - hat * jnp.mean(e * hat, axis=-1, keepdims=True))
    d_resid_out[...] = d_resid
    d_branch = d_resid.astype(BF)
    total[...] = jnp.where(i == 0, 0.0, total[...]) + dot_tn(mix, d_branch)

    @pl.when(i == pl.num_programs(0) - 1)
    def _():
        grad_out[...] = total[...].astype(BF)

    d_mixed = dot_nt(d_branch, wo[...]).astype(BF)
    d_mixed_out[...] = d_mixed

    e_row = lax.broadcasted_iota(jnp.int32, (width, LANES), 0) // HEAD_DIM
    e_lane = lax.broadcasted_iota(jnp.int32, (width, LANES), 1)
    picks = ((e_lane >= 32) & (e_lane < 80) & (e_lane % 16 == e_row)).astype(F32).astype(BF)
    prod = d_mixed.astype(F32) * mix.astype(F32)
    high = prod.astype(BF)
    low = (prod - high.astype(F32)).astype(BF)
    lane = lax.broadcasted_iota(jnp.int32, (count, LANES), 1)
    daug_out[...] = in_thirds(-(dot(high, picks) + dot(low, picks)), lane)


def slots_of(item_lengths, first, count):
    ends = jnp.cumsum(item_lengths[0])[None, :]
    slots = first + jnp.arange(count, dtype=jnp.int32)
    reached = (slots[:, None] >= ends) & (item_lengths[0] > 0)[None, :]
    segment = jnp.sum(reached.astype(jnp.int32), axis=1)
    begin = jnp.max(jnp.where(reached, ends, 0), axis=1)
    return slots, segment % 16, slots - begin


def side_arrays(item_lengths, local_rows, padded):
    offset = lax.axis_index("span") * local_rows
    count = FRONT + padded
    slots, group, position = slots_of(item_lengths, offset - FRONT, count)
    lane = jnp.arange(LANES, dtype=jnp.int32)[None, :]
    away = (slots < 0) | (jnp.arange(count) < FRONT - HALO)
    where_key = jnp.where(away, 16, group)[:, None]
    marks = (lane >= 32) & (lane < 80) & (lane % 16 < 12)
    kaug = ((lane == where_key) | marks).astype(BF)
    qaug = jnp.where((lane <= 16) & (lane != group[FRONT:, None]), AWAY, 0.0).astype(BF)
    half = HEAD_DIM // 2
    frequency = 10000.0 ** (-(lane % half).astype(F32) / half)
    quarter = jnp.where(lane % HEAD_DIM < half, 0.0, 0.5 * math.pi)
    return kaug, qaug, cosine(position[:, None].astype(F32) * frequency - quarter)


def cosine(v):
    number = jnp.floor(v * (0.5 / math.pi) + 0.5)
    rest = (v - number * 6.28125) - number * (2.0 * math.pi - 6.28125)
    square = rest * rest
    total = jnp.full_like(v, 1.0 / math.factorial(18))
    for k in range(8, -1, -1):
        total = 1.0 / math.factorial(2 * k) - total * square
    return total


def vmem():
    return pl.BlockSpec(memory_space=pltpu.VMEM)


def params(**more):
    return pltpu.CompilerParams(vmem_limit_bytes=VMEM_LIMIT, **more)


def call_backward(tok, q, k, v, d_mixed, kaug, qaug, daug, table, gains, d_resid, wq, wk, wv, normed, grad_out, *factors):
    rows, width = tok.shape
    ff = factors[-1].shape[0] * SUB
    padded, ext = q.shape[0], k.shape[0]
    sds = jax.ShapeDtypeStruct
    anywhere = pl.BlockSpec(memory_space=pl.ANY)
    depths = (width // 8, width // 8, width // 8, ff // 8)
    grad_out = grad_out.reshape(2, 2, 2, width // 8, width)
    buffers = []
    for w, _, count in SCATTER_CHUNKS:
        buffers += scatter_buffers(depths[w], count)
    for _ in range(3):
        buffers += scatter_buffers(width // 8, width)
    part = 256
    return pl.pallas_call(
        bwd_scatter_kernel,
        out_shape=[sds((rows, width), BF)] + [sds((width // 32, width), F32)] * 4
        + [sds((width // 32, ff), F32)] * 2 + [sds((ff // 32, width), F32)],
        in_specs=[anywhere] * 4 + [vmem()] * 6 + [anywhere] * 11,
        out_specs=[anywhere] + [vmem()] * 7,
        scratch_shapes=[
            pltpu.VMEM((padded, width), BF), pltpu.VMEM((ext, width), BF), pltpu.VMEM((ext, width), BF),
            pltpu.VMEM((padded, width), BF),
            pltpu.VMEM((WIN // QB, QB, width), F32), pltpu.VMEM((WIN // QB, QB, width), F32),
            pltpu.VMEM((2, max(FRONT, width), width), BF), pltpu.VMEM((2, max(HALO, width), width), BF),
            pltpu.VMEM((2, part, width), F32), pltpu.VMEM((2, part, width), BF),
            pltpu.VMEM((SUB_SLOTS, padded, SUB), BF),
            pltpu.VMEM((3, 2, 2, 2, width // 8, 1024), BF), pltpu.VMEM((width // TALL, 2, 2, 2, ff // 8, TALL), BF),
        ] + buffers + [
            pltpu.SemaphoreType.DMA((2, (len(SCATTER_CHUNKS) + 3) * SCATTER_COPIES)),
            pltpu.SemaphoreType.DMA((20,)),
            pltpu.SemaphoreType.DMA((3 * ff // SUB,)),
            pltpu.SemaphoreType.DMA((2, 1)),
            pltpu.SemaphoreType.DMA((2, -(-rows // part))),
        ],
        compiler_params=params(collective_id=1, has_side_effects=True),
        name="attend_back",
    )(q, k, v, d_mixed, kaug, qaug, daug, table, tok, gains, d_resid, wq, wk, wv, normed, grad_out, *factors)


def per_device(tokens, item_lengths, attn_gain, w_query, w_key, w_value, w_out, mlp_gain, w_gate, w_up, w_down, cotangent):
    rows, width = tokens.shape[1:]
    ff = w_gate.shape[1]
    padded = -(-rows // ROW_STEP) * ROW_STEP
    ext = FRONT + padded
    axes = ("seq", "span")
    seqs, spans = (lax.axis_size(a) for a in axes)
    direct = (seqs, spans) == (8, 4)
    sds = jax.ShapeDtypeStruct
    anywhere = pl.BlockSpec(memory_space=pl.ANY)
    tok, cot = tokens[0], cotangent[0]
    own_gains = jnp.stack([attn_gain, mlp_gain], axis=1)

    kaug, qaug, table = side_arrays(item_lengths, rows, padded)
    fwd_shapes = [
        sds((padded, width), BF), sds((ext, width), BF), sds((ext, width), BF),
        sds((padded, width), BF), sds((padded, LANES), BF), sds((rows, width), BF),
    ]
    if direct:
        shards = [w_query, w_key, w_value, w_out, w_gate, w_up, w_down]
        whole = [(2, 2, 2, 4 * w.shape[0], w.shape[1]) for w in shards]
        whole[0] = whole[0][:4] + (width + 2 * LANES,)
        near = []
        for w, _, count in GATHER_CHUNKS:
            depth = shards[w].shape[0]
            near.append((4, 2 * depth, count // 2) if depth % 16 else (4, depth, count))
        results = pl.pallas_call(
            fwd_gather_kernel,
            out_shape=fwd_shapes + [sds((8, width), F32)] + [sds(w, BF) for w in whole],
            in_specs=[vmem()] * 12,
            out_specs=[anywhere] * 3 + [vmem()] * 2 + [anywhere, vmem()] + [anywhere] * 7,
            scratch_shapes=[pltpu.VMEM((HALO, width), BF)]
            + [pltpu.VMEM(n, BF) for n in near]
            + [pltpu.VMEM(w, BF) for w in whole]
            + [
                pltpu.VMEM((w_query.shape[0], width + 2 * LANES), BF),
                pltpu.VMEM((padded, width), BF), pltpu.VMEM((rows, width), BF),
                pltpu.VMEM((ext, width), BF), pltpu.VMEM((ext, width), BF),
                pltpu.SemaphoreType.DMA((2, len(GATHER_CHUNKS) * GATHER_COPIES)),
                pltpu.SemaphoreType.DMA((2, 1)),
                pltpu.SemaphoreType.DMA((11,)),
            ],
            compiler_params=params(collective_id=0, has_side_effects=True),
            name="attend",
        )(tok, *shards, own_gains, kaug, qaug, table)
        q, k, v, mixed, qaug, normed, gains = results[:7]
        wq, wk, wv, wo, wg, wu, down = (w.reshape(-1, w.shape[-1]) for w in results[7:])
    else:
        packed = lax.all_gather(jnp.concatenate([w_query, w_key, w_value, w_out, w_gate, w_up], axis=1), axes, axis=0, tiled=True)
        down = lax.all_gather(w_down, axes, axis=0, tiled=True)
        gains = lax.all_gather(own_gains, axes, axis=0, tiled=True).astype(F32)
        gains = jnp.concatenate([jnp.transpose(gains), jnp.zeros((6, width), F32)], axis=0)
        wq, wk, wv, wo = (packed[:, i * width : (i + 1) * width] for i in range(4))
        wg, wu = packed[:, 4 * width : 4 * width + ff], packed[:, 4 * width + ff :]
        halo = lax.ppermute(tok[rows - HALO :], "span", [(i, i + 1) for i in range(spans - 1)])
        q, k, v, mixed, qaug, normed = pl.pallas_call(
            fwd_kernel,
            out_shape=fwd_shapes,
            in_specs=[vmem()] * 9,
            out_specs=[vmem()] * 6,
            compiler_params=params(),
            name="attend",
        )(tok, halo, wq, wk, wv, gains, kaug, qaug, table)

    tile = lambda n: pl.BlockSpec((ROW_STEP, n), lambda i: (i, 0))
    whole = lambda a: pl.BlockSpec(a.shape, lambda i: (0, 0), pipeline_mode=pl.Buffered(1))
    weights = (wo, wg, wu, down)
    output, d_resid, d_mixed, daug, g_o, n2, hid, dg, du = pl.pallas_call(
        functools.partial(mlp_kernel, rows),
        grid=(padded // ROW_STEP,),
        out_shape=[
            sds((rows, width), BF), sds((rows, width), F32), sds((padded, width), BF), sds((padded, LANES), BF),
            sds((width, width), BF), sds((padded, width), BF),
        ] + [sds((ff // SUB, padded, SUB), BF)] * 3,
        in_specs=[tile(width)] * 3 + [whole(a) for a in weights + (gains,)],
        out_specs=[tile(width)] * 3 + [tile(LANES), whole(wo), tile(width)]
        + [pl.BlockSpec((ff // SUB, ROW_STEP, SUB), lambda i: (0, i, 0))] * 3,
        scratch_shapes=[pltpu.VMEM((width, width), F32)],
        compiler_params=params(),
        name="mlp",
    )(tok, mixed, cot, *weights, gains)

    if direct:
        results = call_backward(
            tok, q, k, v, d_mixed, kaug, qaug, daug, table, gains, d_resid, wq, wk, wv, normed, g_o, n2, cot, hid, dg, du
        )
        input_grad, g_q, g_k, g_v, g_o, g_g, g_u, g_d = results
    else:
        dq, dk, dv = pl.pallas_call(
            bwd_kernel,
            out_shape=[sds((padded, width), BF), sds((ext, width), F32), sds((ext, width), F32)],
            in_specs=[vmem()] * 8,
            out_specs=[vmem()] * 3,
            compiler_params=params(),
            name="attend_back",
        )(q, k, v, d_mixed, kaug, qaug, daug, table)
        dq = dq[:rows]
        back = jnp.concatenate([dk[FRONT - HALO : FRONT], dv[FRONT - HALO : FRONT]], axis=1).astype(BF)
        back = lax.ppermute(back, "span", [(i + 1, i) for i in range(spans - 1)]).astype(F32)
        dk, dv = dk[FRONT : FRONT + rows], dv[FRONT : FRONT + rows]
        dk = jnp.concatenate([dk[: rows - HALO], dk[rows - HALO :] + back[:, :width]])
        dv = jnp.concatenate([dv[: rows - HALO], dv[rows - HALO :] + back[:, width:]]).astype(BF)
        half = HEAD_DIM // 2
        c, s = (table[FRONT : FRONT + rows, None, i * half : (i + 1) * half] for i in range(2))
        dk3 = dk.reshape(rows, width // HEAD_DIM, HEAD_DIM)
        a, b = dk3[..., :half], dk3[..., half:]
        dk = jnp.concatenate([a * c + b * s, b * c - a * s], axis=-1).reshape(rows, width).astype(BF)
        x = tok.astype(F32)
        inv = norm_rows(x)
        hat = x * inv
        gain_one = gains[:1]
        flat = lambda a: jnp.transpose(a, (1, 0, 2)).reshape(padded, ff)
        dn = sum(dot_nt(d, w) for d, w in ((dq, wq), (dk, wk), (dv, wv)))
        e = dn * gain_one
        input_grad = (d_resid + inv * (e - hat * jnp.mean(e * hat, axis=-1, keepdims=True))).astype(BF)
        sums = jnp.concatenate([dot_tn(normed, d) for d in (dq, dk, dv)] + [g_o.astype(F32), dot_tn(n2, flat(dg)), dot_tn(n2, flat(du))], axis=1)
        scatter = lambda g: lax.psum_scatter(g, axes, scatter_dimension=0, tiled=True)
        sums, g_d = scatter(sums), scatter(dot_tn(flat(hid)[:rows], cot))
        g_q, g_k, g_v, g_o = (sums[:, i * width : (i + 1) * width] for i in range(4))
        g_g, g_u = sums[:, 4 * width : 4 * width + ff], sums[:, 4 * width + ff :]

    grads = (g_q, g_k, g_v, g_o, g_g, g_u, g_d)
    owned = (w_query, w_key, w_value, w_gate, w_up, own_gains)
    shapes = [sds((w_query.shape[0], 2), F32)] + [sds(g.shape, F32) for g in grads]
    input_grad, gain_grads, *grads = pl.pallas_call(
        finish_kernel,
        grid=(padded // ROW_STEP,),
        out_shape=[sds((rows, width), BF)] + shapes,
        in_specs=[tile(width)] + [whole(a) for a in grads + owned],
        out_specs=[tile(width)] + [whole(a) for a in shapes],
        compiler_params=params(),
        name="finish",
    )(input_grad, *grads, *owned)
    g_q, g_k, g_v, g_o, g_g, g_u, g_d = grads
    return output[None], input_grad[None], gain_grads[:, 0], g_q, g_k, g_v, g_o, gain_grads[:, 1], g_g, g_u, g_d


def solution(mesh):
    rows_placed, vector, matrix = P("seq", "span", None), P(("seq", "span")), P(("seq", "span"), None)
    return jax.shard_map(
        per_device,
        mesh=mesh,
        in_specs=(rows_placed, P("seq", None), vector, matrix, matrix, matrix, matrix, vector, matrix, matrix, matrix, rows_placed),
        out_specs=(rows_placed, rows_placed, vector, matrix, matrix, matrix, matrix, vector, matrix, matrix, matrix),
        check_vma=False,
    )
```

```python
import functools
import math

import jax
import jax.numpy as jnp
from jax import lax
from jax.experimental import pallas as pl
from jax.experimental.pallas import tpu as pltpu
from jax.sharding import PartitionSpec as P

HEAD_DIM = 64
HALO = 576
FRONT = 640
QB = 128
WIN = FRONT + QB
LANES = 128
EPS = 1e-5
SCALE = 0.125
AWAY = -1e30
BF = jnp.bfloat16
F32 = jnp.float32
VMEM_LIMIT = 63 * 1024 * 1024


def dot(a, b):
    return lax.dot_general(a, b, (((1,), (0,)), ((), ())), preferred_element_type=F32)


def dot_nt(a, b):
    return lax.dot_general(a, b, (((1,), (1,)), ((), ())), preferred_element_type=F32)


def dot_tn(a, b):
    return lax.dot_general(a, b, (((0,), (0,)), ((), ())), preferred_element_type=F32)


def rotated(v, cos, sin):
    lane = lax.broadcasted_iota(jnp.int32, v.shape, 1)
    swapped = jnp.where(lane % 64 < 32, pltpu.roll(v, 96, 1), pltpu.roll(v, 32, 1))
    return v * cos + swapped * sin


def turns(table):
    first = lax.broadcasted_iota(jnp.int32, table.shape, 1) % 64 < 32
    cos = jnp.where(first, table, pltpu.roll(table, 32, 1))
    sin = jnp.where(first, -pltpu.roll(table, 96, 1), table)
    return cos, sin


def both_heads(v):
    lane = lax.broadcasted_iota(jnp.int32, v.shape, 1)
    zero = jnp.zeros_like(v)
    return jnp.concatenate([jnp.where(lane < 64, v, zero), jnp.where(lane < 64, zero, v)], axis=0)


def one_of_both(v):
    rows = v.shape[0] // 2
    lane = lax.broadcasted_iota(jnp.int32, (rows, v.shape[1]), 1)
    return jnp.where(lane < 64, v[:rows], v[rows:])


def norm_rows(x):
    return lax.rsqrt(jnp.mean(x * x, axis=-1, keepdims=True) + EPS)


def in_thirds(v, lane):
    high = v.astype(BF)
    rest = v - high.astype(F32)
    middle = rest.astype(BF)
    last = (rest - middle.astype(F32)).astype(BF)
    return jnp.where(lane < 48, high, jnp.where(lane < 64, middle, last))


def coordinates():
    seq, span = lax.axis_index("seq"), lax.axis_index("span")
    return seq // 4, seq // 2 % 2, seq % 2, span


def device(y, x, core, span):
    return (y * 4 + x * 2 + core, span)


def greet():
    y, x, core, span = coordinates()
    barrier = pltpu.get_barrier_semaphore()
    peers = [device(y, x, core, (span + d) % 4) for d in (1, 2, 3)]
    peers += [device(1 - y, x, core, span), device(y, 1 - x, core, span), device(y, x, 1 - core, span)]
    for peer in peers:
        pl.semaphore_signal(barrier, inc=1, device_id=peer, device_id_type=pl.DeviceIdType.MESH)
    pl.semaphore_wait(barrier, len(peers))


def remote(src, dst, sems, at, to):
    return pltpu.make_async_remote_copy(
        src_ref=src, dst_ref=dst, send_sem=sems.at[0, at], recv_sem=sems.at[1, at], device_id=to,
        device_id_type=pl.DeviceIdType.MESH,
    )


GATHER_COPIES = 8


class Gathered:
    def __init__(self, shard, near, whole, at, count, sems, number):
        self.shard, self.near, self.whole, self.sems = shard, near, whole, sems
        self.first = number * GATHER_COPIES
        self.split = shard.shape[0] % 16 != 0
        self.columns = pl.ds(at, count)
        y, x, core, span = coordinates()
        half = count // 2
        left, right = pl.ds(at, half), pl.ds(at + half, half)
        over_y, over_x = device(1 - y, x, core, span), device(y, 1 - x, core, span)
        own = whole.at[y, x, core]
        rows = pl.ds(0, own.shape[0])
        refs = [(near.at[0], near.at[d], device(y, x, core, (span + d) % 4)) for d in (1, 2, 3)]
        refs += [(r, r, to) for r, to in (
            (whole.at[y, x, core, rows, left], over_y),
            (whole.at[y, x, core, rows, right], over_x),
            (whole.at[pl.ds(0, 2), x, core, rows, left], over_x),
            (whole.at[y, pl.ds(0, 2), core, rows, right], over_y),
            (whole.at[pl.ds(0, 2), pl.ds(0, 2), core, rows, self.columns], device(y, x, 1 - core, span)),
        )]
        self.copies = [remote(src, dst, sems, self.first + i, to) for i, (src, dst, to) in enumerate(refs)]

    def go(self, stage):
        if stage == 0:
            v = self.shard[:, self.columns]
            if self.split:
                half = v.shape[1] // 2
                v = v.astype(F32)
                v = jnp.concatenate([v[:, :half], v[:, half:]], axis=0).astype(BF)
            self.near[0] = v
            for i in (0, 1, 2):
                self.copies[i].start()
        if stage == 1:
            y, x, core, span = coordinates()
            for i in (0, 1, 2):
                self.copies[i].wait_recv()
            pieces = []
            for s in range(4):
                v = self.near[(span - s + 4) % 4]
                if self.split:
                    v = v.astype(F32)
                    half = v.shape[0] // 2
                    v = jnp.concatenate([v[:half], v[half:]], axis=1)
                pieces.append(v)
            self.whole[y, x, core, :, self.columns] = jnp.concatenate(pieces, axis=0).astype(BF)
            for i in (3, 4):
                self.copies[i].start()
        if stage == 2:
            for i in (3, 4):
                self.copies[i].wait_recv()
            for i in (5, 6):
                self.copies[i].start()
        if stage == 3:
            for i in (5, 6):
                self.copies[i].wait_recv()
            self.copies[7].start()
        if stage == 4:
            self.copies[7].wait_recv()

    def finish(self):
        for c in self.copies:
            c.wait_send()


def attention_forward(refs, q_out, k_out, v_out, mixed_out, qaug_out, normed_out, steps, tick):
    tok, halo, weights, gain, kaug, qaug, table = refs
    rows, width = tok.shape
    padded = q_out.shape[0]
    pairs = width // LANES

    def normal(x):
        x = x.astype(F32)
        return (x * norm_rows(x) * gain[0:1, :]).astype(BF)

    def project(which, normed, key_at, query_at):
        count = normed.shape[0]
        product = dot(normed, weights[which]())
        if which == 2:
            v_out[key_at : key_at + count, :] = product.astype(BF)
            return
        c, s = turns(table[key_at : key_at + count, :])
        for t in range(pairs):
            lanes = slice(t * LANES, (t + 1) * LANES)
            turned = rotated(product[:, lanes], c, s)
            if which == 0:
                q_out[query_at : query_at + count, lanes] = (turned * SCALE).astype(BF)
            else:
                k_out[key_at : key_at + count, lanes] = turned.astype(BF)

    lead = FRONT - HALO
    k_out[:lead, :] = jnp.zeros((lead, width), BF)
    v_out[:lead, :] = jnp.zeros((lead, width), BF)
    if padded > rows:
        blank = jnp.zeros((padded - rows, width), BF)
        q_out[rows:, :] = blank
        k_out[FRONT + rows :, :] = blank
        v_out[FRONT + rows :, :] = blank
    parts = [(at, min(480, rows - at)) for at in range(0, rows, 480)]
    for which in range(3):
        steps(which)
        for i, (at, count) in enumerate(parts):
            if which == 0:
                normed_out[at : at + count, :] = normal(tok[at : at + count, :])
            project(which, normed_out[at : at + count, :], FRONT + at, at)
            steps(which, i)

    lane = lax.broadcasted_iota(jnp.int32, (QB, LANES), 1)
    row = lax.broadcasted_iota(jnp.int32, (2 * QB, QB), 0)
    behind = lax.broadcasted_iota(jnp.int32, (2 * QB, QB), 1) <= row % QB

    blocks = padded // QB

    def block(i, carry):
        tick(i)

        @pl.when(i == blocks - FRONT // QB)
        def _():
            steps(3)
            normed = normal(halo[...])
            for which in (1, 2):
                project(which, normed, lead, None)

        start = pl.multiple_of((blocks - 1 - i) * QB, QB)
        k_a = kaug[pl.ds(start, WIN), :]
        q_a = qaug[pl.ds(start, QB), :]
        q_a2 = jnp.concatenate([q_a, q_a], axis=0)
        logs = jnp.zeros((QB, LANES), F32)
        for t in range(pairs):
            at = slice(t * LANES, (t + 1) * LANES)
            q2 = jnp.concatenate([both_heads(q_out[pl.ds(start, QB), at]), q_a2], axis=1)
            k2 = jnp.concatenate([k_out[pl.ds(start, WIN), at], k_a], axis=1)
            s = dot_nt(q2, k2)
            s = jnp.concatenate([s[:, :FRONT], jnp.where(behind, s[:, FRONT:], AWAY)], axis=1)
            top = jnp.max(s, axis=1, keepdims=True)
            p = jnp.exp(s - top).astype(BF)
            v = v_out[pl.ds(start, WIN), at]
            o = dot(p, jnp.concatenate([v, jnp.ones_like(v)], axis=1))
            total = o[:, LANES:]
            mixed_out[pl.ds(start, QB), at] = one_of_both(o[:, :LANES] / total).astype(BF)
            log = top + jnp.log(total)
            for e in range(2):
                h = 2 * t + e
                mine = (lane == 32 + h) | (lane == 48 + h) | (lane == 64 + h)
                logs = jnp.where(mine, log[e * QB : (e + 1) * QB], logs)
        qaug_out[pl.ds(start, QB), :] = jnp.where(lane < 32, q_a, in_thirds(-logs, lane))
        return carry

    lax.fori_loop(0, blocks, block, 0)


def fwd_kernel(tok, halo, wq, wk, wv, gain, kaug, qaug, table, q_out, k_out, v_out, mixed_out, qaug_out, normed_out):
    weights = [lambda w=w: w[...] for w in (wq, wk, wv)]
    refs = (tok, halo, weights, gain, kaug, qaug, table)
    attention_forward(refs, q_out, k_out, v_out, mixed_out, qaug_out, normed_out, lambda *_: None, lambda *_: None)


GATHER_CHUNKS = (
    (0, 0, 1024), (1, 0, 768), (2, 0, 768), (3, 0, 768), (4, 0, 1024), (4, 1024, 1024), (5, 0, 1024), (5, 1024, 1024),
    (6, 0, 256), (6, 256, 256), (6, 512, 256),
)
HALO_AFTER = (10, 1)
HALO_CHUNK = 11
GATHER_BEFORE = (
    ((0, 0), (1, 0), (2, 0), (3, 0), (0, 1), (4, 0), (1, 1), (0, 2), (2, 1), (5, 0), (1, 2), (3, 1), (6, 0), (0, 3), (4, 1), (2, 2), (7, 0), (0, 4)),
    ((8, 0), (4, 2), (1, 4)),
    ((10, 0), (5, 2), (7, 1), (2, 4)),
)
GATHER_PARTS = (
    (((1, 3),), ((5, 1),), ((3, 2),), ()),
    ((), ((6, 1), (9, 0)), (), ((2, 3),)),
    ((), ((3, 3), (8, 1)), ((11, 0),), ()),
)
GATHER_BLOCKS = (
    (1, ((9, 1),)),
    (2, ((4, 3),)),
    (3, ((10, 1), (6, 2))),
    (5, ((5, 3),)),
    (6, ((7, 2),)),
    (7, ((8, 2),)),
    (8, ((9, 2), (10, 2))),
    (10, ((6, 3), (7, 3))),
    (12, ((8, 3),)),
    (13, ((9, 3),)),
)
GATHER_END = ((10, 3), (3, 4), (4, 4), (5, 4), (6, 4), (7, 4), (8, 4), (9, 4), (10, 4))


def fwd_gather_kernel(tok, *refs):
    shards, refs = refs[:7], refs[7:]
    own_gains, kaug, qaug, table = refs[:4]
    outs, refs = refs[4:10], refs[10:]
    gains, refs = refs[0], refs[1:]
    whole_outs, refs = refs[:7], refs[7:]
    n = len(GATHER_CHUNKS)
    halo, nears, wholes = refs[0], refs[1 : n + 1], refs[n + 1 : n + 8]
    first_shard, *kept, sems, halo_sems, out_sems = refs[n + 8 :]
    q_out, k_out, v_out, mixed_out, qaug_out, normed_out = outs
    blocks = mixed_out.shape[0] // QB
    early_outs = [
        pltpu.make_async_copy(held, out, out_sems.at[7 + i])
        for i, (held, out) in enumerate(zip(kept, (q_out, normed_out, k_out, v_out)))
    ]
    rows, width = tok.shape
    y, x, core, span = coordinates()
    own_gains = own_gains[...].astype(F32)
    first_shard[:, :width] = shards[0][...]
    for i in range(2):
        first_shard[:, width + i * LANES : width + (i + 1) * LANES] = jnp.broadcast_to(
            own_gains[:, i : i + 1], (own_gains.shape[0], LANES)
        ).astype(BF)
    shards = (first_shard,) + tuple(shards[1:])
    greet()
    to_next = remote(tok.at[pl.ds(rows - HALO, HALO)], halo, halo_sems, 0, device(y, x, core, (span + 1) % 4))

    chunks = [
        Gathered(shards[w], nears[i], wholes[w], at, count, sems, i) for i, (w, at, count) in enumerate(GATHER_CHUNKS)
    ]
    out_copies = [pltpu.make_async_copy(w, o, out_sems.at[i]) for i, (w, o) in enumerate(zip(wholes, whole_outs))]

    def go(events):
        for chunk, stage in events:
            if chunk == HALO_CHUNK:
                to_next.start()
                continue
            chunks[chunk].go(stage)
            w, at, count = GATHER_CHUNKS[chunk]
            if stage == 4 and (chunk + 1 == len(GATHER_CHUNKS) or GATHER_CHUNKS[chunk + 1][0] != w):
                out_copies[w].start()

    def steps(which, part=None):
        if which == 3:
            to_next.wait_recv()
            return
        if part is not None:
            go(GATHER_PARTS[which][part])
            if (which, part) == (2, 3):
                for c in early_outs[:2]:
                    c.start()
            return
        go(GATHER_BEFORE[which])
        if which == 0:
            both = wholes[0][...].reshape(width, -1)[:, width:].astype(F32)
            both = [jnp.transpose(both[:, i * LANES : (i + 1) * LANES])[:1] for i in range(2)]
            gains[...] = jnp.concatenate(both + [jnp.zeros((6, width), F32)], axis=0)

    def tick(i):
        for at, events in GATHER_BLOCKS:
            @pl.when(i == at)
            def _():
                go(events)

        @pl.when(i == blocks - 1)
        def _():
            for c in early_outs[2:]:
                c.start()

    weights = [lambda w=w: w[...].reshape(width, w.shape[-1])[:, :width] for w in wholes[:3]]
    q, normed, k, v = kept
    attention_forward((tok, halo, weights, gains, kaug, qaug, table), q, k, v, mixed_out, qaug_out, normed, steps, tick)
    go(GATHER_END)
    to_next.wait_send()
    for c in chunks:
        c.finish()
    for c in out_copies + early_outs:
        c.wait()


def attention_backward(b, refs, dq_out, add):
    q, k, v, dmixed, kaug, qaug, daug, table = refs
    width = q.shape[1]
    lead = FRONT - HALO
    lane = lax.broadcasted_iota(jnp.int32, (QB, LANES), 1)
    key_row = lax.broadcasted_iota(jnp.int32, (QB, 2 * QB), 0)
    behind = key_row <= lax.broadcasted_iota(jnp.int32, (QB, 2 * QB), 1) % QB
    start = pl.multiple_of(b * QB, QB)
    keys = pl.ds(pl.multiple_of(start + lead, lead), WIN - lead)
    k_a = kaug[keys, :]
    q_a = qaug[pl.ds(start, QB), :]
    d_a = daug[pl.ds(start, QB), :]
    c, s_ = turns(table[pl.ds(start + FRONT, QB), :])
    zero = jnp.zeros_like(q_a)
    for t in range(width // LANES):
        at = slice(t * LANES, (t + 1) * LANES)
        mine = [(lane >= 32) & (lane % 16 == 2 * t + e) for e in range(2)]
        q_2 = both_heads(q[pl.ds(start, QB), at])
        q_aug = jnp.concatenate([jnp.where((lane < 32) | mine[e], q_a, zero) for e in range(2)], axis=0)
        d_2 = both_heads(dmixed[pl.ds(start, QB), at])
        d_aug = jnp.concatenate([jnp.where(mine[e], d_a, zero) for e in range(2)], axis=0)
        k_p = k[keys, at]
        st = dot_nt(jnp.concatenate([k_p, k_a], axis=1), jnp.concatenate([q_2, q_aug], axis=1))
        st = jnp.concatenate([st[:HALO], jnp.where(behind, st[HALO:], AWAY)], axis=0)
        pt = jnp.exp(st)
        dpt = dot_nt(jnp.concatenate([v[keys, at], k_a], axis=1), jnp.concatenate([d_2, d_aug], axis=1))
        dst = (pt * dpt).astype(BF)
        add(t, dot(dst, q_2), dot(pt.astype(BF), d_2))
        dq = one_of_both(dot_tn(dst, k_p)) * SCALE
        dq_out[pl.ds(start, QB), at] = rotated(dq, c, -s_).astype(BF)


def bwd_kernel(*refs):
    dq_out, dk_out, dv_out = refs[8:]
    padded = dq_out.shape[0]
    dk_out[...] = jnp.zeros_like(dk_out)
    dv_out[...] = jnp.zeros_like(dv_out)
    lead = FRONT - HALO

    def block(b, carry):
        keys = pl.ds(pl.multiple_of(b * QB + lead, lead), WIN - lead)

        def add(t, dk, dv):
            at = slice(t * LANES, (t + 1) * LANES)
            dk_out[keys, at] += dk
            dv_out[keys, at] += dv

        attention_backward(b, refs[:8], dq_out, add)
        return carry

    lax.fori_loop(0, padded // QB, block, 0)


SCATTER_COPIES = 8
SCATTER_CHUNKS = (
    (0, 0, 768), (1, 0, 1024), (1, 1024, 1024), (2, 0, 1024), (2, 1024, 1024), (3, 0, 256), (3, 256, 256), (3, 512, 256),
)
SUB = 512
SUB_SLOTS = 2
TALL = 256


class Scattered:
    def __init__(self, whole, at, count, out, bufs, sems, number):
        self.whole, self.out = whole, out
        self.got, self.left, self.right, self.left_2, self.right_2, self.near, self.far = bufs
        self.at, self.count = at, count
        self.columns = pl.ds(0, count)
        self.half = half = count // 2
        self.left_whole = False
        y, x, core, span = coordinates()
        rows = pl.ds(0, whole.shape[3])
        two = pl.ds(0, 2)
        lo, hi = pl.ds(0, half), pl.ds(half, half)
        over_y, over_x = device(1 - y, x, core, span), device(y, 1 - x, core, span)
        got = self.got
        refs = [
            (whole.at[two, two, 1 - core, rows, self.columns], got, device(y, x, 1 - core, span)),
            (got.at[two, 1 - x, rows, lo], self.left, over_x),
            (got.at[1 - y, two, rows, hi], self.right, over_y),
            (got.at[1 - y, x, rows, lo], self.left_2, over_y),
            (got.at[y, 1 - x, rows, hi], self.right_2, over_x),
        ]
        refs += [(self.near.at[(span + d) % 4], self.far.at[d - 1], device(y, x, core, (span + d) % 4)) for d in (1, 2, 3)]
        first = number * SCATTER_COPIES
        self.copies = [remote(src, dst, sems, first + i, to) for i, (src, dst, to) in enumerate(refs)]
    def go(self, stage):
        y, x, core, span = coordinates()
        got, half = self.got, self.half
        lo, hi = pl.ds(0, half), pl.ds(half, half)
        if stage == 0:
            self.copies[0].start()
        if stage == 1:
            self.copies[0].wait_recv()
            for i in range(2):
                for j in range(2):
                    got[i, j] = got[i, j] + self.whole[i, j, core, :, self.columns]
            for i in (1, 2):
                self.copies[i].start()
        if stage == 2:
            for i in (1, 2):
                self.copies[i].wait_recv()
            for i in range(2):
                got[i, x, :, lo] = got[i, x, :, lo] + self.left[i]
                got[y, i, :, hi] = got[y, i, :, hi] + self.right[i]
            for i in (3, 4):
                self.copies[i].start()
        if stage == 3:
            for i in (3, 4):
                self.copies[i].wait_recv()
            total = jnp.concatenate(
                [got[y, x, :, r].astype(F32) + other[...].astype(F32) for r, other in ((lo, self.left_2), (hi, self.right_2))],
                axis=1,
            )
            depth = total.shape[0] // 4
            for s in range(4):
                v = total[s * depth : (s + 1) * depth]
                if depth % 16:
                    v = jnp.concatenate([v[:, :half], v[:, half:]], axis=0)
                self.near[s] = v.astype(BF)
            for i in (5, 6, 7):
                self.copies[i].start()
        if stage == 4:
            for i in (5, 6, 7):
                self.copies[i].wait_recv()
            v = self.near[span].astype(F32)
            for d in range(3):
                v = v + self.far[d].astype(F32)
            depth = self.out.shape[0]
            if depth % 16:
                v = jnp.concatenate([v[:depth], v[depth:]], axis=1)
            self.out[:, self.at : self.at + self.count] = v

    def leave_whole(self):
        if not self.left_whole:
            self.copies[0].wait_send()
        self.left_whole = True

    def finish(self):
        self.leave_whole()
        for c in self.copies[1:]:
            c.wait_send()


def scatter_buffers(rows, count):
    depth = rows // 4
    piece = (2 * depth, count // 2) if depth % 16 else (depth, count)
    shapes = [
        (2, 2, rows, count), (2, rows, count // 2), (2, rows, count // 2), (rows, count // 2), (rows, count // 2),
        (4,) + piece, (3,) + piece,
    ]
    return [pltpu.VMEM(shape, BF) for shape in shapes]


HALO_BLOCKS = FRONT // QB
SCATTER_AT = ((0, 1, 3, 5), (5, 6, 8, 11), (6, 7, 10, 14), (7, 8, 12, 15), (8, 9, 13, 16))
GRAD_TICKS = 4


def scatter_plan(blocks):
    ticks = [[] for _ in range(blocks + GRAD_TICKS)]
    for t, j, stage in sorted((t, j, stage) for j, when in enumerate(SCATTER_AT) for stage, t in enumerate(when)):
        ticks[t].append((j, stage))
    return ticks


def bwd_scatter_kernel(
    q_in, k_in, v_in, dmixed_in, kaug, qaug, daug, table, tok, gains, d_resid, wq_in, wk_in, wv_in,
    normed_in, g_out, n2_in, cot_in, hid_in, dg_in, du_in,
    input_grad, s_query, s_key, s_value, s_out, s_gate, s_up, s_down,
    q, k, v, dmixed, dk_win, dv_win, halo_out, halo_in, resid_block, out_block, subs, wide, tall, *refs,
):
    rows, width = tok.shape
    padded = q.shape[0]
    blocks = padded // QB
    pairs = width // LANES
    lead = FRONT - HALO
    slots = WIN // QB
    n = len(SCATTER_CHUNKS)
    chunk_bufs = [refs[7 * i : 7 * i + 7] for i in range(n + 3)]
    refs = refs[7 * (n + 3) :]
    sems, in_sems, sub_sems, halo_sems, block_sems = refs
    y, x, core, span = coordinates()

    near_q, near_k = HALO_BLOCKS * QB, 2 * FRONT
    far_q = pl.ds(near_q, padded - near_q)
    lower, upper = pl.ds(0, padded - near_q), pl.ds(padded - near_q, near_q)
    far_k = pl.ds(near_k, near_q)
    rest = pl.ds(near_k + near_q, k.shape[0] - near_k - near_q)
    one, two = pl.ds(0, near_q), pl.ds(0, near_k)
    early_rows = (blocks - 3) * QB
    weights = [halo_out.at[0], halo_out.at[1], halo_in.at[0]]
    by_name = dict(
        q=(q_in.at[one], q.at[one]), k=(k_in.at[two], k.at[two]), v=(v_in.at[two], v.at[two]),
        d=(dmixed_in.at[one], dmixed.at[one]),
        o=(g_out, wide.at[0, pl.ds(0, 2), pl.ds(0, 2), pl.ds(0, 2), pl.ds(0, width // 8), pl.ds(0, width)]),
        n_low=(n2_in.at[lower], q.at[far_q]), n_high=(n2_in.at[upper], k.at[far_k]),
        c=(cot_in, dmixed.at[pl.ds(0, rows)]),
        k_rest=(k_in.at[rest], k.at[rest]), v_rest=(v_in.at[rest], v.at[rest]),
        q_far=(q_in.at[far_q], q.at[far_q]), k_far=(k_in.at[far_k], k.at[far_k]),
        d_far=(dmixed_in.at[far_q], dmixed.at[far_q]), v_far=(v_in.at[far_k], v.at[far_k]),
        w_q=(wq_in.at[pl.ds(0, width), pl.ds(0, width)], weights[0]),
        w_k=(wk_in, weights[1]), w_v=(wv_in, weights[2]),
        normed_low=(normed_in.at[pl.ds(0, early_rows)], dmixed.at[pl.ds(0, early_rows)]),
        normed_high=(
            normed_in.at[pl.ds(early_rows, rows - early_rows)], dmixed.at[pl.ds(early_rows, rows - early_rows)]
        ),
    )
    arrivals = {
        name: pltpu.make_async_copy(src, dst, in_sems.at[i]) for i, (name, (src, dst)) in enumerate(by_name.items())
    }
    brought = [(src, f) for src in (dg_in, du_in, hid_in) for f in range(src.shape[0])]
    sub_copies = [
        pltpu.make_async_copy(src.at[f], subs.at[i % SUB_SLOTS], sub_sems.at[i])
        for i, (src, f) in enumerate(brought)
    ]

    def bring(*names):
        for name in names:
            arrivals[name].start()

    def await_all(*names):
        for name in names:
            arrivals[name].wait()

    bring("o", "q", "k", "v", "d", "n_low", "n_high", "k_rest", "v_rest", "d_far", "v_far")
    for c in sub_copies[:SUB_SLOTS]:
        c.start()
    greet()

    sums = (s_out, s_gate, s_up, s_down)
    chunks = []
    for i, (w, at, count) in enumerate(SCATTER_CHUNKS):
        whole = wide.at[i % 3] if w < 3 else tall.at[at // count]
        chunks.append(Scattered(whole, at, count, sums[w], chunk_bufs[i], sems, i))
    own = [wide.at[i] for i in (2, 0, 1)]
    chunks += [
        Scattered(own[i], 0, width, (s_query, s_key, s_value)[i], chunk_bufs[n + i], sems, n + i) for i in range(3)
    ]
    to_last = remote(
        halo_out.at[pl.ds(0, 2), pl.ds(0, HALO)], halo_in.at[pl.ds(0, 2), pl.ds(0, HALO)], halo_sems, 0, device(y, x, core, (span + 3) % 4))
    ticks = scatter_plan(blocks)
    dk_win[...] = jnp.zeros_like(dk_win)
    dv_win[...] = jnp.zeros_like(dv_win)
    await_all("o", "q", "k", "v", "d")

    def block_of(inside):
        return functools.partial(block, inside)

    def block(inside, b, carry):
        for i, todo in inside.items():
            if todo:
                @pl.when(b == i)
                def _():
                    for chunk, stage in todo:
                        chunks[chunk].go(stage)

        @pl.when(b == blocks - 3)
        def _():
            bring("normed_low")

        def add(t, dk, dv):
            at = slice(t * LANES, (t + 1) * LANES)
            for win, grad in ((dk_win, dk), (dv_win, dv)):
                for j in range(slots):
                    count = min(QB, WIN - lead - j * QB)
                    win[lax.rem(b + j, slots), :count, at] += grad[j * QB : j * QB + count]

        attention_backward(b, (q, k, v, dmixed, kaug, qaug, daug, table), q, add)

        slot = lax.rem(b, slots)
        at = pl.ds(pl.multiple_of(b * QB + lead, lead), QB)

        @pl.when(b < FRONT // QB)
        def _():
            to = pl.ds(pl.multiple_of(b * QB, QB), QB)
            halo_out[0, to, :] = dk_win[slot].astype(BF)
            halo_out[1, to, :] = dv_win[slot].astype(BF)

        @pl.when((b >= FRONT // QB - 1) & (b < blocks - 1))
        def _():
            c, s_ = turns(table[at, :])
            for t in range(pairs):
                lanes = slice(t * LANES, (t + 1) * LANES)
                k[at, lanes] = rotated(dk_win[slot, :, lanes], c, -s_).astype(BF)
            v[at, :] = dv_win[slot].astype(BF)

        @pl.when(b < blocks - 1)
        def _():
            dk_win[slot] = jnp.zeros((QB, width), F32)
            dv_win[slot] = jnp.zeros((QB, width), F32)

        return carry

    lax.fori_loop(0, HALO_BLOCKS, block_of({b: ticks[b] for b in range(HALO_BLOCKS)}), 0)
    to_last.start()

    sub = 0
    low, group = padded - near_q, tall.shape[4]
    await_all("n_low", "n_high")

    def next_sub():
        nonlocal sub
        if sub + SUB_SLOTS < len(sub_copies):
            sub_copies[sub + SUB_SLOTS].start()
        sub += 1

    for i, (w, at, count) in enumerate(SCATTER_CHUNKS[: GRAD_TICKS + 1]):
        if w == 0:
            continue
        if i >= 3:
            chunks[i - 3].leave_whole()
        for f in range(0, count, SUB):
            sub_copies[sub].wait()
            here = subs.at[sub % SUB_SLOTS]
            total = dot_tn(q[near_q:, :], here[:low, :]) + dot_tn(k[near_k : near_k + near_q, :], here[low:, :])
            wide[i % 3, :, :, :, :, f : f + SUB] = total.reshape(2, 2, 2, width // 8, SUB).astype(BF)
            next_sub()
        if i == GRAD_TICKS:
            bring("q_far", "k_far")
        for chunk, stage in ticks[HALO_BLOCKS + i - 1]:
            chunks[chunk].go(stage)
    await_all("q_far", "k_far", "d_far", "v_far", "k_rest", "v_rest")
    lax.fori_loop(HALO_BLOCKS, blocks, block_of({b: ticks[b + GRAD_TICKS] for b in range(HALO_BLOCKS, blocks)}), 0)
    bring("normed_high")
    to_last.wait_send()
    bring("w_q", "w_k")

    step = resid_block.shape[1]
    parts = [(at, min(step, rows - at)) for at in range(0, rows, step)]
    resid_in = [
        pltpu.make_async_copy(
            d_resid.at[pl.ds(at, count)], resid_block.at[i % 2, pl.ds(0, count)], block_sems.at[0, i]
        ) for i, (at, count) in enumerate(parts)
    ]
    grad_copies = [
        pltpu.make_async_copy(
            out_block.at[i % 2, pl.ds(0, count)], input_grad.at[pl.ds(at, count)], block_sems.at[1, i]
        ) for i, (at, count) in enumerate(parts)
    ]
    resid_in[0].start()
    resid_in[1].start()

    def go(*events):
        for chunk, stage in events:
            chunks[chunk].go(stage)

    g = gains[0:1, :]
    normed = dmixed
    await_all("normed_low", "normed_high")

    def weight_grad(i, grad):
        for j in range(2):
            half = width // 2
            total = dot_tn(normed[:rows, j * half : (j + 1) * half], grad)
            own[i][j, :, :, :, pl.ds(0, width)] = total.reshape(2, 2, half // 4, width).astype(BF)

    for i in (2, 3, 4):
        chunks[i].leave_whole()
    weight_grad(0, q[:rows, :])
    go((n, 0), (0, 4))
    to_last.wait_recv()
    for j in range(slots):
        base = (blocks - 1) * QB + lead + j * QB
        slot = (blocks - 1 + j) % slots
        count = min(QB, FRONT + rows - base)
        first = max(base, FRONT + rows - HALO)
        for which, win, whole in ((0, dk_win, k), (1, dv_win, v)):
            grad = win[slot, :count, :]
            more = halo_in[which, first - (FRONT + rows - HALO) : base + count - (FRONT + rows - HALO), :].astype(F32)
            if first > base:
                more = jnp.concatenate([jnp.zeros((first - base, width), F32), more], axis=0)
            grad = grad + more
            if which:
                whole[base : base + count, :] = grad.astype(BF)
                continue
            c, s_ = turns(table[base : base + count, :])
            for t in range(pairs):
                lanes = slice(t * LANES, (t + 1) * LANES)
                whole[base : base + count, lanes] = rotated(grad[:, lanes], c, -s_).astype(BF)
    bring("w_v")
    weight_grad(1, k[FRONT : FRONT + rows, :])
    go((n, 1), (n + 1, 0), (1, 4))
    weight_grad(2, v[FRONT : FRONT + rows, :])
    bring("c")
    go((n, 2), (n + 1, 1), (n + 2, 0), (2, 4))

    await_all("c")
    beside = (((n + 1, 2), (n + 2, 1)), ((n, 3),), ((n + 1, 3), (n + 2, 2)), ((n + 2, 3),))
    for i in range(hid_in.shape[0]):
        sub_copies[sub].wait()
        total = dot_tn(subs[sub % SUB_SLOTS, :rows, :], dmixed[:rows, :]).astype(BF)
        for r in range(0, SUB, group):
            to = (i * SUB + r) // group
            for j in range(width // TALL):
                tall[j, to // 4, to // 2 % 2, to % 2] = total[r : r + group, j * TALL : (j + 1) * TALL]
        next_sub()
        go(*beside[i])
    go((5, 0), (6, 0), (7, 0))
    await_all("w_q", "w_k", "w_v")
    between = (
        ((5, 1), (6, 1), (7, 1)), ((n, 4), (3, 4)), ((5, 2), (6, 2)), ((7, 2), (n + 1, 4)), ((5, 3), (6, 3)),
        ((7, 3), (n + 2, 4)), ((4, 4), (5, 4)), ((6, 4), (7, 4)),
    )
    for i, (at, count) in enumerate(parts):
        grads = (q[at : at + count, :], k[FRONT + at : FRONT + at + count, :], v[FRONT + at : FRONT + at + count, :])
        dn = sum(dot_nt(d, weights[w][...]) for w, d in enumerate(grads))
        x = tok[at : at + count, :].astype(F32)
        inv = norm_rows(x)
        hat = x * inv
        e = dn * g
        resid_in[i].wait()
        total = resid_block[i % 2, :count] + inv * (e - hat * jnp.mean(e * hat, axis=-1, keepdims=True))
        if i >= 2:
            grad_copies[i - 2].wait()
        out_block[i % 2, :count] = total.astype(BF)
        grad_copies[i].start()
        if i + 2 < len(parts):
            resid_in[i + 2].start()
        go(*between[i])
    for c in chunks:
        c.finish()
    for c in grad_copies[-2:]:
        c.wait()


def finish_kernel(input_in, *refs):
    grads, (wq, wk, wv, wg, wu, gains) = refs[:7], refs[7:13]
    input_out, gain_out, outs = refs[13], refs[14], refs[15:]
    input_out[...] = input_in[...]

    @pl.when(pl.program_id(0) == 0)
    def _():
        for grad, out in zip(grads, outs):
            out[...] = grad[...]
        sums = []
        for pairs in (((0, wq), (1, wk), (2, wv)), ((4, wg), (5, wu))):
            sums.append(sum(jnp.sum(grads[i][...] * w[...].astype(F32), axis=1, keepdims=True) for i, w in pairs))
        gain_out[...] = jnp.concatenate(sums, axis=1) / gains[...].astype(F32)


FF_STEP = 512
ROW_STEP = 480


def mlp_kernel(rows, x_ref, mixed, c_ref, wo, wg, wu, wd, gains,
               out, d_resid_out, d_mixed_out, daug_out, grad_out, n2_out, hid_out, dg_out, du_out, total):
    i = pl.program_id(0)
    count, width = x_ref.shape
    valid = lax.broadcasted_iota(jnp.int32, (count, width), 0) + i * count < rows
    c = jnp.where(valid, c_ref[...], jnp.zeros((count, width), BF))
    x = jnp.where(valid, x_ref[...].astype(F32), 0.0)
    mix = mixed[...]
    resid = x + dot(mix, wo[...])
    r = norm_rows(resid)
    g = gains[1:2, :]
    hat = resid * r
    n2 = (hat * g).astype(BF)
    n2_out[...] = n2
    acc = resid
    dn = jnp.zeros((count, width), F32)
    for f in range(0, wg.shape[1], FF_STEP):
        at = slice(f, f + FF_STEP)
        gate = dot(n2, wg[:, at])
        up = dot(n2, wu[:, at])
        sig = jax.nn.sigmoid(gate)
        silu = gate * sig
        hid = (silu * up).astype(BF)
        for j in range(0, FF_STEP, SUB):
            hid_out[(f + j) // SUB] = hid[:, j : j + SUB]
        acc = acc + dot(hid, wd[at, :])
        dh = dot_nt(c, wd[at, :])
        dg = (dh * up * sig * (1.0 + gate * (1.0 - sig))).astype(BF)
        du = (dh * silu).astype(BF)
        for j in range(0, FF_STEP, SUB):
            dg_out[(f + j) // SUB] = dg[:, j : j + SUB]
            du_out[(f + j) // SUB] = du[:, j : j + SUB]
        dn = dn + dot_nt(dg, wg[:, at]) + dot_nt(du, wu[:, at])
    out[...] = acc.astype(BF)
    e = dn * g
    d_resid = c.astype(F32) + r * (e - hat * jnp.mean(e * hat, axis=-1, keepdims=True))
    d_resid_out[...] = d_resid
    d_branch = d_resid.astype(BF)
    total[...] = jnp.where(i == 0, 0.0, total[...]) + dot_tn(mix, d_branch)

    @pl.when(i == pl.num_programs(0) - 1)
    def _():
        grad_out[...] = total[...].astype(BF)

    d_mixed = dot_nt(d_branch, wo[...]).astype(BF)
    d_mixed_out[...] = d_mixed

    e_row = lax.broadcasted_iota(jnp.int32, (width, LANES), 0) // HEAD_DIM
    e_lane = lax.broadcasted_iota(jnp.int32, (width, LANES), 1)
    picks = ((e_lane >= 32) & (e_lane < 80) & (e_lane % 16 == e_row)).astype(F32).astype(BF)
    prod = d_mixed.astype(F32) * mix.astype(F32)
    high = prod.astype(BF)
    low = (prod - high.astype(F32)).astype(BF)
    lane = lax.broadcasted_iota(jnp.int32, (count, LANES), 1)
    daug_out[...] = in_thirds(-(dot(high, picks) + dot(low, picks)), lane)


def slots_of(item_lengths, first, count):
    ends = jnp.cumsum(item_lengths[0])[None, :]
    slots = first + jnp.arange(count, dtype=jnp.int32)
    reached = (slots[:, None] >= ends) & (item_lengths[0] > 0)[None, :]
    segment = jnp.sum(reached.astype(jnp.int32), axis=1)
    begin = jnp.max(jnp.where(reached, ends, 0), axis=1)
    return slots, segment % 16, slots - begin


def side_arrays(item_lengths, local_rows, padded):
    offset = lax.axis_index("span") * local_rows
    count = FRONT + padded
    slots, group, position = slots_of(item_lengths, offset - FRONT, count)
    lane = jnp.arange(LANES, dtype=jnp.int32)[None, :]
    away = (slots < 0) | (jnp.arange(count) < FRONT - HALO)
    where_key = jnp.where(away, 16, group)[:, None]
    marks = (lane >= 32) & (lane < 80) & (lane % 16 < 12)
    kaug = ((lane == where_key) | marks).astype(BF)
    qaug = jnp.where((lane <= 16) & (lane != group[FRONT:, None]), AWAY, 0.0).astype(BF)
    half = HEAD_DIM // 2
    frequency = 10000.0 ** (-(lane % half).astype(F32) / half)
    quarter = jnp.where(lane % HEAD_DIM < half, 0.0, 0.5 * math.pi)
    return kaug, qaug, cosine(position[:, None].astype(F32) * frequency - quarter)


def cosine(v):
    number = jnp.floor(v * (0.5 / math.pi) + 0.5)
    rest = (v - number * 6.28125) - number * (2.0 * math.pi - 6.28125)
    square = rest * rest
    total = jnp.full_like(v, 1.0 / math.factorial(18))
    for k in range(8, -1, -1):
        total = 1.0 / math.factorial(2 * k) - total * square
    return total


def vmem():
    return pl.BlockSpec(memory_space=pltpu.VMEM)


def params(**more):
    return pltpu.CompilerParams(vmem_limit_bytes=VMEM_LIMIT, **more)


def call_backward(tok, q, k, v, d_mixed, kaug, qaug, daug, table, gains, d_resid, wq, wk, wv, normed, grad_out, *factors):
    rows, width = tok.shape
    ff = factors[-1].shape[0] * SUB
    padded, ext = q.shape[0], k.shape[0]
    sds = jax.ShapeDtypeStruct
    anywhere = pl.BlockSpec(memory_space=pl.ANY)
    depths = (width // 8, width // 8, width // 8, ff // 8)
    grad_out = grad_out.reshape(2, 2, 2, width // 8, width)
    buffers = []
    for w, _, count in SCATTER_CHUNKS:
        buffers += scatter_buffers(depths[w], count)
    for _ in range(3):
        buffers += scatter_buffers(width // 8, width)
    part = 256
    return pl.pallas_call(
        bwd_scatter_kernel,
        out_shape=[sds((rows, width), BF)] + [sds((width // 32, width), F32)] * 4
        + [sds((width // 32, ff), F32)] * 2 + [sds((ff // 32, width), F32)],
        in_specs=[anywhere] * 4 + [vmem()] * 6 + [anywhere] * 11,
        out_specs=[anywhere] + [vmem()] * 7,
        scratch_shapes=[
            pltpu.VMEM((padded, width), BF), pltpu.VMEM((ext, width), BF), pltpu.VMEM((ext, width), BF),
            pltpu.VMEM((padded, width), BF),
            pltpu.VMEM((WIN // QB, QB, width), F32), pltpu.VMEM((WIN // QB, QB, width), F32),
            pltpu.VMEM((2, max(FRONT, width), width), BF), pltpu.VMEM((2, max(HALO, width), width), BF),
            pltpu.VMEM((2, part, width), F32), pltpu.VMEM((2, part, width), BF),
            pltpu.VMEM((SUB_SLOTS, padded, SUB), BF),
            pltpu.VMEM((3, 2, 2, 2, width // 8, 1024), BF), pltpu.VMEM((width // TALL, 2, 2, 2, ff // 8, TALL), BF),
        ] + buffers + [
            pltpu.SemaphoreType.DMA((2, (len(SCATTER_CHUNKS) + 3) * SCATTER_COPIES)),
            pltpu.SemaphoreType.DMA((20,)),
            pltpu.SemaphoreType.DMA((3 * ff // SUB,)),
            pltpu.SemaphoreType.DMA((2, 1)),
            pltpu.SemaphoreType.DMA((2, -(-rows // part))),
        ],
        compiler_params=params(collective_id=1, has_side_effects=True),
        name="attend_back",
    )(q, k, v, d_mixed, kaug, qaug, daug, table, tok, gains, d_resid, wq, wk, wv, normed, grad_out, *factors)


def per_device(tokens, item_lengths, attn_gain, w_query, w_key, w_value, w_out, mlp_gain, w_gate, w_up, w_down, cotangent):
    rows, width = tokens.shape[1:]
    ff = w_gate.shape[1]
    padded = -(-rows // ROW_STEP) * ROW_STEP
    ext = FRONT + padded
    axes = ("seq", "span")
    seqs, spans = (lax.axis_size(a) for a in axes)
    direct = (seqs, spans) == (8, 4)
    sds = jax.ShapeDtypeStruct
    anywhere = pl.BlockSpec(memory_space=pl.ANY)
    tok, cot = tokens[0], cotangent[0]
    own_gains = jnp.stack([attn_gain, mlp_gain], axis=1)

    kaug, qaug, table = side_arrays(item_lengths, rows, padded)
    fwd_shapes = [
        sds((padded, width), BF), sds((ext, width), BF), sds((ext, width), BF),
        sds((padded, width), BF), sds((padded, LANES), BF), sds((rows, width), BF),
    ]
    if direct:
        shards = [w_query, w_key, w_value, w_out, w_gate, w_up, w_down]
        whole = [(2, 2, 2, 4 * w.shape[0], w.shape[1]) for w in shards]
        whole[0] = whole[0][:4] + (width + 2 * LANES,)
        near = []
        for w, _, count in GATHER_CHUNKS:
            depth = shards[w].shape[0]
            near.append((4, 2 * depth, count // 2) if depth % 16 else (4, depth, count))
        results = pl.pallas_call(
            fwd_gather_kernel,
            out_shape=fwd_shapes + [sds((8, width), F32)] + [sds(w, BF) for w in whole],
            in_specs=[vmem()] * 12,
            out_specs=[anywhere] * 3 + [vmem()] * 2 + [anywhere, vmem()] + [anywhere] * 7,
            scratch_shapes=[pltpu.VMEM((HALO, width), BF)]
            + [pltpu.VMEM(n, BF) for n in near]
            + [pltpu.VMEM(w, BF) for w in whole]
            + [
                pltpu.VMEM((w_query.shape[0], width + 2 * LANES), BF),
                pltpu.VMEM((padded, width), BF), pltpu.VMEM((rows, width), BF),
                pltpu.VMEM((ext, width), BF), pltpu.VMEM((ext, width), BF),
                pltpu.SemaphoreType.DMA((2, len(GATHER_CHUNKS) * GATHER_COPIES)),
                pltpu.SemaphoreType.DMA((2, 1)),
                pltpu.SemaphoreType.DMA((11,)),
            ],
            compiler_params=params(collective_id=0, has_side_effects=True),
            name="attend",
        )(tok, *shards, own_gains, kaug, qaug, table)
        q, k, v, mixed, qaug, normed, gains = results[:7]
        wq, wk, wv, wo, wg, wu, down = (w.reshape(-1, w.shape[-1]) for w in results[7:])
    else:
        packed = lax.all_gather(jnp.concatenate([w_query, w_key, w_value, w_out, w_gate, w_up], axis=1), axes, axis=0, tiled=True)
        down = lax.all_gather(w_down, axes, axis=0, tiled=True)
        gains = lax.all_gather(own_gains, axes, axis=0, tiled=True).astype(F32)
        gains = jnp.concatenate([jnp.transpose(gains), jnp.zeros((6, width), F32)], axis=0)
        wq, wk, wv, wo = (packed[:, i * width : (i + 1) * width] for i in range(4))
        wg, wu = packed[:, 4 * width : 4 * width + ff], packed[:, 4 * width + ff :]
        halo = lax.ppermute(tok[rows - HALO :], "span", [(i, i + 1) for i in range(spans - 1)])
        q, k, v, mixed, qaug, normed = pl.pallas_call(
            fwd_kernel,
            out_shape=fwd_shapes,
            in_specs=[vmem()] * 9,
            out_specs=[vmem()] * 6,
            compiler_params=params(),
            name="attend",
        )(tok, halo, wq, wk, wv, gains, kaug, qaug, table)

    tile = lambda n: pl.BlockSpec((ROW_STEP, n), lambda i: (i, 0))
    whole = lambda a: pl.BlockSpec(a.shape, lambda i: (0, 0), pipeline_mode=pl.Buffered(1))
    weights = (wo, wg, wu, down)
    output, d_resid, d_mixed, daug, g_o, n2, hid, dg, du = pl.pallas_call(
        functools.partial(mlp_kernel, rows),
        grid=(padded // ROW_STEP,),
        out_shape=[
            sds((rows, width), BF), sds((rows, width), F32), sds((padded, width), BF), sds((padded, LANES), BF),
            sds((width, width), BF), sds((padded, width), BF),
        ] + [sds((ff // SUB, padded, SUB), BF)] * 3,
        in_specs=[tile(width)] * 3 + [whole(a) for a in weights + (gains,)],
        out_specs=[tile(width)] * 3 + [tile(LANES), whole(wo), tile(width)]
        + [pl.BlockSpec((ff // SUB, ROW_STEP, SUB), lambda i: (0, i, 0))] * 3,
        scratch_shapes=[pltpu.VMEM((width, width), F32)],
        compiler_params=params(),
        name="mlp",
    )(tok, mixed, cot, *weights, gains)

    if direct:
        results = call_backward(
            tok, q, k, v, d_mixed, kaug, qaug, daug, table, gains, d_resid, wq, wk, wv, normed, g_o, n2, cot, hid, dg, du
        )
        input_grad, g_q, g_k, g_v, g_o, g_g, g_u, g_d = results
    else:
        dq, dk, dv = pl.pallas_call(
            bwd_kernel,
            out_shape=[sds((padded, width), BF), sds((ext, width), F32), sds((ext, width), F32)],
            in_specs=[vmem()] * 8,
            out_specs=[vmem()] * 3,
            compiler_params=params(),
            name="attend_back",
        )(q, k, v, d_mixed, kaug, qaug, daug, table)
        dq = dq[:rows]
        back = jnp.concatenate([dk[FRONT - HALO : FRONT], dv[FRONT - HALO : FRONT]], axis=1).astype(BF)
        back = lax.ppermute(back, "span", [(i + 1, i) for i in range(spans - 1)]).astype(F32)
        dk, dv = dk[FRONT : FRONT + rows], dv[FRONT : FRONT + rows]
        dk = jnp.concatenate([dk[: rows - HALO], dk[rows - HALO :] + back[:, :width]])
        dv = jnp.concatenate([dv[: rows - HALO], dv[rows - HALO :] + back[:, width:]]).astype(BF)
        half = HEAD_DIM // 2
        c, s = (table[FRONT : FRONT + rows, None, i * half : (i + 1) * half] for i in range(2))
        dk3 = dk.reshape(rows, width // HEAD_DIM, HEAD_DIM)
        a, b = dk3[..., :half], dk3[..., half:]
        dk = jnp.concatenate([a * c + b * s, b * c - a * s], axis=-1).reshape(rows, width).astype(BF)
        x = tok.astype(F32)
        inv = norm_rows(x)
        hat = x * inv
        gain_one = gains[:1]
        flat = lambda a: jnp.transpose(a, (1, 0, 2)).reshape(padded, ff)
        dn = sum(dot_nt(d, w) for d, w in ((dq, wq), (dk, wk), (dv, wv)))
        e = dn * gain_one
        input_grad = (d_resid + inv * (e - hat * jnp.mean(e * hat, axis=-1, keepdims=True))).astype(BF)
        sums = jnp.concatenate([dot_tn(normed, d) for d in (dq, dk, dv)] + [g_o.astype(F32), dot_tn(n2, flat(dg)), dot_tn(n2, flat(du))], axis=1)
        scatter = lambda g: lax.psum_scatter(g, axes, scatter_dimension=0, tiled=True)
        sums, g_d = scatter(sums), scatter(dot_tn(flat(hid)[:rows], cot))
        g_q, g_k, g_v, g_o = (sums[:, i * width : (i + 1) * width] for i in range(4))
        g_g, g_u = sums[:, 4 * width : 4 * width + ff], sums[:, 4 * width + ff :]

    grads = (g_q, g_k, g_v, g_o, g_g, g_u, g_d)
    owned = (w_query, w_key, w_value, w_gate, w_up, own_gains)
    shapes = [sds((w_query.shape[0], 2), F32)] + [sds(g.shape, F32) for g in grads]
    input_grad, gain_grads, *grads = pl.pallas_call(
        finish_kernel,
        grid=(padded // ROW_STEP,),
        out_shape=[sds((rows, width), BF)] + shapes,
        in_specs=[tile(width)] + [whole(a) for a in grads + owned],
        out_specs=[tile(width)] + [whole(a) for a in shapes],
        compiler_params=params(),
        name="finish",
    )(input_grad, *grads, *owned)
    g_q, g_k, g_v, g_o, g_g, g_u, g_d = grads
    return output[None], input_grad[None], gain_grads[:, 0], g_q, g_k, g_v, g_o, gain_grads[:, 1], g_g, g_u, g_d


def solution(mesh):
    rows_placed, vector, matrix = P("seq", "span", None), P(("seq", "span")), P(("seq", "span"), None)
    return jax.shard_map(
        per_device,
        mesh=mesh,
        in_specs=(rows_placed, P("seq", None), vector, matrix, matrix, matrix, matrix, vector, matrix, matrix, matrix, rows_placed),
        out_specs=(rows_placed, rows_placed, vector, matrix, matrix, matrix, matrix, vector, matrix, matrix, matrix),
        check_vma=False,
    )
```
